128 devices in a mesh: ctx: 32 (over y, z, core), zero: 4 (over x).
Axes of the slice: x: 4, y: 4, z: 4, core: 2. Of those that a mesh axis runs over, the one named last changes fastest.
Arguments:
- inputs: bfloat16 [4, 4096, 2048], P('zero', 'ctx'), may hold values from -6 to 6
- grad_out: bfloat16 [4, 4096, 1024], P('zero', 'ctx'), may hold values from -6 to 6
- saved: float32 [4, 32, 8, 128, 128], P('zero', 'ctx'), may hold values from -6 to 6
- w_qkv: bfloat16 [2048, 3072], P('zero'), may hold values from -0.125 to 0.125
Outputs:
- grad_x: bfloat16 [4, 4096, 2048], P('zero', 'ctx')
- grad_w: float32 [2048, 3072], P(('ctx', 'zero'))
The draws below stay inside these ranges and needn't reach their ends.
All inputs are finite; a program needn't handle non-finite values.
Results may differ from the reference program's by a relative error of at most 0.012.
Values may be sent and summed in bfloat16 or wider, within the bound.
No kernel may reach another device: no remote copies, remote signals or barrier semaphores. Data moves between devices by JAX's collectives and lax.ppermute only.
A program may use at most 192 MiB of HBM per device.

```python
import jax
import jax.numpy as jnp
from jax import lax

D = 2048
HEADS = 8
HEAD_DIM = 128
TOK_DEV = 128
LENGTH = 4096
SEQS = 4
N_CTX = 32


def spiked(array, own_key, source, target, shards_of, factor):
    owner, partner = [(jnp.arange(array.shape[dim]) // (array.shape[dim] // shards_of)).reshape([-1 if axis == dim else 1 for axis in range(array.ndim)]) for dim in (source, target)]
    chosen = jax.random.permutation(own_key, shards_of)[partner]
    strong = (owner == chosen) | (owner == (partner + shards_of // 2) % shards_of)
    return jnp.where(strong, factor * array, array)


def block_scale(rng, extent, split, low, largest):
    loudness = 1.0
    for position, blocks in split:
        heights = jax.random.uniform(jax.random.fold_in(jax.random.fold_in(rng, 6), position), (blocks,), jnp.float32, low / len(split), largest / len(split))
        loudness = loudness * jnp.repeat(jnp.exp(heights), extent[position] // blocks).reshape((-1,) + (1,) * (len(extent) - 1 - position))
    return loudness


def bell_draw(own_key, dims, scale, limit, split=(), kind=jnp.bfloat16):
    loudness = block_scale(own_key, dims, split, -0.22, 0.18) if split else 1.0
    drawn = jax.random.normal(own_key, dims, jnp.float32) * scale * loudness
    return jnp.minimum(jnp.maximum(drawn, -limit), limit).astype(kind)


def heavy_noise(own_key, dims, scale, reach, cuts, heavy, dtype=jnp.bfloat16):
    result = scale * jax.random.normal(own_key, dims, jnp.float32)
    if cuts:
        result = result * block_scale(own_key, dims, cuts, -0.22, 0.18)
    return jnp.clip(spiked(result, jax.random.fold_in(own_key, 3), *heavy), -reach, reach).astype(dtype)


def setup_inputs(seed: int = 0) -> dict:
    key_list = jax.random.split(jax.random.key(seed), 5)
    inputs = heavy_noise(key_list[0], (SEQS, LENGTH, D), 1.0, 6.0, ((0, 4), (1, 32)), (1, 2, 32, 2.75))
    grad_out = bell_draw(key_list[1], (SEQS, LENGTH, HEADS * HEAD_DIM), 1.0, 6.0, ((0, 4), (1, 32)))
    saved = bell_draw(key_list[2], (SEQS, N_CTX, HEADS, HEAD_DIM, HEAD_DIM), 0.7, 6.0, ((0, 4), (1, 32)), jnp.float32)
    w_qkv = bell_draw(key_list[3], (D, 3 * HEADS * HEAD_DIM), D ** -0.5, 0.125, ((0, 4),))
    return {"inputs": inputs, "grad_out": grad_out, "saved": saved, "w_qkv": w_qkv}


def block_grads(carry, pieces):
    rows, qkv, cot, state, later = pieces
    width = HEADS * HEAD_DIM
    alpha = 1.0 / (HEAD_DIM ** 0.5)
    beta = 1.0 / ((HEAD_DIM * LENGTH) ** 0.5)
    query = qkv[:, 0].astype(jnp.float32)
    keyed = qkv[:, 1].astype(jnp.float32)
    valued = qkv[:, 2].astype(jnp.float32)
    cotf = cot.astype(jnp.float32)
    pos = jnp.arange(TOK_DEV)
    mask = (pos[:, None] >= pos[None, :])[None]
    first = jnp.where(mask, jnp.einsum("thj,shj->hts", cotf, valued), 0.0).astype(jnp.bfloat16).astype(jnp.float32)
    second = jnp.where(mask, jnp.einsum("thi,shi->hts", query, keyed), 0.0).astype(jnp.bfloat16).astype(jnp.float32)
    hp = lax.Precision.HIGHEST
    grad_q = alpha * jnp.einsum("thj,hij->thi", cotf, state, precision=hp) + beta * jnp.einsum("hts,shi->thi", first, keyed)
    grad_k = beta * (jnp.einsum("hts,thi->shi", first, query) + jnp.einsum("shj,hij->shi", valued, later, precision=hp))
    grad_v = beta * (jnp.einsum("hts,thj->shj", second, cotf) + jnp.einsum("shi,hij->shj", keyed, later, precision=hp))
    dqkv = jnp.concatenate([grad_q.reshape(TOK_DEV, width), grad_k.reshape(TOK_DEV, width), grad_v.reshape(TOK_DEV, width)], axis=1).astype(jnp.bfloat16)
    carry = carry + jnp.dot(rows.T, dqkv, preferred_element_type=jnp.float32)
    return carry, dqkv


def reference(inputs, grad_out, saved, w_qkv):
    blocks = SEQS * N_CTX
    flat = inputs.reshape(-1, D)
    qkv = jnp.dot(flat, w_qkv, preferred_element_type=jnp.float32).astype(jnp.bfloat16)
    qkv = qkv.reshape(blocks, TOK_DEV, 3, HEADS, HEAD_DIM)
    cot = grad_out.reshape(blocks, TOK_DEV, HEADS, HEAD_DIM)
    local_r = jnp.einsum("cthi,cthj->chij", qkv[:, :, 0].astype(jnp.float32), cot.astype(jnp.float32))
    local_r = local_r.reshape(SEQS, N_CTX, HEADS, HEAD_DIM, HEAD_DIM)
    inclusive = jnp.cumsum(local_r[:, ::-1], axis=1)[:, ::-1]
    later = jnp.concatenate([inclusive[:, 1:], jnp.zeros_like(inclusive[:, :1])], axis=1)
    pieces = (inputs.reshape(blocks, TOK_DEV, D), qkv, cot, saved.reshape(blocks, HEADS, HEAD_DIM, HEAD_DIM), later.reshape(blocks, HEADS, HEAD_DIM, HEAD_DIM))
    start = jnp.zeros((D, 3 * HEADS * HEAD_DIM), jnp.float32)
    total, dqkv = lax.scan(block_grads, start, pieces)
    grad_x = jnp.dot(dqkv.reshape(-1, 3 * HEADS * HEAD_DIM), w_qkv.T, preferred_element_type=jnp.float32).astype(jnp.bfloat16)
    grad_w = total * (1.0 / ((SEQS * LENGTH) ** 0.5))
    return grad_x.reshape(SEQS, LENGTH, D), grad_w
```

```python
import jax
import jax.numpy as jnp
from jax import lax
from jax.experimental import pallas as pl
from jax.experimental.pallas import tpu as pltpu
from jax.sharding import PartitionSpec as P

NY, NZ, NC, NX = 4, 4, 2, 4
TOK, HD = 128, 128
BF, F32 = jnp.bfloat16, jnp.float32


def ctx_index(y, z, c):
    return (y * NZ + z) * NC + c


def ctx_hop(block, dy=0, dz=0, dc=0):
    route = [
        (ctx_index(y, z, c), ctx_index((y + dy) % NY, (z + dz) % NZ, (c + dc) % NC))
        for y in range(NY)
        for z in range(NZ)
        for c in range(NC)
    ]
    return lax.ppermute(block, "ctx", route)


def x_hop(block, dx):
    return lax.ppermute(block, "zero", [(i, (i + dx) % NX) for i in range(NX)])


def dot(a, b):
    return lax.dot_general(a, b, (((1,), (0,)), ((), ())), preferred_element_type=F32)


def dot_nt(a, b):
    return lax.dot_general(a, b, (((1,), (1,)), ((), ())), preferred_element_type=F32)


def dot_tn(a, b):
    return lax.dot_general(a, b, (((0,), (0,)), ((), ())), preferred_element_type=F32)


def call(kernel, outs, ins, scratch=(), flops=0, limit=24):
    moved = sum(a.size * a.dtype.itemsize for a in list(ins) + list(outs))
    vmem = pl.BlockSpec(memory_space=pltpu.VMEM)
    return pl.pallas_call(
        kernel,
        out_shape=list(outs),
        in_specs=[pl.BlockSpec(memory_space=pltpu.SMEM)] + [vmem] * (len(ins) - 1),
        out_specs=[vmem] * len(outs),
        scratch_shapes=list(scratch),
        compiler_params=pltpu.CompilerParams(vmem_limit_bytes=limit << 20),
        cost_estimate=pl.CostEstimate(flops=flops, bytes_accessed=moved, transcendentals=0),
    )(*ins)


def shape(dims, dtype):
    return jax.ShapeDtypeStruct(dims, dtype)


def column_block(place, step):
    return pl.ds(pl.multiple_of(lax.rem(place + NX - step, NX) * 512, 512), 512)


def project(idx, *refs):
    xs, own, other, gs = refs[0:4], refs[4:8], refs[8:12], refs[12:16]
    qkv, r, xcat = refs[16], refs[17], refs[18]
    xi, ci = idx[0], idx[3]
    for s in range(NZ):
        xcat[s * TOK : (s + 1) * TOK, :] = xs[s][...]
    for j, w in enumerate((own, other)):
        acc = dot(xcat[:, column_block(xi, 0)], w[0][...])
        for s in range(1, NX):
            acc += dot(xcat[:, column_block(xi, s)], w[s][...])
        head = lax.rem(ci + j, 2)
        rounded = acc.astype(BF)
        qkv[head] = rounded
        for s in range(NZ):
            r[head, s] = dot_tn(rounded[s * TOK : (s + 1) * TOK, :HD], gs[s][0, head])


def within(alpha, beta, idx, *refs):
    xs, gs, qkv = refs[0:4], refs[4:8], refs[8]
    dq, dk0, dv0, xt = refs[9:]
    rowi = lax.broadcasted_iota(jnp.int32, (TOK, TOK), 0)
    coli = lax.broadcasted_iota(jnp.int32, (TOK, TOK), 1)
    mask = rowi >= coli
    for head in range(2):
        for s in range(NZ):
            rows = slice(s * TOK, (s + 1) * TOK)
            q, k, v = (qkv[head, rows, i * HD : (i + 1) * HD] for i in range(3))
            g, state = gs[s][0, head], gs[s][1, head]
            p1 = jnp.where(mask, dot_nt(g, v), 0.0).astype(BF)
            p2 = jnp.where(mask, dot_nt(q, k), 0.0).astype(BF)
            dq[head, rows, :] = (alpha * dot_nt(g, state) + beta * dot(p1, k)).astype(BF)
            dk0[head, rows, :] = dot_tn(p1, q)
            dv0[head, rows, :] = dot_tn(p2, g)
    for s in range(NZ):
        xt[:, s * TOK : (s + 1) * TOK] = xs[s][...].T


def finish(beta, idx, *refs):
    qkv, dq, dk0, dv0, r_own, r_other, t1, t2, t3, xt = refs[:10]
    dqkv, p_own, p_other, later = refs[10:]
    yi, zi, ci = idx[1], idx[2], idx[3]
    first = jnp.where(ci == 0, 1.0, 0.0).astype(F32)
    for head in range(2):
        acc = jnp.zeros((HD, HD), F32)
        for step, total in enumerate((t1, t2, t3)):
            use = jnp.where(yi < step + 1, 1.0, 0.0).astype(F32)
            acc += use * total[head].astype(F32)
        for z in range(NZ - 1, -1, -1):
            slot = lax.rem(zi + NZ - z, NZ)
            mate = r_other[head, slot]
            later[head, slot] = (acc + first * mate).astype(BF)
            acc += mate + r_own[head, slot]
        for s in range(NZ):
            rows = slice(s * TOK, (s + 1) * TOK)
            k, v = qkv[head, rows, HD : 2 * HD], qkv[head, rows, 2 * HD :]
            lat = later[head, s]
            dqkv[head, rows, :HD] = dq[head, rows, :]
            dqkv[head, rows, HD : 2 * HD] = (beta * (dk0[head, rows, :] + dot_nt(v, lat))).astype(BF)
            dqkv[head, rows, 2 * HD :] = (beta * (dv0[head, rows, :] + dot(k, lat))).astype(BF)
    for j, part in ((1, p_other), (0, p_own)):
        grads = dqkv[lax.rem(ci + j, 2)]
        for m in range(4):
            rows = slice(m * 512, (m + 1) * 512)
            part[rows, :] = dot(xt[rows, :], grads).astype(BF)


def back(idx, *refs):
    dqkv, own, other = refs[0], refs[1:5], refs[5:9]
    gx = refs[9:13]
    xi, ci = idx[0], idx[3]
    mine, theirs = dqkv[ci], dqkv[1 - ci]
    for s in range(NX):
        part = dot_nt(mine, own[s][...]) + dot_nt(theirs, other[s][...])
        for t in range(NZ):
            gx[t][:, column_block(xi, s)] = part[t * TOK : (t + 1) * TOK].astype(gx[t].dtype)


def split(idx, own, other, *outs):
    a, b = outs[:4], outs[4:]
    xi, yi = idx[0], idx[1]
    for s in range(4):
        to_x, to_y = lax.rem(xi + s, NX), lax.rem(yi + s, NY)
        for y in range(NY):
            for g in range(4):
                a[s][y, g] = (own[y, g, to_x].astype(F32) + other[y, g, to_x].astype(F32)).astype(BF)
        for g in range(4):
            for x in range(NX):
                b[s][g, x] = (own[to_y, 4 + g, x].astype(F32) + other[to_y, 4 + g, x].astype(F32)).astype(BF)


def turn(idx, *refs):
    a, b = refs[0:4], refs[4:8]
    a2, b2 = refs[8:12], refs[12:16]
    xi, yi = idx[0], idx[1]
    for s in range(4):
        to_x, to_y = lax.rem(xi + s, NX), lax.rem(yi + s, NY)
        for g in range(4):
            a2[s][g] = sum(p[to_y, g].astype(F32) for p in a).astype(BF)
            b2[s][g] = sum(p[g, to_x].astype(F32) for p in b).astype(BF)


def body(inputs, grad_out, saved, w_qkv):
    x = inputs[0]
    heads, head_size = saved.shape[2], saved.shape[3]
    length = x.shape[0] * lax.axis_size("ctx")
    alpha = 1.0 / head_size**0.5
    beta = 1.0 / (head_size * length) ** 0.5
    scale = 1.0 / (length * lax.axis_size("zero")) ** 0.5
    ctx = lax.axis_index("ctx")
    xi, yi, zi, ci = lax.axis_index("zero"), ctx // 8, (ctx // 2) % 4, ctx % 2
    idx = jnp.stack([xi, yi, zi, ci]).astype(jnp.int32)

    by_head = w_qkv.reshape(512, 3, heads, HD)
    own_w = lax.dynamic_index_in_dim(by_head, 2 * zi + ci, 2, keepdims=False).reshape(512, 3 * HD)
    other_w = lax.dynamic_index_in_dim(by_head, 2 * zi + 1 - ci, 2, keepdims=False).reshape(512, 3 * HD)
    steps = (1, 3, 2)
    xs = {0: x} | {s: ctx_hop(x, dz=s) for s in steps}
    own = {0: own_w} | {s: x_hop(own_w, s) for s in steps}
    other = {0: other_w} | {s: ctx_hop(own[s], dc=1) for s in steps}
    cot = grad_out[0].reshape(TOK, NZ, 2, HD).transpose(1, 2, 0, 3)
    state = saved[0, 0].astype(BF).reshape(NZ, 2, HD, HD)
    bundle = jnp.stack([cot, state], axis=1)
    gs = {}
    for s in range(4):
        piece = lax.dynamic_index_in_dim(bundle, (zi + s) % NZ, 0, keepdims=False)
        gs[s] = ctx_hop(piece, dz=s) if s else piece
    xs, own, other, gs = ([d[s] for s in range(4)] for d in (xs, own, other, gs))

    qkv, r = call(
        project,
        [shape((2, 512, 384), BF), shape((2, NZ, HD, HD), F32)],
        [idx, *xs, *own, *other, *gs],
        [pltpu.VMEM((512, 2048), BF)],
        flops=2 * 512 * 2048 * 768,
    )
    r_other = ctx_hop(r, dc=1)
    total = jnp.sum(r + r_other, axis=1).astype(BF)
    t = [ctx_hop(total, dy=s) for s in (1, 2, 3)]
    dq, dk0, dv0, xt = call(
        lambda *refs: within(alpha, beta, *refs),
        [shape((2, 512, HD), BF), shape((2, 512, HD), F32), shape((2, 512, HD), F32), shape((2048, 512), BF)],
        [idx, *xs, *gs, qkv],
        flops=8 * 6 * 2 * 128**3 * 4,
    )
    dqkv, p_own, p_other = call(
        lambda *refs: finish(beta, *refs),
        [shape((2, 512, 384), BF), shape((2048, 384), BF), shape((2048, 384), BF)],
        [idx, qkv, dq, dk0, dv0, r, r_other, *t, xt],
        [pltpu.VMEM((2, NZ, HD, HD), BF)],
        flops=2 * 512 * 2048 * 768,
    )
    p_mate = ctx_hop(p_other, dc=1)
    gx = call(
        back,
        [shape((TOK, 2048), F32)] + [shape((TOK, 2048), BF)] * 3,
        [idx, dqkv, *own, *other],
        flops=2 * 512 * 2048 * 768,
    )
    five = (NY, 8, NX, 16, 384)
    parts = call(
        split,
        [shape((NY, 4, 16, 384), BF)] * 4 + [shape((4, NX, 16, 384), BF)] * 4,
        [idx, p_own.reshape(five), p_mate.reshape(five)],
    )
    a, b = parts[:4], parts[4:]
    a = [a[0]] + [x_hop(a[s], s) for s in (1, 2, 3)]
    b = [b[0]] + [ctx_hop(b[s], dy=s) for s in (1, 2, 3)]
    gx = [gx[0]] + [ctx_hop(gx[s], dz=-s) for s in (1, 2, 3)]
    parts = call(turn, [shape((4, 16, 384), BF)] * 8, [idx, *a, *b])
    a, b = parts[:4], parts[4:]
    a = [a[0]] + [ctx_hop(a[s], dy=s) for s in (1, 2, 3)]
    b = [b[0]] + [x_hop(b[s], s) for s in (1, 2, 3)]
    owned = jnp.concatenate([sum(p.astype(F32) for p in a), sum(p.astype(F32) for p in b)], axis=0)
    groups = [[y * 8 + i for i in range(8)] for y in range(NY)]
    owned = lax.all_to_all(owned, "ctx", 0, 0, axis_index_groups=groups)
    owned = owned.reshape(heads, 16, 3, HD).transpose(1, 2, 0, 3).reshape(16, 3 * heads * HD)
    grad_x = sum(p.astype(F32) for p in gx).astype(BF)
    return (grad_x[None], owned * scale)


def solution(mesh):
    in_specs = (
        P("zero", "ctx", None),
        P("zero", "ctx", None),
        P("zero", "ctx", None, None, None),
        P("zero", None),
    )
    out_specs = (P("zero", "ctx", None), P(("ctx", "zero"), None))
    return jax.shard_map(body, mesh=mesh, in_specs=in_specs, out_specs=out_specs, check_vma=False)
```

```python
import jax
import jax.numpy as jnp
from jax import lax
from jax.experimental import pallas as pl
from jax.experimental.pallas import tpu as pltpu
from jax.sharding import PartitionSpec as P

NY, NZ, NC, NX = 4, 4, 2, 4
TOK, HD = 128, 128
BF, F32 = jnp.bfloat16, jnp.float32


def ctx_index(y, z, c):
    return (y * NZ + z) * NC + c


def ctx_hop(block, dy=0, dz=0, dc=0):
    route = [
        (ctx_index(y, z, c), ctx_index((y + dy) % NY, (z + dz) % NZ, (c + dc) % NC))
        for y in range(NY)
        for z in range(NZ)
        for c in range(NC)
    ]
    return lax.ppermute(block, "ctx", route)


def x_hop(block, dx):
    return lax.ppermute(block, "zero", [(i, (i + dx) % NX) for i in range(NX)])


def dot(a, b):
    return lax.dot_general(a, b, (((1,), (0,)), ((), ())), preferred_element_type=F32)


def dot_nt(a, b):
    return lax.dot_general(a, b, (((1,), (1,)), ((), ())), preferred_element_type=F32)


def dot_tn(a, b):
    return lax.dot_general(a, b, (((0,), (0,)), ((), ())), preferred_element_type=F32)


def call(kernel, outs, ins, scratch=(), flops=0, limit=16):
    moved = sum(a.size * a.dtype.itemsize for a in list(ins) + list(outs))
    vmem = pl.BlockSpec(memory_space=pltpu.VMEM)
    return pl.pallas_call(
        kernel,
        out_shape=list(outs),
        in_specs=[pl.BlockSpec(memory_space=pltpu.SMEM)] + [vmem] * (len(ins) - 1),
        out_specs=[vmem] * len(outs),
        scratch_shapes=list(scratch),
        compiler_params=pltpu.CompilerParams(vmem_limit_bytes=limit << 20),
        cost_estimate=pl.CostEstimate(flops=flops, bytes_accessed=moved, transcendentals=0),
    )(*ins)


def shape(dims, dtype):
    return jax.ShapeDtypeStruct(dims, dtype)


def after(value, deps):
    return lax.optimization_barrier((value, deps))[0]


def columns(place, step, start=0, size=512):
    block = lax.rem(place + NX - step, NX)
    return pl.ds(pl.multiple_of(block * 512 + start, 256), size)


PIECES = ((0, 0, 512), (1, 0, 512), (3, 0, 512), (2, 0, 256), (2, 256, 256))
TOKENS = ((0, 0, 128), (1, 0, 128), (3, 0, 128), (2, 0, 64), (2, 64, 64))


def take(idx, w, own, other, sem):
    head = 2 * idx[2] + idx[3]
    mate = 2 * idx[2] + 1 - idx[3]
    copies = []
    for i in range(3):
        for j, (h, out) in enumerate(((head, own), (mate, other))):
            at = pl.multiple_of(i * 1024 + h * HD, HD)
            copies.append(
                pltpu.make_async_copy(
                    w.at[:, pl.ds(at, HD)], out.at[:, i * HD : (i + 1) * HD], sem.at[2 * i + j]
                )
            )
    for copy in copies:
        copy.start()
    for copy in copies:
        copy.wait()


def project(idx, *refs):
    xs, mates, w, gs = refs[0:5], refs[5:10], refs[10:15], refs[15]
    xcat, qkv, r, total = refs[16:]
    xi, zi, ci = idx[0], idx[2], idx[3]
    for parity, parts in ((ci, xs), (1 - ci, mates)):
        for part, (s, start, size) in zip(parts, TOKENS, strict=True):
            block = lax.rem(zi + NZ - s, NZ) * 2 + parity
            xcat[pl.ds(pl.multiple_of(block * TOK + start, 64), size), :] = part[...]
    whole = jnp.zeros((HD, HD), F32)
    for m in range(4):
        rows = slice(m * 256, (m + 1) * 256)
        acc = jnp.zeros((256, 384), F32)
        for part, (s, start, size) in zip(w, PIECES, strict=True):
            acc += dot(xcat[rows, columns(xi, s, start, size)], part[...])
        rounded = acc.astype(BF)
        qkv[rows, :] = rounded
        for i in range(2):
            piece = dot_tn(rounded[i * TOK : (i + 1) * TOK, :HD], gs[2 * m + i, 0])
            r[2 * m + i] = piece
            whole += piece
    total[...] = whole.astype(BF)


def within(alpha, beta, idx, xcat, gs, qkv, dq, dk0, dv0, xt):
    rowi = lax.broadcasted_iota(jnp.int32, (TOK, TOK), 0)
    coli = lax.broadcasted_iota(jnp.int32, (TOK, TOK), 1)
    mask = rowi >= coli
    for b in range(8):
        rows = slice(b * TOK, (b + 1) * TOK)
        q, k, v = (qkv[rows, i * HD : (i + 1) * HD] for i in range(3))
        g, state = gs[b, 0], gs[b, 1]
        p1 = jnp.where(mask, dot_nt(g, v), 0.0).astype(BF)
        p2 = jnp.where(mask, dot_nt(q, k), 0.0).astype(BF)
        dq[rows, :] = (alpha * dot_nt(g, state) + beta * dot(p1, k)).astype(BF)
        dk0[rows, :] = dot_tn(p1, q)
        dv0[rows, :] = dot_tn(p2, g)
        xt[:, rows] = xcat[rows, :].T


def finish(beta, idx, qkv, dq, dk0, dv0, r, t1, t2, t3, dqkv, keep, send):
    yi, ci = idx[1], idx[3]
    acc = jnp.zeros((HD, HD), F32)
    for step, total in enumerate((t1, t2, t3)):
        use = jnp.where(yi < step + 1, 1.0, 0.0).astype(F32)
        acc += use * total[...].astype(F32)
    for b in range(7, -1, -1):
        rows = slice(b * TOK, (b + 1) * TOK)
        k, v = qkv[rows, HD : 2 * HD], qkv[rows, 2 * HD :]
        later = acc.astype(BF)
        dqkv[rows, :HD] = dq[rows, :]
        dqkv[rows, HD : 2 * HD] = (beta * (dk0[rows, :] + dot_nt(v, later))).astype(BF)
        dqkv[rows, 2 * HD :] = (beta * (dv0[rows, :] + dot(k, later))).astype(BF)
        acc += r[b]
    for z in range(NZ):
        keep[z] = dqkv[pl.ds(pl.multiple_of((2 * z + ci) * TOK, TOK), TOK), :]
        send[z] = dqkv[pl.ds(pl.multiple_of((2 * z + 1 - ci) * TOK, TOK), TOK), :]


def weights(idx, xt, dqkv, *refs):
    a, b, buf = refs[:4], refs[4:8], refs[8]
    xi, yi = idx[0], idx[1]
    for m in range(4):
        tile = dot(xt[m * 512 : (m + 1) * 512, :], dqkv[...])
        buf[m] = tile.reshape(8, NX, 16, 384)
    for s in range(4):
        to_x, to_y = lax.rem(xi + s, NX), lax.rem(yi + s, NY)
        for i in range(4):
            for g in range(4):
                a[s][i, g] = buf[i, g, to_x].astype(BF)
                b[s][g, i] = buf[to_y, 4 + g, i].astype(BF)


def back(idx, *refs):
    keep, got, own, other = refs[0], refs[1], refs[2:7], refs[7:12]
    mine_gx, up, down, far_up, far_down, gx = refs[12:]
    xi, zi = idx[0], idx[2]
    mine = keep[...].reshape(512, 384)
    theirs = got[...].reshape(512, 384)
    for p, q, (s, start, size) in zip(own, other, PIECES, strict=True):
        part = dot_nt(mine, p[...]) + dot_nt(theirs, q[...])
        gx[:, :, columns(xi, s, start, size)] = part.reshape(NZ, TOK, size)
    mine_gx[...] = gx[zi]
    up[...] = gx[lax.rem(zi + 1, NZ)].astype(BF)
    down[...] = gx[lax.rem(zi + 3, NZ)].astype(BF)
    far = lax.rem(zi + 2, NZ)
    far_up[...] = gx[far, :64, :].astype(BF)
    far_down[...] = gx[far, 64:, :].astype(BF)


def merge(idx, up, down, from_low, from_high, new_up, new_down):
    new_up[:64, :] = (up[:64, :].astype(F32) + from_low[...].astype(F32)).astype(BF)
    new_up[64:, :] = up[64:, :]
    new_down[:64, :] = down[:64, :]
    new_down[64:, :] = (down[64:, :].astype(F32) + from_high[...].astype(F32)).astype(BF)


def turn(idx, *refs):
    a, b = refs[0:4], refs[4:8]
    a2, b2 = refs[8:12], refs[12:16]
    xi, yi = idx[0], idx[1]
    for s in range(4):
        to_x, to_y = lax.rem(xi + s, NX), lax.rem(yi + s, NY)
        for g in range(4):
            a2[s][g] = sum(p[to_y, g].astype(F32) for p in a).astype(BF)
            b2[s][g] = sum(p[g, to_x].astype(F32) for p in b).astype(BF)


def body(inputs, grad_out, saved, w_qkv):
    x = inputs[0]
    heads, head_size = saved.shape[2], saved.shape[3]
    length = x.shape[0] * lax.axis_size("ctx")
    alpha = 1.0 / head_size**0.5
    beta = 1.0 / (head_size * length) ** 0.5
    scale = 1.0 / (length * lax.axis_size("zero")) ** 0.5
    ctx = lax.axis_index("ctx")
    xi, yi, zi, ci = lax.axis_index("zero"), ctx // 8, (ctx // 2) % 4, ctx % 2
    idx = jnp.stack([xi, yi, zi, ci]).astype(jnp.int32)
    rows_y = [[ctx_index(y, z, c) for z in range(NZ) for c in range(NC)] for y in range(NY)]

    x1, x3 = ctx_hop(x, dz=1), ctx_hop(x, dz=-1)
    own_w, other_w = pl.pallas_call(
        take,
        out_shape=[shape((512, 384), BF)] * 2,
        in_specs=[pl.BlockSpec(memory_space=pltpu.SMEM), pl.BlockSpec(memory_space=pltpu.HBM)],
        out_specs=[pl.BlockSpec(memory_space=pltpu.VMEM)] * 2,
        scratch_shapes=[pltpu.SemaphoreType.DMA((6,))],
        compiler_params=pltpu.CompilerParams(vmem_limit_bytes=4 << 20),
    )(idx, w_qkv)
    w1, w3 = x_hop(own_w, 1), x_hop(own_w, -1)
    x2a, x2b = ctx_hop(x1[:64], dz=1), ctx_hop(x3[64:], dz=-1)
    w2a, w2b = x_hop(w1[:256], 1), x_hop(w3[256:], -1)
    xs, own = [x, x1, x3, x2a, x2b], [own_w, w1, w3, w2a, w2b]
    mates = [ctx_hop(p, dc=1) for p in xs]
    other = [other_w] + [ctx_hop(p, dc=1) for p in own[1:]]
    cot = grad_out[0].reshape(TOK, heads, HD).transpose(1, 0, 2)
    bundle = jnp.stack([cot, saved[0, 0].astype(BF)], axis=1)
    gs = lax.all_to_all(bundle, "ctx", 0, 0, axis_index_groups=rows_y)

    big = 2 * 1024 * 2048 * 384
    xcat, qkv, r, total = call(
        project,
        [shape((1024, 2048), BF), shape((1024, 384), BF), shape((8, HD, HD), F32), shape((HD, HD), BF)],
        [idx, *xs, *mates, *own, gs],
        flops=big,
    )
    totals = [ctx_hop(total, dy=s) for s in (1, 2, 3)]
    dq, dk0, dv0, xt = call(
        lambda *refs: within(alpha, beta, *refs),
        [shape((1024, HD), BF), shape((1024, HD), F32), shape((1024, HD), F32), shape((2048, 1024), BF)],
        [idx, xcat, gs, qkv],
        flops=big // 4,
    )
    dqkv, keep, send = call(
        lambda *refs: finish(beta, *refs),
        [shape((1024, 384), BF), shape((NZ, TOK, 384), BF), shape((NZ, TOK, 384), BF)],
        [after(idx, other), qkv, dq, dk0, dv0, r, *totals],
        flops=big // 16,
    )
    got = ctx_hop(send, dc=1)
    parts = call(
        weights,
        [shape((NY, 4, 16, 384), BF)] * 4 + [shape((4, NX, 16, 384), BF)] * 4,
        [idx, xt, dqkv],
        [pltpu.VMEM((NY, 8, NX, 16, 384), F32)],
        flops=big,
    )
    a, b = parts[:4], parts[4:]
    a = [a[0]] + [x_hop(a[s], s) for s in (1, 2, 3)]
    b = [b[0]] + [ctx_hop(b[s], dy=s) for s in (1, 2, 3)]
    gx, up, down, far_up, far_down = call(
        back,
        [shape((TOK, 2048), F32)] + [shape((TOK, 2048), BF)] * 2 + [shape((64, 2048), BF)] * 2,
        [idx, keep, got, *own, *other],
        [pltpu.VMEM((NZ, TOK, 2048), F32)],
        flops=big,
    )
    far_up, far_down = ctx_hop(far_up, dz=1), ctx_hop(far_down, dz=-1)
    up, down = call(merge, [shape((TOK, 2048), BF)] * 2, [idx, up, down, far_up, far_down])
    parts = call(turn, [shape((4, 16, 384), BF)] * 8, [after(idx, up), *a, *b])
    up, down = ctx_hop(up, dz=1), ctx_hop(down, dz=-1)
    a, b = parts[:4], parts[4:]
    a = [a[0]] + [ctx_hop(a[s], dy=s) for s in (1, 2, 3)]
    b = [b[0]] + [x_hop(b[s], s) for s in (1, 2, 3)]
    owned = jnp.concatenate([sum(p.astype(F32) for p in a), sum(p.astype(F32) for p in b)], axis=0)
    owned = lax.all_to_all(owned, "ctx", 0, 0, axis_index_groups=rows_y)
    owned = owned.reshape(heads, 16, 3, HD).transpose(1, 2, 0, 3).reshape(16, 3 * heads * HD)
    grad_x = (gx + up.astype(F32) + down.astype(F32)).astype(BF)
    return (grad_x[None], owned * scale)


def solution(mesh):
    in_specs = (
        P("zero", "ctx", None),
        P("zero", "ctx", None),
        P("zero", "ctx", None, None, None),
        P("zero", None),
    )
    out_specs = (P("zero", "ctx", None), P(("ctx", "zero"), None))
    return jax.shard_map(body, mesh=mesh, in_specs=in_specs, out_specs=out_specs, check_vma=False)
```

```python
import jax
import jax.numpy as jnp
from jax import lax
from jax.experimental import pallas as pl
from jax.experimental.pallas import tpu as pltpu
from jax.sharding import PartitionSpec as P

NY, NZ, NC, NX = 4, 4, 2, 4
TOK, HD = 128, 128
BF, F32 = jnp.bfloat16, jnp.float32


def ctx_index(y, z, c):
    return (y * NZ + z) * NC + c


def ctx_hop(block, dy=0, dz=0, dc=0):
    route = [
        (ctx_index(y, z, c), ctx_index((y + dy) % NY, (z + dz) % NZ, (c + dc) % NC))
        for y in range(NY)
        for z in range(NZ)
        for c in range(NC)
    ]
    return lax.ppermute(block, "ctx", route)


def x_hop(block, dx):
    return lax.ppermute(block, "zero", [(i, (i + dx) % NX) for i in range(NX)])


def dot(a, b):
    return lax.dot_general(a, b, (((1,), (0,)), ((), ())), preferred_element_type=F32)


def dot_nt(a, b):
    return lax.dot_general(a, b, (((1,), (1,)), ((), ())), preferred_element_type=F32)


def dot_tn(a, b):
    return lax.dot_general(a, b, (((0,), (0,)), ((), ())), preferred_element_type=F32)


def call(kernel, outs, ins, scratch=(), flops=0, limit=16):
    moved = sum(a.size * a.dtype.itemsize for a in list(ins) + list(outs))
    vmem = pl.BlockSpec(memory_space=pltpu.VMEM)
    return pl.pallas_call(
        kernel,
        out_shape=list(outs),
        in_specs=[pl.BlockSpec(memory_space=pltpu.SMEM)] + [vmem] * (len(ins) - 1),
        out_specs=[vmem] * len(outs),
        scratch_shapes=list(scratch),
        compiler_params=pltpu.CompilerParams(vmem_limit_bytes=limit << 20),
        cost_estimate=pl.CostEstimate(flops=flops, bytes_accessed=moved, transcendentals=0),
    )(*ins)


def shape(dims, dtype):
    return jax.ShapeDtypeStruct(dims, dtype)


def after(value, deps):
    return lax.optimization_barrier((value, deps))[0]


def columns(place, step, start=0, size=512):
    block = lax.rem(place + NX - step, NX)
    return pl.ds(pl.multiple_of(block * 512 + start, 256), size)


PIECES = ((0, 0, 512), (1, 0, 512), (3, 0, 512), (2, 0, 256), (2, 256, 256))
TOKENS = ((0, 0, 128), (1, 0, 128), (3, 0, 128), (2, 0, 64), (2, 64, 64))


def take(idx, w, own, sem):
    head = 2 * idx[2] + idx[3]
    copies = []
    for i in range(3):
        at = pl.multiple_of(i * 1024 + head * HD, HD)
        copies.append(
            pltpu.make_async_copy(w.at[:, pl.ds(at, HD)], own.at[:, i * HD : (i + 1) * HD], sem.at[i])
        )
    for copy in copies:
        copy.start()
    for copy in copies:
        copy.wait()


def project(idx, *refs):
    xs, mates, w, gs = refs[0:5], refs[5:10], refs[10:15], refs[15]
    xcat, qkv, r, total, wkeep = refs[16:]
    xi, zi, ci = idx[0], idx[2], idx[3]
    for parity, parts in ((ci, xs), (1 - ci, mates)):
        for part, (s, start, size) in zip(parts, TOKENS, strict=True):
            block = lax.rem(zi + NZ - s, NZ) * 2 + parity
            xcat[pl.ds(pl.multiple_of(block * TOK + start, 64), size), :] = part[...]
    for part, (s, start, size) in zip(w, PIECES, strict=True):
        wkeep[columns(xi, s, start, size), :] = part[...]
    whole = jnp.zeros((HD, HD), F32)
    for m in range(4):
        rows = slice(m * 256, (m + 1) * 256)
        rounded = dot(xcat[rows, :], wkeep[...]).astype(BF)
        qkv[rows, :] = rounded
        for i in range(2):
            piece = dot_tn(rounded[i * TOK : (i + 1) * TOK, :HD], gs[2 * m + i, 0])
            r[2 * m + i] = piece
            whole += piece
    total[...] = whole.astype(BF)


def within(alpha, beta, idx, xcat, gs, qkv, dq, dk0, dv0, xt):
    rowi = lax.broadcasted_iota(jnp.int32, (TOK, TOK), 0)
    coli = lax.broadcasted_iota(jnp.int32, (TOK, TOK), 1)
    mask = rowi >= coli
    for b in range(8):
        rows = slice(b * TOK, (b + 1) * TOK)
        q, k, v = (qkv[rows, i * HD : (i + 1) * HD] for i in range(3))
        g, state = gs[b, 0], gs[b, 1]
        p1 = jnp.where(mask, dot_nt(g, v), 0.0).astype(BF)
        p2 = jnp.where(mask, dot_nt(q, k), 0.0).astype(BF)
        dq[rows, :] = (alpha * dot_nt(g, state) + beta * dot(p1, k)).astype(BF)
        dk0[rows, :] = dot_tn(p1, q)
        dv0[rows, :] = dot_tn(p2, g)
        xt[:, rows] = xcat[rows, :].T


def finish(beta, idx, qkv, dq, dk0, dv0, r, t1, t2, t3, dqkv, keep, send):
    yi, ci = idx[1], idx[3]
    acc = jnp.zeros((HD, HD), F32)
    for step, total in enumerate((t1, t2, t3)):
        use = jnp.where(yi < step + 1, 1.0, 0.0).astype(F32)
        acc += use * total[...].astype(F32)
    for b in range(7, -1, -1):
        rows = slice(b * TOK, (b + 1) * TOK)
        k, v = qkv[rows, HD : 2 * HD], qkv[rows, 2 * HD :]
        later = acc.astype(BF)
        dqkv[rows, :HD] = dq[rows, :]
        dqkv[rows, HD : 2 * HD] = (beta * (dk0[rows, :] + dot_nt(v, later))).astype(BF)
        dqkv[rows, 2 * HD :] = (beta * (dv0[rows, :] + dot(k, later))).astype(BF)
        acc += r[b]
    for z in range(NZ):
        keep[z] = dqkv[pl.ds(pl.multiple_of((2 * z + ci) * TOK, TOK), TOK), :]
        send[z] = dqkv[pl.ds(pl.multiple_of((2 * z + 1 - ci) * TOK, TOK), TOK), :]


def weights(idx, xt, dqkv, part):
    for m in range(4):
        rows = slice(m * 512, (m + 1) * 512)
        part[rows, :] = dot(xt[rows, :], dqkv[...]).astype(BF)


def back(idx, keep, got, own, other, mine_gx, up, down, far_up, far_down, gx):
    zi = idx[2]
    mine = keep[...].reshape(512, 384)
    theirs = got[...].reshape(512, 384)
    for n in range(4):
        cols = slice(n * 512, (n + 1) * 512)
        part = dot_nt(mine, own[cols, :]) + dot_nt(theirs, other[cols, :])
        gx[:, :, cols] = part.reshape(NZ, TOK, 512)
    mine_gx[...] = gx[zi]
    up[...] = gx[lax.rem(zi + 1, NZ)].astype(BF)
    down[...] = gx[lax.rem(zi + 3, NZ)].astype(BF)
    far = lax.rem(zi + 2, NZ)
    far_up[...] = gx[far, :64, :].astype(BF)
    far_down[...] = gx[far, 64:, :].astype(BF)


def merge(idx, up, down, from_low, from_high, new_up, new_down):
    new_up[:64, :] = (up[:64, :].astype(F32) + from_low[...].astype(F32)).astype(BF)
    new_up[64:, :] = up[64:, :]
    new_down[:64, :] = down[:64, :]
    new_down[64:, :] = (down[64:, :].astype(F32) + from_high[...].astype(F32)).astype(BF)


def collect(scale, idx, parts, out):
    for head in range(8):
        acc = jnp.zeros((16, 384), F32)
        for y in range(NY):
            for x in range(NX):
                acc += parts[(y * 8 + head) * NX + x].astype(F32)
        for i in range(3):
            at = i * 1024 + head * HD
            out[:, at : at + HD] = acc[:, i * HD : (i + 1) * HD] * scale


def body(inputs, grad_out, saved, w_qkv):
    x = inputs[0]
    heads, head_size = saved.shape[2], saved.shape[3]
    length = x.shape[0] * lax.axis_size("ctx")
    alpha = 1.0 / head_size**0.5
    beta = 1.0 / (head_size * length) ** 0.5
    scale = 1.0 / (length * lax.axis_size("zero")) ** 0.5
    ctx = lax.axis_index("ctx")
    xi, yi, zi, ci = lax.axis_index("zero"), ctx // 8, (ctx // 2) % 4, ctx % 2
    idx = jnp.stack([xi, yi, zi, ci]).astype(jnp.int32)
    rows_y = [[ctx_index(y, z, c) for z in range(NZ) for c in range(NC)] for y in range(NY)]

    x1, x3 = ctx_hop(x, dz=1), ctx_hop(x, dz=-1)
    (own_w,) = pl.pallas_call(
        take,
        out_shape=[shape((512, 384), BF)],
        in_specs=[pl.BlockSpec(memory_space=pltpu.SMEM), pl.BlockSpec(memory_space=pltpu.HBM)],
        out_specs=[pl.BlockSpec(memory_space=pltpu.VMEM)],
        scratch_shapes=[pltpu.SemaphoreType.DMA((3,))],
        compiler_params=pltpu.CompilerParams(vmem_limit_bytes=4 << 20),
        cost_estimate=pl.CostEstimate(flops=0, bytes_accessed=2 * 512 * 384 * 2, transcendentals=0),
    )(idx, w_qkv)
    cot = grad_out[0].reshape(TOK, heads, HD).transpose(1, 0, 2)
    bundle = jnp.stack([cot, saved[0, 0].astype(BF)], axis=1)
    gs = lax.all_to_all(bundle, "ctx", 0, 0, axis_index_groups=rows_y)
    w1, w3 = x_hop(own_w, 1), x_hop(own_w, -1)
    x2a, x2b = ctx_hop(x1[:64], dz=1), ctx_hop(x3[64:], dz=-1)
    w2a, w2b = x_hop(w1[:256], 1), x_hop(w3[256:], -1)
    xs, own = [x, x1, x3, x2a, x2b], [own_w, w1, w3, w2a, w2b]
    mates = [ctx_hop(after(p, gs) if i else p, dc=1) for i, p in enumerate(xs)]

    big = 2 * 1024 * 2048 * 384
    xcat, qkv, r, total, own_w = call(
        project,
        [
            shape((1024, 2048), BF),
            shape((1024, 384), BF),
            shape((8, HD, HD), F32),
            shape((HD, HD), BF),
            shape((2048, 384), BF),
        ],
        [idx, *xs, *mates, *own, gs],
        flops=big,
    )
    totals = [ctx_hop(total, dy=s) for s in (1, 2, 3)]
    other_w = ctx_hop(own_w, dc=1)
    dq, dk0, dv0, xt = call(
        lambda *refs: within(alpha, beta, *refs),
        [shape((1024, HD), BF), shape((1024, HD), F32), shape((1024, HD), F32), shape((2048, 1024), BF)],
        [idx, xcat, gs, qkv],
        flops=big // 4,
    )
    dqkv, keep, send = call(
        lambda *refs: finish(beta, *refs),
        [shape((1024, 384), BF), shape((NZ, TOK, 384), BF), shape((NZ, TOK, 384), BF)],
        [idx, qkv, dq, dk0, dv0, r, *totals],
        flops=big // 16,
    )
    got = ctx_hop(send, dc=1)
    (part,) = call(weights, [shape((2048, 384), BF)], [idx, xt, dqkv], flops=big)
    parts = lax.all_to_all(part.reshape(128, 16, 384), ("ctx", "zero"), 0, 0)
    gx, up, down, far_up, far_down = call(
        back,
        [shape((TOK, 2048), F32)] + [shape((TOK, 2048), BF)] * 2 + [shape((64, 2048), BF)] * 2,
        [after(idx, part), keep, got, own_w, other_w],
        [pltpu.VMEM((NZ, TOK, 2048), F32)],
        flops=big,
    )
    far_up, far_down = ctx_hop(far_up, dz=1), ctx_hop(far_down, dz=-1)
    up, down = call(merge, [shape((TOK, 2048), BF)] * 2, [idx, up, down, far_up, far_down])
    up, down = ctx_hop(up, dz=1), ctx_hop(down, dz=-1)
    (grad_w,) = call(
        lambda *refs: collect(scale, *refs), [shape((16, 3 * heads * HD), F32)], [idx, parts]
    )
    grad_x = (gx + up.astype(F32) + down.astype(F32)).astype(BF)
    return (grad_x[None], grad_w)


def solution(mesh):
    in_specs = (
        P("zero", "ctx", None),
        P("zero", "ctx", None),
        P("zero", "ctx", None, None, None),
        P("zero", None),
    )
    out_specs = (P("zero", "ctx", None), P(("ctx", "zero"), None))
    return jax.shard_map(body, mesh=mesh, in_specs=in_specs, out_specs=out_specs, check_vma=False)
```

```python
import jax
import jax.numpy as jnp
from jax import lax
from jax.experimental import pallas as pl
from jax.experimental.pallas import tpu as pltpu
from jax.sharding import PartitionSpec as P

NY, NZ, NC, NX = 4, 4, 2, 4
TOK, HD = 128, 128
BF, F32 = jnp.bfloat16, jnp.float32


def ctx_index(y, z, c):
    return (y * NZ + z) * NC + c


def ctx_hop(block, dy=0, dz=0, dc=0):
    route = [
        (ctx_index(y, z, c), ctx_index((y + dy) % NY, (z + dz) % NZ, (c + dc) % NC))
        for y in range(NY)
        for z in range(NZ)
        for c in range(NC)
    ]
    return lax.ppermute(block, "ctx", route)


def x_hop(block, dx):
    return lax.ppermute(block, "zero", [(i, (i + dx) % NX) for i in range(NX)])


def plane_hop(block, step, stage):
    route = []
    for y in range(NY):
        for z in range(NZ):
            for c in range(NC):
                for x in range(NX):
                    dx, dy = (step, 0) if c == stage else (0, step)
                    to = ctx_index((y + dy) % NY, z, c) * NX + (x + dx) % NX
                    route.append((ctx_index(y, z, c) * NX + x, to))
    return lax.ppermute(block, ("ctx", "zero"), route)


def dot(a, b):
    return lax.dot_general(a, b, (((1,), (0,)), ((), ())), preferred_element_type=F32)


def dot_nt(a, b):
    return lax.dot_general(a, b, (((1,), (1,)), ((), ())), preferred_element_type=F32)


def dot_tn(a, b):
    return lax.dot_general(a, b, (((0,), (0,)), ((), ())), preferred_element_type=F32)


def call(kernel, outs, ins, scratch=(), flops=0, limit=16):
    moved = sum(a.size * a.dtype.itemsize for a in list(ins) + list(outs))
    vmem = pl.BlockSpec(memory_space=pltpu.VMEM)
    return pl.pallas_call(
        kernel,
        out_shape=list(outs),
        in_specs=[pl.BlockSpec(memory_space=pltpu.SMEM)] + [vmem] * (len(ins) - 1),
        out_specs=[vmem] * len(outs),
        scratch_shapes=list(scratch),
        compiler_params=pltpu.CompilerParams(vmem_limit_bytes=limit << 20),
        cost_estimate=pl.CostEstimate(flops=flops, bytes_accessed=moved, transcendentals=0),
    )(*ins)


def shape(dims, dtype):
    return jax.ShapeDtypeStruct(dims, dtype)


def after(value, deps):
    return lax.optimization_barrier((value, deps))[0]


def columns(place, step, start=0, size=512):
    block = lax.rem(place + NX - step, NX)
    return pl.ds(pl.multiple_of(block * 512 + start, 256), size)


PIECES = ((0, 0, 512), (1, 0, 512), (3, 0, 512), (2, 0, 256), (2, 256, 256))
TOKENS = ((0, 0, 128), (1, 0, 128), (3, 0, 128), (2, 0, 64), (2, 64, 64))


def pack(idx, cot, state, out):
    for h in range(8):
        out[h, 0] = cot[:, h * HD : (h + 1) * HD]
        out[h, 1] = state[h].astype(BF)


def project(idx, *refs):
    xs, mates, w, gs = refs[0:5], refs[5:10], refs[10:15], refs[15]
    xcat, qkv, r, total, wkeep = refs[16:]
    xi, zi, ci = idx[0], idx[2], idx[3]
    for parity, parts in ((ci, xs), (1 - ci, mates)):
        for part, (s, start, size) in zip(parts, TOKENS, strict=True):
            block = lax.rem(zi + NZ - s, NZ) * 2 + parity
            xcat[pl.ds(pl.multiple_of(block * TOK + start, 64), size), :] = part[...]
    for part, (s, start, size) in zip(w, PIECES, strict=True):
        wkeep[columns(xi, s, start, size), :] = part[...]
    whole = jnp.zeros((HD, HD), F32)
    for m in range(4):
        rows = slice(m * 256, (m + 1) * 256)
        rounded = dot(xcat[rows, :], wkeep[...]).astype(BF)
        qkv[rows, :] = rounded
        for i in range(2):
            piece = dot_tn(rounded[i * TOK : (i + 1) * TOK, :HD], gs[2 * m + i, 0])
            r[2 * m + i] = piece
            whole += piece
    total[...] = whole.astype(BF)


def within(alpha, beta, idx, xcat, gs, qkv, dq, dk0, dv0, xt):
    rowi = lax.broadcasted_iota(jnp.int32, (TOK, TOK), 0)
    coli = lax.broadcasted_iota(jnp.int32, (TOK, TOK), 1)
    mask = rowi >= coli
    for b in range(8):
        rows = slice(b * TOK, (b + 1) * TOK)
        q, k, v = (qkv[rows, i * HD : (i + 1) * HD] for i in range(3))
        g, state = gs[b, 0], gs[b, 1]
        p1 = jnp.where(mask, dot_nt(g, v), 0.0).astype(BF)
        p2 = jnp.where(mask, dot_nt(q, k), 0.0).astype(BF)
        dq[rows, :] = (alpha * dot_nt(g, state) + beta * dot(p1, k)).astype(BF)
        dk0[rows, :] = dot_tn(p1, q)
        dv0[rows, :] = dot_tn(p2, g)
        xt[:, rows] = xcat[rows, :].T


def finish(beta, idx, qkv, dq, dk0, dv0, r, t1, t2, t3, dqkv, keep, send):
    yi, ci = idx[1], idx[3]
    acc = jnp.zeros((HD, HD), F32)
    for step, total in enumerate((t1, t2, t3)):
        use = jnp.where(yi < step + 1, 1.0, 0.0).astype(F32)
        acc += use * total[...].astype(F32)
    for b in range(7, -1, -1):
        rows = slice(b * TOK, (b + 1) * TOK)
        k, v = qkv[rows, HD : 2 * HD], qkv[rows, 2 * HD :]
        later = acc.astype(BF)
        dqkv[rows, :HD] = dq[rows, :]
        dqkv[rows, HD : 2 * HD] = (beta * (dk0[rows, :] + dot_nt(v, later))).astype(BF)
        dqkv[rows, 2 * HD :] = (beta * (dv0[rows, :] + dot(k, later))).astype(BF)
        acc += r[b]
    for z in range(NZ):
        keep[z] = dqkv[pl.ds(pl.multiple_of((2 * z + ci) * TOK, TOK), TOK), :]
        send[z] = dqkv[pl.ds(pl.multiple_of((2 * z + 1 - ci) * TOK, TOK), TOK), :]


def weights(idx, xt, dqkv, *refs):
    outs, buf = refs[:4], refs[4]
    xi, yi, ci = idx[0], idx[1], idx[3]
    for m in range(4):
        tile = dot(xt[m * 512 : (m + 1) * 512, :], dqkv[...]).astype(BF)
        buf[m] = tile.reshape(8, NX, 16, 384)
    for s in range(4):
        for j in range(4):
            y = jnp.where(ci == 0, j, lax.rem(yi + s, NY))
            x = jnp.where(ci == 0, lax.rem(xi + s, NX), j)
            for g in range(8):
                outs[s][j, g] = buf[y, g, x]


def turn(idx, *refs):
    parts, outs = refs[:4], refs[4:]
    place = jnp.where(idx[3] == 0, idx[1], idx[0])
    for s in range(4):
        j = lax.rem(place + s, 4)
        for g in range(8):
            outs[s][g] = sum(p[j, g].astype(F32) for p in parts).astype(BF)


def back(idx, keep, got, own, other, mine_gx, up, down, far_up, far_down, gx):
    zi = idx[2]
    mine = keep[...].reshape(512, 384)
    theirs = got[...].reshape(512, 384)
    for n in range(4):
        cols = slice(n * 512, (n + 1) * 512)
        part = dot_nt(mine, own[cols, :]) + dot_nt(theirs, other[cols, :])
        gx[:, :, cols] = part.reshape(NZ, TOK, 512)
    mine_gx[...] = gx[zi]
    up[...] = gx[lax.rem(zi + 1, NZ)].astype(BF)
    down[...] = gx[lax.rem(zi + 3, NZ)].astype(BF)
    far = lax.rem(zi + 2, NZ)
    far_up[...] = gx[far, :64, :].astype(BF)
    far_down[...] = gx[far, 64:, :].astype(BF)


def merge(idx, up, down, from_low, from_high, new_up, new_down):
    new_up[:64, :] = (up[:64, :].astype(F32) + from_low[...].astype(F32)).astype(BF)
    new_up[64:, :] = up[64:, :]
    new_down[:64, :] = down[:64, :]
    new_down[64:, :] = (down[64:, :].astype(F32) + from_high[...].astype(F32)).astype(BF)


def collect(scale, idx, parts, out):
    for head in range(8):
        for i in range(3):
            at = i * 1024 + head * HD
            out[:, at : at + HD] = parts[head, :, i * HD : (i + 1) * HD] * scale


def body(inputs, grad_out, saved, w_qkv):
    x = inputs[0]
    heads, head_size = saved.shape[2], saved.shape[3]
    length = x.shape[0] * lax.axis_size("ctx")
    alpha = 1.0 / head_size**0.5
    beta = 1.0 / (head_size * length) ** 0.5
    scale = 1.0 / (length * lax.axis_size("zero")) ** 0.5
    ctx = lax.axis_index("ctx")
    xi, yi, zi, ci = lax.axis_index("zero"), ctx // 8, (ctx // 2) % 4, ctx % 2
    idx = jnp.stack([xi, yi, zi, ci]).astype(jnp.int32)
    rows_y = [[ctx_index(y, z, c) for z in range(NZ) for c in range(NC)] for y in range(NY)]

    x1, x3 = ctx_hop(x, dz=1), ctx_hop(x, dz=-1)
    at = (2 * zi + ci) * HD
    own_w = jnp.concatenate(
        [lax.dynamic_slice(w_qkv, (0, i * heads * HD + at), (512, HD)) for i in range(3)], axis=1
    )
    (bundle,) = call(
        pack, [shape((8, 2, HD, HD), BF)], [after(idx, own_w), grad_out[0], saved[0, 0]]
    )
    gs = lax.all_to_all(bundle, "ctx", 0, 0, axis_index_groups=rows_y)
    w1, w3 = x_hop(own_w, 1), x_hop(own_w, -1)
    x2a, x2b = ctx_hop(x1[:64], dz=1), ctx_hop(x3[64:], dz=-1)
    w2a, w2b = x_hop(w1[:256], 1), x_hop(w3[256:], -1)
    xs, own = [x, x1, x3, x2a, x2b], [own_w, w1, w3, w2a, w2b]
    mates = [ctx_hop(after(p, gs) if i in (0, 3, 4) else p, dc=1) for i, p in enumerate(xs)]

    big = 2 * 1024 * 2048 * 384
    xcat, qkv, r, total, own_w = call(
        project,
        [
            shape((1024, 2048), BF),
            shape((1024, 384), BF),
            shape((8, HD, HD), F32),
            shape((HD, HD), BF),
            shape((2048, 384), BF),
        ],
        [idx, *xs, *mates, *own, gs],
        flops=big,
    )
    totals = [ctx_hop(total, dy=s) for s in (1, 2, 3)]
    dq, dk0, dv0, xt = call(
        lambda *refs: within(alpha, beta, *refs),
        [shape((1024, HD), BF), shape((1024, HD), F32), shape((1024, HD), F32), shape((2048, 1024), BF)],
        [idx, xcat, gs, qkv],
        flops=big // 4,
    )
    dqkv, keep, send = call(
        lambda *refs: finish(beta, *refs),
        [shape((1024, 384), BF), shape((NZ, TOK, 384), BF), shape((NZ, TOK, 384), BF)],
        [idx, qkv, dq, dk0, dv0, r, *totals],
        flops=big // 16,
    )
    got = ctx_hop(send, dc=1)
    other_w = ctx_hop(after(own_w, send), dc=1)
    parts = call(
        weights,
        [shape((4, 8, 16, 384), BF)] * 4,
        [idx, xt, dqkv],
        [pltpu.VMEM((NY, 8, NX, 16, 384), BF)],
        flops=big,
    )
    late = after(idx, parts[0])
    parts = [parts[0]] + [plane_hop(parts[s], s, 0) for s in (1, 2, 3)]
    gx, up, down, far_up, far_down = call(
        back,
        [shape((TOK, 2048), F32)] + [shape((TOK, 2048), BF)] * 2 + [shape((64, 2048), BF)] * 2,
        [late, keep, got, own_w, other_w],
        [pltpu.VMEM((NZ, TOK, 2048), F32)],
        flops=big,
    )
    parts = call(turn, [shape((8, 16, 384), BF)] * 4, [after(idx, far_up), *parts])
    parts = [parts[0]] + [plane_hop(parts[s], s, 1) for s in (1, 2, 3)]
    owned = sum(p.astype(F32) for p in parts)
    owned = lax.all_to_all(owned, "ctx", 0, 0, axis_index_groups=rows_y)
    far_up, far_down = ctx_hop(far_up, dz=1), ctx_hop(far_down, dz=-1)
    up, down = call(merge, [shape((TOK, 2048), BF)] * 2, [idx, up, down, far_up, far_down])
    up, down = ctx_hop(up, dz=1), ctx_hop(down, dz=-1)
    (grad_w,) = call(
        lambda *refs: collect(scale, *refs), [shape((16, 3 * heads * HD), F32)], [idx, owned]
    )
    grad_x = (gx + up.astype(F32) + down.astype(F32)).astype(BF)
    return (grad_x[None], grad_w)


def solution(mesh):
    in_specs = (
        P("zero", "ctx", None),
        P("zero", "ctx", None),
        P("zero", "ctx", None, None, None),
        P("zero", None),
    )
    out_specs = (P("zero", "ctx", None), P(("ctx", "zero"), None))
    return jax.shard_map(body, mesh=mesh, in_specs=in_specs, out_specs=out_specs, check_vma=False)
```

```python
import jax
import jax.numpy as jnp
from jax import lax
from jax.experimental import pallas as pl
from jax.experimental.pallas import tpu as pltpu
from jax.sharding import PartitionSpec as P

NY, NZ, NC, NX = 4, 4, 2, 4
TOK, HD = 128, 128
BF, F32 = jnp.bfloat16, jnp.float32


def ctx_index(y, z, c):
    return (y * NZ + z) * NC + c


def ctx_hop(block, dy=0, dz=0, dc=0):
    route = [
        (ctx_index(y, z, c), ctx_index((y + dy) % NY, (z + dz) % NZ, (c + dc) % NC))
        for y in range(NY)
        for z in range(NZ)
        for c in range(NC)
    ]
    return lax.ppermute(block, "ctx", route)


def x_hop(block, dx):
    return lax.ppermute(block, "zero", [(i, (i + dx) % NX) for i in range(NX)])


def plane_hop(block, step, stage):
    route = []
    for y in range(NY):
        for z in range(NZ):
            for c in range(NC):
                for x in range(NX):
                    dx, dy = (step, 0) if c == stage else (0, step)
                    to = ctx_index((y + dy) % NY, z, c) * NX + (x + dx) % NX
                    route.append((ctx_index(y, z, c) * NX + x, to))
    return lax.ppermute(block, ("ctx", "zero"), route)


def dot(a, b):
    return lax.dot_general(a, b, (((1,), (0,)), ((), ())), preferred_element_type=F32)


def dot_nt(a, b):
    return lax.dot_general(a, b, (((1,), (1,)), ((), ())), preferred_element_type=F32)


def dot_tn(a, b):
    return lax.dot_general(a, b, (((0,), (0,)), ((), ())), preferred_element_type=F32)


def call(kernel, outs, ins, scratch=(), flops=0, limit=16, deps=(), free=()):
    count = len(ins)

    def run(*refs):
        kernel(*refs[:count], *refs[count + len(deps) :])

    moved = sum(a.size * a.dtype.itemsize for a in list(ins) + list(outs))
    vmem = pl.BlockSpec(memory_space=pltpu.VMEM)
    return pl.pallas_call(
        run,
        out_shape=list(outs),
        in_specs=[pl.BlockSpec(memory_space=pltpu.SMEM)]
        + [pl.BlockSpec(memory_space=pl.ANY) if i in free else vmem for i in range(1, count)]
        + [pl.BlockSpec(memory_space=pl.ANY)] * len(deps),
        out_specs=[vmem] * len(outs),
        scratch_shapes=list(scratch),
        compiler_params=pltpu.CompilerParams(vmem_limit_bytes=limit << 20),
        cost_estimate=pl.CostEstimate(flops=flops, bytes_accessed=moved, transcendentals=0),
    )(*ins, *deps)


def shape(dims, dtype):
    return jax.ShapeDtypeStruct(dims, dtype)


def after(value, deps):
    return lax.optimization_barrier((value, deps))[0]


def columns(place, step, start=0, size=512):
    block = lax.rem(place + NX - step, NX)
    return pl.ds(pl.multiple_of(block * 512 + start, 256), size)


PIECES = ((0, 0, 512), (1, 0, 512), (3, 0, 512), (2, 0, 256), (2, 256, 256))
TOKENS = ((0, 0, 128), (1, 0, 128), (3, 0, 128), (2, 0, 64), (2, 64, 64))


def pack(idx, cot, state, out):
    for h in range(8):
        out[h, 0] = cot[:, h * HD : (h + 1) * HD]
        out[h, 1] = state[h].astype(BF)


def project(idx, *refs):
    xs, mates, w, gs = refs[0:5], refs[5:10], refs[10:15], refs[15]
    xcat, qkv, r, total, wkeep = refs[16:]
    xi, zi, ci = idx[0], idx[2], idx[3]
    for parity, parts in ((ci, xs), (1 - ci, mates)):
        for part, (s, start, size) in zip(parts, TOKENS, strict=True):
            block = lax.rem(zi + NZ - s, NZ) * 2 + parity
            xcat[pl.ds(pl.multiple_of(block * TOK + start, 64), size), :] = part[...]
    for part, (s, start, size) in zip(w, PIECES, strict=True):
        wkeep[columns(xi, s, start, size), :] = part[...]
    whole = jnp.zeros((HD, HD), F32)
    for m in range(4):
        rows = slice(m * 256, (m + 1) * 256)
        rounded = dot(xcat[rows, :], wkeep[...]).astype(BF)
        qkv[rows, :] = rounded
        for i in range(2):
            piece = dot_tn(rounded[i * TOK : (i + 1) * TOK, :HD], gs[2 * m + i, 0])
            r[2 * m + i] = piece
            whole += piece
    total[...] = whole.astype(BF)


def within(alpha, beta, idx, xcat, gs, qkv, dq, dk0, dv0, xt):
    rowi = lax.broadcasted_iota(jnp.int32, (TOK, TOK), 0)
    coli = lax.broadcasted_iota(jnp.int32, (TOK, TOK), 1)
    mask = rowi >= coli
    for b in range(8):
        rows = slice(b * TOK, (b + 1) * TOK)
        q, k, v = (qkv[rows, i * HD : (i + 1) * HD] for i in range(3))
        g, state = gs[b, 0], gs[b, 1]
        p1 = jnp.where(mask, dot_nt(g, v), 0.0).astype(BF)
        p2 = jnp.where(mask, dot_nt(q, k), 0.0).astype(BF)
        dq[rows, :] = (alpha * dot_nt(g, state) + beta * dot(p1, k)).astype(BF)
        dk0[rows, :] = dot_tn(p1, q)
        dv0[rows, :] = dot_tn(p2, g)
        xt[:, rows] = xcat[rows, :].T


def finish(beta, idx, qkv, dq, dk0, dv0, r, t1, t2, t3, dqkv, keep, send):
    yi, ci = idx[1], idx[3]
    acc = jnp.zeros((HD, HD), F32)
    for step, total in enumerate((t1, t2, t3)):
        use = jnp.where(yi < step + 1, 1.0, 0.0).astype(F32)
        acc += use * total[...].astype(F32)
    for b in range(7, -1, -1):
        rows = slice(b * TOK, (b + 1) * TOK)
        k, v = qkv[rows, HD : 2 * HD], qkv[rows, 2 * HD :]
        later = acc.astype(BF)
        dqkv[rows, :HD] = dq[rows, :]
        dqkv[rows, HD : 2 * HD] = (beta * (dk0[rows, :] + dot_nt(v, later))).astype(BF)
        dqkv[rows, 2 * HD :] = (beta * (dv0[rows, :] + dot(k, later))).astype(BF)
        acc += r[b]
    for z in range(NZ):
        keep[z] = dqkv[pl.ds(pl.multiple_of((2 * z + ci) * TOK, TOK), TOK), :]
        send[z] = dqkv[pl.ds(pl.multiple_of((2 * z + 1 - ci) * TOK, TOK), TOK), :]


def weights(idx, xt, dqkv, *refs):
    outs, buf = refs[:4], refs[4]
    xi, yi, ci = idx[0], idx[1], idx[3]
    for m in range(4):
        tile = dot(xt[m * 512 : (m + 1) * 512, :], dqkv[...]).astype(BF)
        buf[m] = tile.reshape(8, NX, 16, 384)
    for s in range(4):
        for j in range(4):
            y = jnp.where(ci == 0, j, lax.rem(yi + s, NY))
            x = jnp.where(ci == 0, lax.rem(xi + s, NX), j)
            for g in range(8):
                outs[s][j, g] = buf[y, g, x]


def turn(idx, *refs):
    parts, outs = refs[:4], refs[4:]
    place = jnp.where(idx[3] == 0, idx[1], idx[0])
    for s in range(4):
        j = lax.rem(place + s, 4)
        for g in range(8):
            outs[s][g] = sum(p[j, g].astype(F32) for p in parts).astype(BF)


def back(idx, keep, got, own, other, mine_gx, up, down, far_up, far_down, gx):
    zi = idx[2]
    mine = keep[...].reshape(512, 384)
    theirs = got[...].reshape(512, 384)
    for n in range(4):
        cols = slice(n * 512, (n + 1) * 512)
        part = dot_nt(mine, own[cols, :]) + dot_nt(theirs, other[cols, :])
        gx[:, :, cols] = part.reshape(NZ, TOK, 512)
    mine_gx[...] = gx[zi]
    up[...] = gx[lax.rem(zi + 1, NZ)].astype(BF)
    down[...] = gx[lax.rem(zi + 3, NZ)].astype(BF)
    far = lax.rem(zi + 2, NZ)
    far_up[...] = gx[far, :64, :].astype(BF)
    far_down[...] = gx[far, 64:, :].astype(BF)


def merge(idx, up, down, from_low, from_high, new_up, new_down):
    new_up[:64, :] = (up[:64, :].astype(F32) + from_low[...].astype(F32)).astype(BF)
    new_up[64:, :] = up[64:, :]
    new_down[:64, :] = down[:64, :]
    new_down[64:, :] = (down[64:, :].astype(F32) + from_high[...].astype(F32)).astype(BF)


def collect(scale, idx, parts, out):
    for head in range(8):
        for i in range(3):
            at = i * 1024 + head * HD
            out[:, at : at + HD] = parts[head, :, i * HD : (i + 1) * HD] * scale


def body(inputs, grad_out, saved, w_qkv):
    x = inputs[0]
    heads, head_size = saved.shape[2], saved.shape[3]
    length = x.shape[0] * lax.axis_size("ctx")
    alpha = 1.0 / head_size**0.5
    beta = 1.0 / (head_size * length) ** 0.5
    scale = 1.0 / (length * lax.axis_size("zero")) ** 0.5
    ctx = lax.axis_index("ctx")
    xi, yi, zi, ci = lax.axis_index("zero"), ctx // 8, (ctx // 2) % 4, ctx % 2
    idx = jnp.stack([xi, yi, zi, ci]).astype(jnp.int32)
    rows_y = [[ctx_index(y, z, c) for z in range(NZ) for c in range(NC)] for y in range(NY)]

    x1, x3 = ctx_hop(x, dz=1), ctx_hop(x, dz=-1)
    at = (2 * zi + ci) * HD
    own_w = jnp.concatenate(
        [lax.dynamic_slice(w_qkv, (0, i * heads * HD + at), (512, HD)) for i in range(3)], axis=1
    )
    (bundle,) = call(
        pack, [shape((8, 2, HD, HD), BF)], [after(idx, own_w), grad_out[0], saved[0, 0]]
    )
    gs = lax.all_to_all(bundle, "ctx", 0, 0, axis_index_groups=rows_y)
    w1, w3 = x_hop(own_w, 1), x_hop(own_w, -1)
    x2a, x2b = ctx_hop(x1[:64], dz=1), ctx_hop(x3[64:], dz=-1)
    w2a, w2b = x_hop(w1[:256], 1), x_hop(w3[256:], -1)
    xs, own = [x, x1, x3, x2a, x2b], [own_w, w1, w3, w2a, w2b]
    mates = [ctx_hop(after(p, gs) if i in (0, 3, 4) else p, dc=1) for i, p in enumerate(xs)]

    big = 2 * 1024 * 2048 * 384
    xcat, qkv, r, total, own_w = call(
        project,
        [
            shape((1024, 2048), BF),
            shape((1024, 384), BF),
            shape((8, HD, HD), F32),
            shape((HD, HD), BF),
            shape((2048, 384), BF),
        ],
        [idx, *xs, *mates, *own, gs],
        flops=big,
    )
    totals = [ctx_hop(total, dy=s) for s in (1, 2, 3)]
    dq, dk0, dv0, xt = call(
        lambda *refs: within(alpha, beta, *refs),
        [shape((1024, HD), BF), shape((1024, HD), F32), shape((1024, HD), F32), shape((2048, 1024), BF)],
        [idx, xcat, gs, qkv],
        flops=big // 4,
    )
    dqkv, keep, send = call(
        lambda *refs: finish(beta, *refs),
        [shape((1024, 384), BF), shape((NZ, TOK, 384), BF), shape((NZ, TOK, 384), BF)],
        [idx, qkv, dq, dk0, dv0, r, *totals],
        flops=big // 16,
    )
    got = ctx_hop(send, dc=1)
    other_w = ctx_hop(after(own_w, send), dc=1)
    parts = call(
        weights,
        [shape((4, 8, 16, 384), BF)] * 4,
        [idx, xt, dqkv],
        [pltpu.VMEM((NY, 8, NX, 16, 384), BF)],
        flops=big,
    )
    gx, up, down, far_up, far_down = call(
        back,
        [shape((TOK, 2048), F32)] + [shape((TOK, 2048), BF)] * 2 + [shape((64, 2048), BF)] * 2,
        [idx, keep, got, own_w, other_w],
        [pltpu.VMEM((NZ, TOK, 2048), F32)],
        flops=big,
        deps=(parts[0],),
    )
    parts = [parts[0]] + [plane_hop(parts[s], s, 0) for s in (1, 2, 3)]
    far_up, far_down = ctx_hop(far_up, dz=1), ctx_hop(far_down, dz=-1)
    parts = call(turn, [shape((8, 16, 384), BF)] * 4, [idx, *parts], deps=(gx,), limit=4)
    up, down = call(
        merge, [shape((TOK, 2048), BF)] * 2, [idx, up, down, far_up, far_down], deps=(parts[0],), limit=6
    )
    parts = [parts[0]] + [plane_hop(parts[s], s, 1) for s in (1, 2, 3)]
    up, down = ctx_hop(up, dz=1), ctx_hop(down, dz=-1)
    owned = sum(p.astype(F32) for p in parts)
    owned = lax.all_to_all(owned, "ctx", 0, 0, axis_index_groups=rows_y)
    (grad_w,) = call(
        lambda *refs: collect(scale, *refs),
        [shape((16, 3 * heads * HD), F32)],
        [idx, owned],
        limit=4,
    )
    grad_x = (gx + up.astype(F32) + down.astype(F32)).astype(BF)
    return (grad_x[None], grad_w)


def solution(mesh):
    in_specs = (
        P("zero", "ctx", None),
        P("zero", "ctx", None),
        P("zero", "ctx", None, None, None),
        P("zero", None),
    )
    out_specs = (P("zero", "ctx", None), P(("ctx", "zero"), None))
    return jax.shard_map(body, mesh=mesh, in_specs=in_specs, out_specs=out_specs, check_vma=False)
```

```python
import jax
import jax.numpy as jnp
from jax import lax
from jax.experimental import pallas as pl
from jax.experimental.pallas import tpu as pltpu
from jax.sharding import PartitionSpec as P

NY, NZ, NC, NX = 4, 4, 2, 4
TOK, HD = 128, 128
BF, F32 = jnp.bfloat16, jnp.float32


def ctx_index(y, z, c):
    return (y * NZ + z) * NC + c


def ctx_hop(block, dy=0, dz=0, dc=0):
    route = [
        (ctx_index(y, z, c), ctx_index((y + dy) % NY, (z + dz) % NZ, (c + dc) % NC))
        for y in range(NY)
        for z in range(NZ)
        for c in range(NC)
    ]
    return lax.ppermute(block, "ctx", route)


def x_hop(block, dx):
    return lax.ppermute(block, "zero", [(i, (i + dx) % NX) for i in range(NX)])


def plane_hop(block, step, stage):
    route = []
    for y in range(NY):
        for z in range(NZ):
            for c in range(NC):
                for x in range(NX):
                    dx, dy = (step, 0) if c == stage else (0, step)
                    to = ctx_index((y + dy) % NY, z, c) * NX + (x + dx) % NX
                    route.append((ctx_index(y, z, c) * NX + x, to))
    return lax.ppermute(block, ("ctx", "zero"), route)


def dot(a, b):
    return lax.dot_general(a, b, (((1,), (0,)), ((), ())), preferred_element_type=F32)


def dot_nt(a, b):
    return lax.dot_general(a, b, (((1,), (1,)), ((), ())), preferred_element_type=F32)


def dot_tn(a, b):
    return lax.dot_general(a, b, (((0,), (0,)), ((), ())), preferred_element_type=F32)


def call(kernel, outs, ins, scratch=(), flops=0, limit=16, deps=(), free=()):
    count = len(ins)

    def run(*refs):
        kernel(*refs[:count], *refs[count + len(deps) :])

    moved = sum(a.size * a.dtype.itemsize for a in list(ins) + list(outs))
    vmem = pl.BlockSpec(memory_space=pltpu.VMEM)
    return pl.pallas_call(
        run,
        out_shape=list(outs),
        in_specs=[pl.BlockSpec(memory_space=pltpu.SMEM)]
        + [pl.BlockSpec(memory_space=pl.ANY) if i in free else vmem for i in range(1, count)]
        + [pl.BlockSpec(memory_space=pl.ANY)] * len(deps),
        out_specs=[vmem] * len(outs),
        scratch_shapes=list(scratch),
        compiler_params=pltpu.CompilerParams(vmem_limit_bytes=limit << 20),
        cost_estimate=pl.CostEstimate(flops=flops, bytes_accessed=moved, transcendentals=0),
    )(*ins, *deps)


def shape(dims, dtype):
    return jax.ShapeDtypeStruct(dims, dtype)


def after(value, deps):
    return lax.optimization_barrier((value, deps))[0]


def columns(place, step, start=0, size=512):
    block = lax.rem(place + NX - step, NX)
    return pl.ds(pl.multiple_of(block * 512 + start, 256), size)


PIECES = ((0, 0, 512), (1, 0, 512), (3, 0, 512), (2, 0, 256), (2, 256, 256))
TOKENS = ((0, 0, 128), (1, 0, 128), (3, 0, 128), (2, 0, 64), (2, 64, 64))


def pack(idx, cot, state, out):
    for h in range(8):
        out[h, 0] = cot[:, h * HD : (h + 1) * HD]
        out[h, 1] = state[h].astype(BF)


def relay(idx, w1, w3, low, high):
    low[...] = w1[:256, :]
    high[...] = w3[256:, :]


def project(idx, *refs):
    xs, mates, w, gs = refs[0:5], refs[5:10], refs[10:15], refs[15]
    xcat, qkv, r, total, wkeep = refs[16:]
    xi, zi, ci = idx[0], idx[2], idx[3]
    for parity, parts in ((ci, xs), (1 - ci, mates)):
        for part, (s, start, size) in zip(parts, TOKENS, strict=True):
            block = lax.rem(zi + NZ - s, NZ) * 2 + parity
            xcat[pl.ds(pl.multiple_of(block * TOK + start, 64), size), :] = part[...]
    for part, (s, start, size) in zip(w, PIECES, strict=True):
        wkeep[columns(xi, s, start, size), :] = part[...]
    whole = jnp.zeros((HD, HD), F32)
    for m in range(4):
        rows = slice(m * 256, (m + 1) * 256)
        rounded = dot(xcat[rows, :], wkeep[...]).astype(BF)
        qkv[rows, :] = rounded
        for i in range(2):
            piece = dot_tn(rounded[i * TOK : (i + 1) * TOK, :HD], gs[2 * m + i, 0])
            r[2 * m + i] = piece
            whole += piece
    total[...] = whole.astype(BF)


def within(alpha, beta, idx, xcat, gs, qkv, dq, dk0, dv0, xt):
    rowi = lax.broadcasted_iota(jnp.int32, (TOK, TOK), 0)
    coli = lax.broadcasted_iota(jnp.int32, (TOK, TOK), 1)
    mask = rowi >= coli
    for b in range(8):
        rows = slice(b * TOK, (b + 1) * TOK)
        q, k, v = (qkv[rows, i * HD : (i + 1) * HD] for i in range(3))
        g, state = gs[b, 0], gs[b, 1]
        p1 = jnp.where(mask, dot_nt(g, v), 0.0).astype(BF)
        p2 = jnp.where(mask, dot_nt(q, k), 0.0).astype(BF)
        dq[rows, :] = (alpha * dot_nt(g, state) + beta * dot(p1, k)).astype(BF)
        dk0[rows, :] = dot_tn(p1, q)
        dv0[rows, :] = dot_tn(p2, g)
        xt[:, rows] = xcat[rows, :].T


def finish(beta, idx, qkv, dq, dk0, dv0, r, t1, t2, t3, dqkv, keep, send):
    yi, ci = idx[1], idx[3]
    acc = jnp.zeros((HD, HD), F32)
    for step, total in enumerate((t1, t2, t3)):
        use = jnp.where(yi < step + 1, 1.0, 0.0).astype(F32)
        acc += use * total[...].astype(F32)
    for b in range(7, -1, -1):
        rows = slice(b * TOK, (b + 1) * TOK)
        k, v = qkv[rows, HD : 2 * HD], qkv[rows, 2 * HD :]
        later = acc.astype(BF)
        dqkv[rows, :HD] = dq[rows, :]
        dqkv[rows, HD : 2 * HD] = (beta * (dk0[rows, :] + dot_nt(v, later))).astype(BF)
        dqkv[rows, 2 * HD :] = (beta * (dv0[rows, :] + dot(k, later))).astype(BF)
        acc += r[b]
    for z in range(NZ):
        keep[z] = dqkv[pl.ds(pl.multiple_of((2 * z + ci) * TOK, TOK), TOK), :]
        send[z] = dqkv[pl.ds(pl.multiple_of((2 * z + 1 - ci) * TOK, TOK), TOK), :]


def weights(idx, xt, dqkv, *refs):
    outs, buf = refs[:4], refs[4]
    xi, yi, ci = idx[0], idx[1], idx[3]
    for m in range(4):
        tile = dot(xt[m * 512 : (m + 1) * 512, :], dqkv[...]).astype(BF)
        buf[m] = tile.reshape(8, NX, 16, 384)
    for s in range(4):
        for j in range(4):
            y = jnp.where(ci == 0, j, lax.rem(yi + s, NY))
            x = jnp.where(ci == 0, lax.rem(xi + s, NX), j)
            for g in range(8):
                outs[s][j, g] = buf[y, g, x]


def turn(idx, *refs):
    parts, outs = refs[:4], refs[4:]
    place = jnp.where(idx[3] == 0, idx[1], idx[0])
    for s in range(4):
        j = lax.rem(place + s, 4)
        for g in range(8):
            outs[s][g] = sum(p[j, g].astype(F32) for p in parts).astype(BF)


def back(idx, keep, got, own, other, mine_gx, up, down, far_up, far_down, gx):
    zi = idx[2]
    mine = keep[...].reshape(512, 384)
    theirs = got[...].reshape(512, 384)
    for n in range(4):
        cols = slice(n * 512, (n + 1) * 512)
        part = dot_nt(mine, own[cols, :]) + dot_nt(theirs, other[cols, :])
        gx[:, :, cols] = part.reshape(NZ, TOK, 512)
    mine_gx[...] = gx[zi]
    up[...] = gx[lax.rem(zi + 1, NZ)].astype(BF)
    down[...] = gx[lax.rem(zi + 3, NZ)].astype(BF)
    far = lax.rem(zi + 2, NZ)
    far_up[...] = gx[far, :64, :].astype(BF)
    far_down[...] = gx[far, 64:, :].astype(BF)


def merge(idx, up, down, from_low, from_high, new_up, new_down):
    new_up[:64, :] = (up[:64, :].astype(F32) + from_low[...].astype(F32)).astype(BF)
    new_up[64:, :] = up[64:, :]
    new_down[:64, :] = down[:64, :]
    new_down[64:, :] = (down[64:, :].astype(F32) + from_high[...].astype(F32)).astype(BF)


def collect(scale, idx, parts, out):
    for head in range(8):
        for i in range(3):
            at = i * 1024 + head * HD
            out[:, at : at + HD] = parts[head, :, i * HD : (i + 1) * HD] * scale


def body(inputs, grad_out, saved, w_qkv):
    x = inputs[0]
    heads, head_size = saved.shape[2], saved.shape[3]
    length = x.shape[0] * lax.axis_size("ctx")
    alpha = 1.0 / head_size**0.5
    beta = 1.0 / (head_size * length) ** 0.5
    scale = 1.0 / (length * lax.axis_size("zero")) ** 0.5
    ctx = lax.axis_index("ctx")
    xi, yi, zi, ci = lax.axis_index("zero"), ctx // 8, (ctx // 2) % 4, ctx % 2
    idx = jnp.stack([xi, yi, zi, ci]).astype(jnp.int32)
    rows_y = [[ctx_index(y, z, c) for z in range(NZ) for c in range(NC)] for y in range(NY)]

    x1, x3 = ctx_hop(x, dz=1), ctx_hop(x, dz=-1)
    at = (2 * zi + ci) * HD
    own_w = jnp.concatenate(
        [lax.dynamic_slice(w_qkv, (0, i * heads * HD + at), (512, HD)) for i in range(3)], axis=1
    )
    (bundle,) = call(
        pack, [shape((8, 2, HD, HD), BF)], [after(idx, own_w), grad_out[0], saved[0, 0]]
    )
    gs = lax.all_to_all(bundle, "ctx", 0, 0, axis_index_groups=rows_y)
    w1, w3 = x_hop(own_w, 1), x_hop(own_w, -1)
    x2a, x2b = ctx_hop(x1[:64], dz=1), ctx_hop(x3[64:], dz=-1)
    low, high = call(relay, [shape((256, 384), BF)] * 2, [idx, w1, w3], flops=1 << 34, limit=4)
    w2a, w2b = x_hop(low, 1), x_hop(high, -1)
    xs, own = [x, x1, x3, x2a, x2b], [own_w, w1, w3, w2a, w2b]
    mates = [ctx_hop(after(p, gs if i else x1) if i > 2 or i == 0 else p, dc=1) for i, p in enumerate(xs)]

    big = 2 * 1024 * 2048 * 384
    xcat, qkv, r, total, own_w = call(
        project,
        [
            shape((1024, 2048), BF),
            shape((1024, 384), BF),
            shape((8, HD, HD), F32),
            shape((HD, HD), BF),
            shape((2048, 384), BF),
        ],
        [idx, *xs, *mates, *own, gs],
        flops=big,
    )
    totals = [ctx_hop(total, dy=s) for s in (1, 2, 3)]
    dq, dk0, dv0, xt = call(
        lambda *refs: within(alpha, beta, *refs),
        [shape((1024, HD), BF), shape((1024, HD), F32), shape((1024, HD), F32), shape((2048, 1024), BF)],
        [idx, xcat, gs, qkv],
        flops=big // 4,
    )
    dqkv, keep, send = call(
        lambda *refs: finish(beta, *refs),
        [shape((1024, 384), BF), shape((NZ, TOK, 384), BF), shape((NZ, TOK, 384), BF)],
        [idx, qkv, dq, dk0, dv0, r, *totals],
        flops=big // 16,
    )
    got = ctx_hop(send, dc=1)
    other_w = ctx_hop(after(own_w, send), dc=1)
    parts = call(
        weights,
        [shape((4, 8, 16, 384), BF)] * 4,
        [idx, xt, dqkv],
        [pltpu.VMEM((NY, 8, NX, 16, 384), BF)],
        flops=big,
    )
    gx, up, down, far_up, far_down = call(
        back,
        [shape((TOK, 2048), F32)] + [shape((TOK, 2048), BF)] * 2 + [shape((64, 2048), BF)] * 2,
        [idx, keep, got, own_w, other_w],
        [pltpu.VMEM((NZ, TOK, 2048), F32)],
        flops=big,
        deps=(parts[0],),
    )
    parts = [parts[0]] + [plane_hop(parts[s], s, 0) for s in (1, 2, 3)]
    far_up, far_down = ctx_hop(far_up, dz=1), ctx_hop(far_down, dz=-1)
    parts = call(turn, [shape((8, 16, 384), BF)] * 4, [idx, *parts], deps=(gx,), limit=4)
    up, down = call(
        merge, [shape((TOK, 2048), BF)] * 2, [idx, up, down, far_up, far_down], flops=1 << 33, deps=(parts[0],), limit=6
    )
    parts = [parts[0]] + [plane_hop(parts[s], s, 1) for s in (1, 2, 3)]
    up, down = ctx_hop(up, dz=1), ctx_hop(down, dz=-1)
    owned = sum(p.astype(F32) for p in parts)
    owned = lax.all_to_all(owned, "ctx", 0, 0, axis_index_groups=rows_y)
    (grad_w,) = call(
        lambda *refs: collect(scale, *refs),
        [shape((16, 3 * heads * HD), F32)],
        [idx, owned],
        flops=1 << 31,
        limit=4,
    )
    grad_x = (gx + up.astype(F32) + down.astype(F32)).astype(BF)
    return (grad_x[None], grad_w)


def solution(mesh):
    in_specs = (
        P("zero", "ctx", None),
        P("zero", "ctx", None),
        P("zero", "ctx", None, None, None),
        P("zero", None),
    )
    out_specs = (P("zero", "ctx", None), P(("ctx", "zero"), None))
    return jax.shard_map(body, mesh=mesh, in_specs=in_specs, out_specs=out_specs, check_vma=False)
```

```python
import jax
import jax.numpy as jnp
from jax import lax
from jax.experimental import pallas as pl
from jax.experimental.pallas import tpu as pltpu
from jax.sharding import PartitionSpec as P

NY, NZ, NC, NX = 4, 4, 2, 4
TOK, HD = 128, 128
BF, F32 = jnp.bfloat16, jnp.float32


def ctx_index(y, z, c):
    return (y * NZ + z) * NC + c


def ctx_hop(block, dy=0, dz=0, dc=0):
    route = [
        (ctx_index(y, z, c), ctx_index((y + dy) % NY, (z + dz) % NZ, (c + dc) % NC))
        for y in range(NY)
        for z in range(NZ)
        for c in range(NC)
    ]
    return lax.ppermute(block, "ctx", route)


def x_hop(block, dx):
    return lax.ppermute(block, "zero", [(i, (i + dx) % NX) for i in range(NX)])


def plane_hop(block, step, stage):
    route = []
    for y in range(NY):
        for z in range(NZ):
            for c in range(NC):
                for x in range(NX):
                    dx, dy = (step, 0) if c == stage else (0, step)
                    to = ctx_index((y + dy) % NY, z, c) * NX + (x + dx) % NX
                    route.append((ctx_index(y, z, c) * NX + x, to))
    return lax.ppermute(block, ("ctx", "zero"), route)


def dot(a, b):
    return lax.dot_general(a, b, (((1,), (0,)), ((), ())), preferred_element_type=F32)


def dot_nt(a, b):
    return lax.dot_general(a, b, (((1,), (1,)), ((), ())), preferred_element_type=F32)


def dot_tn(a, b):
    return lax.dot_general(a, b, (((0,), (0,)), ((), ())), preferred_element_type=F32)


def call(kernel, outs, ins, scratch=(), flops=0, limit=16, deps=(), free=()):
    count = len(ins)

    def run(*refs):
        kernel(*refs[:count], *refs[count + len(deps) :])

    moved = sum(a.size * a.dtype.itemsize for a in list(ins) + list(outs))
    vmem = pl.BlockSpec(memory_space=pltpu.VMEM)
    return pl.pallas_call(
        run,
        out_shape=list(outs),
        in_specs=[pl.BlockSpec(memory_space=pltpu.SMEM)]
        + [pl.BlockSpec(memory_space=pl.ANY) if i in free else vmem for i in range(1, count)]
        + [pl.BlockSpec(memory_space=pl.ANY)] * len(deps),
        out_specs=[vmem] * len(outs),
        scratch_shapes=list(scratch),
        compiler_params=pltpu.CompilerParams(vmem_limit_bytes=limit << 20),
        cost_estimate=pl.CostEstimate(flops=flops, bytes_accessed=moved, transcendentals=0),
    )(*ins, *deps)


def shape(dims, dtype):
    return jax.ShapeDtypeStruct(dims, dtype)


def after(value, deps):
    return lax.optimization_barrier((value, deps))[0]


def columns(place, step, start=0, size=512):
    block = lax.rem(place + NX - step, NX)
    return pl.ds(pl.multiple_of(block * 512 + start, 256), size)


NEAR = (0, 1, 3)


def block_at(idx, place):
    slot = NEAR[place % 3] if place < 6 else 2
    mate = place in (3, 4, 5, 7)
    core = 1 - idx[3] if mate else idx[3]
    return lax.rem(idx[2] + NZ - slot, NZ) * 2 + core


def rows_of(idx, z, mate):
    slot = lax.rem(idx[2] + NZ - z, NZ)
    near = jnp.where(slot == 3, 2, slot) + 3 * mate
    return pl.ds(pl.multiple_of(jnp.where(slot == 2, 6 + mate, near) * TOK, TOK), TOK)


def pack(idx, cot, state, out):
    for h in range(8):
        out[h, 0] = cot[:, h * HD : (h + 1) * HD]
        out[h, 1] = state[h].astype(BF)


def relay(idx, w0, w1, w3, w2, wkeep):
    for part, step in ((w0, 0), (w1, 1), (w3, 3), (w2, 2)):
        wkeep[columns(idx[0], step, 0, 512), :] = part[...]


def stack(idx, *refs):
    parts, xa, xta = refs[:6], refs[6], refs[7]
    for i, part in enumerate(parts):
        xa[i * TOK : (i + 1) * TOK, :] = part[...]
        xta[:, i * TOK : (i + 1) * TOK] = part[...].T


def project(idx, xa, x2a, x2b, m2a, m2b, wkeep, gs, qkv, r, total, xtb, xb):
    for i, part in enumerate((x2a, x2b, m2a, m2b)):
        xb[i * 64 : (i + 1) * 64, :] = part[...]
    whole = jnp.zeros((HD, HD), F32)
    for m in range(4):
        rows = slice(m * 256, (m + 1) * 256)
        tokens = xa[rows, :] if m < 3 else xb[...]
        rounded = dot(tokens, wkeep[...]).astype(BF)
        qkv[rows, :] = rounded
        for i in range(2):
            block = block_at(idx, 2 * m + i)
            piece = dot_tn(rounded[i * TOK : (i + 1) * TOK, :HD], gs[block, 0])
            r[block] = piece
            whole += piece
    total[...] = whole.astype(BF)
    for i in range(2):
        xtb[:, i * TOK : (i + 1) * TOK] = xb[i * TOK : (i + 1) * TOK, :].T


def within(alpha, beta, idx, gs, qkv, dq, dk0, dv0):
    rowi = lax.broadcasted_iota(jnp.int32, (TOK, TOK), 0)
    coli = lax.broadcasted_iota(jnp.int32, (TOK, TOK), 1)
    mask = rowi >= coli
    for place in range(8):
        rows = slice(place * TOK, (place + 1) * TOK)
        q, k, v = (qkv[rows, i * HD : (i + 1) * HD] for i in range(3))
        block = block_at(idx, place)
        g, state = gs[block, 0], gs[block, 1]
        p1 = jnp.where(mask, dot_nt(g, v), 0.0).astype(BF)
        p2 = jnp.where(mask, dot_nt(q, k), 0.0).astype(BF)
        dq[rows, :] = (alpha * dot_nt(g, state) + beta * dot(p1, k)).astype(BF)
        dk0[rows, :] = dot_tn(p1, q)
        dv0[rows, :] = dot_tn(p2, g)


def finish(beta, idx, qkv, dq, dk0, dv0, r, t1, t2, t3, dqkv, keep, send):
    yi, ci = idx[1], idx[3]
    acc = jnp.zeros((HD, HD), F32)
    for step, total in enumerate((t1, t2, t3)):
        use = jnp.where(yi < step + 1, 1.0, 0.0).astype(F32)
        acc += use * total[...].astype(F32)
    for b in range(7, -1, -1):
        rows = rows_of(idx, b // 2, jnp.where(ci == b % 2, 0, 1))
        k, v = qkv[rows, HD : 2 * HD], qkv[rows, 2 * HD :]
        later = acc.astype(BF)
        dqkv[rows, :HD] = dq[rows, :]
        dqkv[rows, HD : 2 * HD] = (beta * (dk0[rows, :] + dot_nt(v, later))).astype(BF)
        dqkv[rows, 2 * HD :] = (beta * (dv0[rows, :] + dot(k, later))).astype(BF)
        acc += r[b]
    for z in range(NZ):
        keep[z] = dqkv[rows_of(idx, z, 0), :]
        send[z] = dqkv[rows_of(idx, z, 1), :]


def weights(idx, xta, xtb, dqkv, *refs):
    outs, buf = refs[:4], refs[4]
    xi, yi, ci = idx[0], idx[1], idx[3]
    for m in range(4):
        rows = slice(m * 512, (m + 1) * 512)
        tile = (dot(xta[rows, :], dqkv[:768, :]) + dot(xtb[rows, :], dqkv[768:, :])).astype(BF)
        buf[m] = tile.reshape(8, NX, 16, 384)
    for s in range(4):
        for j in range(4):
            y = jnp.where(ci == 0, j, lax.rem(yi + s, NY))
            x = jnp.where(ci == 0, lax.rem(xi + s, NX), j)
            for g in range(8):
                outs[s][j, g] = buf[y, g, x]


def turn(idx, *refs):
    parts, outs = refs[:4], refs[4:]
    place = jnp.where(idx[3] == 0, idx[1], idx[0])
    for s in range(4):
        j = lax.rem(place + s, 4)
        for g in range(8):
            outs[s][g] = sum(p[j, g].astype(F32) for p in parts).astype(BF)


def back(idx, keep, got, own, other, mine_gx, up, down, far_up, far_down, gx):
    zi = idx[2]
    mine = keep[...].reshape(512, 384)
    theirs = got[...].reshape(512, 384)
    for n in range(4):
        cols = slice(n * 512, (n + 1) * 512)
        part = dot_nt(mine, own[cols, :]) + dot_nt(theirs, other[cols, :])
        gx[:, :, cols] = part.reshape(NZ, TOK, 512)
    mine_gx[...] = gx[zi]
    up[...] = gx[lax.rem(zi + 1, NZ)].astype(BF)
    down[...] = gx[lax.rem(zi + 3, NZ)].astype(BF)
    far = lax.rem(zi + 2, NZ)
    far_up[...] = gx[far, :64, :].astype(BF)
    far_down[...] = gx[far, 64:, :].astype(BF)


def merge(idx, up, down, from_low, from_high, new_up, new_down):
    new_up[:64, :] = (up[:64, :].astype(F32) + from_low[...].astype(F32)).astype(BF)
    new_up[64:, :] = up[64:, :]
    new_down[:64, :] = down[:64, :]
    new_down[64:, :] = (down[64:, :].astype(F32) + from_high[...].astype(F32)).astype(BF)


def collect(scale, idx, parts, out):
    for head in range(8):
        for i in range(3):
            at = i * 1024 + head * HD
            out[:, at : at + HD] = parts[head, :, i * HD : (i + 1) * HD] * scale


def body(inputs, grad_out, saved, w_qkv):
    x = inputs[0]
    heads, head_size = saved.shape[2], saved.shape[3]
    length = x.shape[0] * lax.axis_size("ctx")
    alpha = 1.0 / head_size**0.5
    beta = 1.0 / (head_size * length) ** 0.5
    scale = 1.0 / (length * lax.axis_size("zero")) ** 0.5
    ctx = lax.axis_index("ctx")
    xi, yi, zi, ci = lax.axis_index("zero"), ctx // 8, (ctx // 2) % 4, ctx % 2
    idx = jnp.stack([xi, yi, zi, ci]).astype(jnp.int32)
    rows_y = [[ctx_index(y, z, c) for z in range(NZ) for c in range(NC)] for y in range(NY)]

    x1, x3 = ctx_hop(x, dz=1), ctx_hop(x, dz=-1)
    at = (2 * zi + ci) * HD
    own_w = jnp.concatenate(
        [lax.dynamic_slice(w_qkv, (0, i * heads * HD + at), (512, HD)) for i in range(3)], axis=1
    )
    (bundle,) = call(
        pack, [shape((8, 2, HD, HD), BF)], [after(idx, own_w), grad_out[0], saved[0, 0]]
    )
    gs = lax.all_to_all(bundle, "ctx", 0, 0, axis_index_groups=rows_y)
    w2, w1, w3 = (x_hop(own_w, s) for s in (2, 1, -1))
    x2a, x2b = ctx_hop(x1[:64], dz=1), ctx_hop(x3[64:], dz=-1)
    (own_w,) = call(relay, [shape((2048, 384), BF)], [idx, own_w, w1, w3, w2], flops=1 << 33, limit=6)
    first = [x, x1, x3]
    first += [ctx_hop(p, dc=1) for p in first]
    xa, xta = call(
        stack, [shape((768, 2048), BF), shape((2048, 768), BF)], [idx, *first], flops=1 << 33, limit=10
    )
    last = [x2a, x2b]
    last += [ctx_hop(after(p, gs), dc=1) for p in last]

    big = 2 * 1024 * 2048 * 384
    qkv, r, total, xtb = call(
        project,
        [
            shape((1024, 384), BF),
            shape((8, HD, HD), F32),
            shape((HD, HD), BF),
            shape((2048, 256), BF),
        ],
        [idx, xa, *last, own_w, gs],
        [pltpu.VMEM((256, 2048), BF)],
        flops=big,
    )
    totals = [ctx_hop(total, dy=s) for s in (1, 2, 3)]
    dq, dk0, dv0 = call(
        lambda *refs: within(alpha, beta, *refs),
        [shape((1024, HD), BF), shape((1024, HD), F32), shape((1024, HD), F32)],
        [idx, gs, qkv],
        flops=big // 4,
    )
    dqkv, keep, send = call(
        lambda *refs: finish(beta, *refs),
        [shape((1024, 384), BF), shape((NZ, TOK, 384), BF), shape((NZ, TOK, 384), BF)],
        [idx, qkv, dq, dk0, dv0, r, *totals],
        flops=big // 16,
    )
    got = ctx_hop(send, dc=1)
    other_w = ctx_hop(after(own_w, send), dc=1)
    parts = call(
        weights,
        [shape((4, 8, 16, 384), BF)] * 4,
        [idx, xta, xtb, dqkv],
        [pltpu.VMEM((NY, 8, NX, 16, 384), BF)],
        flops=big,
    )
    gx, up, down, far_up, far_down = call(
        back,
        [shape((TOK, 2048), F32)] + [shape((TOK, 2048), BF)] * 2 + [shape((64, 2048), BF)] * 2,
        [idx, keep, got, own_w, other_w],
        [pltpu.VMEM((NZ, TOK, 2048), F32)],
        flops=big,
        deps=(parts[0],),
    )
    parts = [parts[0]] + [plane_hop(parts[s], s, 0) for s in (1, 2, 3)]
    far_up, far_down = ctx_hop(far_up, dz=1), ctx_hop(far_down, dz=-1)
    parts = call(turn, [shape((8, 16, 384), BF)] * 4, [idx, *parts], deps=(gx,), limit=4)
    up, down = call(
        merge, [shape((TOK, 2048), BF)] * 2, [idx, up, down, far_up, far_down], flops=1 << 33, deps=(parts[0],), limit=6
    )
    parts = [parts[0]] + [plane_hop(parts[s], s, 1) for s in (1, 2, 3)]
    up, down = ctx_hop(up, dz=1), ctx_hop(down, dz=-1)
    owned = sum(p.astype(F32) for p in parts)
    owned = lax.all_to_all(owned, "ctx", 0, 0, axis_index_groups=rows_y)
    (grad_w,) = call(
        lambda *refs: collect(scale, *refs),
        [shape((16, 3 * heads * HD), F32)],
        [idx, owned],
        flops=1 << 31,
        limit=4,
    )
    grad_x = (gx + up.astype(F32) + down.astype(F32)).astype(BF)
    return (grad_x[None], grad_w)


def solution(mesh):
    in_specs = (
        P("zero", "ctx", None),
        P("zero", "ctx", None),
        P("zero", "ctx", None, None, None),
        P("zero", None),
    )
    out_specs = (P("zero", "ctx", None), P(("ctx", "zero"), None))
    return jax.shard_map(body, mesh=mesh, in_specs=in_specs, out_specs=out_specs, check_vma=False)
```

```python
import jax
import jax.numpy as jnp
from jax import lax
from jax.experimental import pallas as pl
from jax.experimental.pallas import tpu as pltpu
from jax.sharding import PartitionSpec as P

NY, NZ, NC, NX = 4, 4, 2, 4
TOK, HD = 128, 128
BF, F32 = jnp.bfloat16, jnp.float32


def ctx_index(y, z, c):
    return (y * NZ + z) * NC + c


def ctx_hop(block, dy=0, dz=0, dc=0):
    route = [
        (ctx_index(y, z, c), ctx_index((y + dy) % NY, (z + dz) % NZ, (c + dc) % NC))
        for y in range(NY)
        for z in range(NZ)
        for c in range(NC)
    ]
    return lax.ppermute(block, "ctx", route)


def x_hop(block, dx):
    return lax.ppermute(block, "zero", [(i, (i + dx) % NX) for i in range(NX)])


def plane_hop(block, step, stage):
    route = []
    for y in range(NY):
        for z in range(NZ):
            for c in range(NC):
                for x in range(NX):
                    dx, dy = (step, 0) if c == stage else (0, step)
                    to = ctx_index((y + dy) % NY, z, c) * NX + (x + dx) % NX
                    route.append((ctx_index(y, z, c) * NX + x, to))
    return lax.ppermute(block, ("ctx", "zero"), route)


def dot(a, b):
    return lax.dot_general(a, b, (((1,), (0,)), ((), ())), preferred_element_type=F32)


def dot_nt(a, b):
    return lax.dot_general(a, b, (((1,), (1,)), ((), ())), preferred_element_type=F32)


def dot_tn(a, b):
    return lax.dot_general(a, b, (((0,), (0,)), ((), ())), preferred_element_type=F32)


def call(kernel, outs, ins, scratch=(), flops=0, limit=16, deps=(), free=()):
    count = len(ins)

    def run(*refs):
        kernel(*refs[:count], *refs[count + len(deps) :])

    moved = sum(a.size * a.dtype.itemsize for a in list(ins) + list(outs))
    vmem = pl.BlockSpec(memory_space=pltpu.VMEM)
    return pl.pallas_call(
        run,
        out_shape=list(outs),
        in_specs=[pl.BlockSpec(memory_space=pltpu.SMEM)]
        + [pl.BlockSpec(memory_space=pl.ANY) if i in free else vmem for i in range(1, count)]
        + [pl.BlockSpec(memory_space=pl.ANY)] * len(deps),
        out_specs=[vmem] * len(outs),
        scratch_shapes=list(scratch),
        compiler_params=pltpu.CompilerParams(vmem_limit_bytes=limit << 20),
        cost_estimate=pl.CostEstimate(flops=flops, bytes_accessed=moved, transcendentals=0),
    )(*ins, *deps)


def shape(dims, dtype):
    return jax.ShapeDtypeStruct(dims, dtype)


def after(value, deps):
    return lax.optimization_barrier((value, deps))[0]


def columns(place, step, start=0, size=512):
    block = lax.rem(place + NX - step, NX)
    return pl.ds(pl.multiple_of(block * 512 + start, 256), size)


NEAR = (0, 1, 3)


def block_at(idx, place):
    slot = NEAR[place % 3] if place < 6 else 2
    mate = place in (3, 4, 5, 7)
    core = 1 - idx[3] if mate else idx[3]
    return lax.rem(idx[2] + NZ - slot, NZ) * 2 + core


def rows_of(idx, z, mate):
    slot = lax.rem(idx[2] + NZ - z, NZ)
    near = jnp.where(slot == 3, 2, slot) + 3 * mate
    return pl.ds(pl.multiple_of(jnp.where(slot == 2, 6 + mate, near) * TOK, TOK), TOK)


def pack(idx, cot, state, out):
    for h in range(8):
        out[h, 0] = cot[:, h * HD : (h + 1) * HD]
        out[h, 1] = state[h].astype(BF)


def relay(idx, w0, w1, w3, w2, wkeep):
    for part, step in ((w0, 0), (w1, 1), (w3, 3), (w2, 2)):
        wkeep[columns(idx[0], step, 0, 512), :] = part[...]


def stack(idx, *refs):
    parts, xa = refs[:6], refs[6]
    for i, part in enumerate(parts):
        xa[i * TOK : (i + 1) * TOK, :] = part[...]


def project(idx, xa, x2a, x2b, m2a, m2b, wkeep, gs, qkv, r, total, xb):
    for i, part in enumerate((x2a, x2b, m2a, m2b)):
        xb[i * 64 : (i + 1) * 64, :] = part[...]
    whole = jnp.zeros((HD, HD), F32)
    for m in range(4):
        rows = slice(m * 256, (m + 1) * 256)
        tokens = xa[rows, :] if m < 3 else xb[...]
        rounded = dot(tokens, wkeep[...]).astype(BF)
        qkv[rows, :] = rounded
        for i in range(2):
            block = block_at(idx, 2 * m + i)
            piece = dot_tn(rounded[i * TOK : (i + 1) * TOK, :HD], gs[block, 0])
            r[block] = piece
            whole += piece
    total[...] = whole.astype(BF)


def within(alpha, beta, idx, xa, xb, gs, qkv, dq, dk0, dv0, xt):
    rowi = lax.broadcasted_iota(jnp.int32, (TOK, TOK), 0)
    coli = lax.broadcasted_iota(jnp.int32, (TOK, TOK), 1)
    mask = rowi >= coli
    for place in range(8):
        rows = slice(place * TOK, (place + 1) * TOK)
        q, k, v = (qkv[rows, i * HD : (i + 1) * HD] for i in range(3))
        block = block_at(idx, place)
        g, state = gs[block, 0], gs[block, 1]
        p1 = jnp.where(mask, dot_nt(g, v), 0.0).astype(BF)
        p2 = jnp.where(mask, dot_nt(q, k), 0.0).astype(BF)
        dq[rows, :] = (alpha * dot_nt(g, state) + beta * dot(p1, k)).astype(BF)
        dk0[rows, :] = dot_tn(p1, q)
        dv0[rows, :] = dot_tn(p2, g)
        xt[:, rows] = xa[rows, :].T if place < 6 else xb[place * TOK - 768 : place * TOK - 640, :].T


def finish(beta, idx, qkv, dq, dk0, dv0, r, t1, t2, t3, dqkv, keep, send):
    yi, ci = idx[1], idx[3]
    acc = jnp.zeros((HD, HD), F32)
    for step, total in enumerate((t1, t2, t3)):
        use = jnp.where(yi < step + 1, 1.0, 0.0).astype(F32)
        acc += use * total[...].astype(F32)
    for b in range(7, -1, -1):
        rows = rows_of(idx, b // 2, jnp.where(ci == b % 2, 0, 1))
        k, v = qkv[rows, HD : 2 * HD], qkv[rows, 2 * HD :]
        later = acc.astype(BF)
        dqkv[rows, :HD] = dq[rows, :]
        dqkv[rows, HD : 2 * HD] = (beta * (dk0[rows, :] + dot_nt(v, later))).astype(BF)
        dqkv[rows, 2 * HD :] = (beta * (dv0[rows, :] + dot(k, later))).astype(BF)
        acc += r[b]
    for z in range(NZ):
        keep[z] = dqkv[rows_of(idx, z, 0), :]
        send[z] = dqkv[rows_of(idx, z, 1), :]


def weights(idx, xt, dqkv, *refs):
    outs, buf = refs[:4], refs[4]
    xi, yi, ci = idx[0], idx[1], idx[3]
    for m in range(4):
        rows = slice(m * 512, (m + 1) * 512)
        tile = dot(xt[rows, :], dqkv[...]).astype(BF)
        buf[m] = tile.reshape(8, NX, 16, 384)
    for s in range(4):
        for j in range(4):
            y = jnp.where(ci == 0, j, lax.rem(yi + s, NY))
            x = jnp.where(ci == 0, lax.rem(xi + s, NX), j)
            for g in range(8):
                outs[s][j, g] = buf[y, g, x]


def turn(idx, *refs):
    parts, outs = refs[:4], refs[4:]
    place = jnp.where(idx[3] == 0, idx[1], idx[0])
    for s in range(4):
        j = lax.rem(place + s, 4)
        for g in range(8):
            outs[s][g] = sum(p[j, g].astype(F32) for p in parts).astype(BF)


def back(idx, keep, got, own, other, mine_gx, up, down, far_up, far_down, gx):
    zi = idx[2]
    mine = keep[...].reshape(512, 384)
    theirs = got[...].reshape(512, 384)
    for n in range(4):
        cols = slice(n * 512, (n + 1) * 512)
        part = dot_nt(mine, own[cols, :]) + dot_nt(theirs, other[cols, :])
        gx[:, :, cols] = part.reshape(NZ, TOK, 512)
    mine_gx[...] = gx[zi]
    up[...] = gx[lax.rem(zi + 1, NZ)].astype(BF)
    down[...] = gx[lax.rem(zi + 3, NZ)].astype(BF)
    far = lax.rem(zi + 2, NZ)
    far_up[...] = gx[far, :64, :].astype(BF)
    far_down[...] = gx[far, 64:, :].astype(BF)


def merge(idx, up, down, from_low, from_high, new_up, new_down):
    new_up[:64, :] = (up[:64, :].astype(F32) + from_low[...].astype(F32)).astype(BF)
    new_up[64:, :] = up[64:, :]
    new_down[:64, :] = down[:64, :]
    new_down[64:, :] = (down[64:, :].astype(F32) + from_high[...].astype(F32)).astype(BF)


def collect(scale, idx, parts, out):
    for head in range(8):
        for i in range(3):
            at = i * 1024 + head * HD
            out[:, at : at + HD] = parts[head, :, i * HD : (i + 1) * HD] * scale


def body(inputs, grad_out, saved, w_qkv):
    x = inputs[0]
    heads, head_size = saved.shape[2], saved.shape[3]
    length = x.shape[0] * lax.axis_size("ctx")
    alpha = 1.0 / head_size**0.5
    beta = 1.0 / (head_size * length) ** 0.5
    scale = 1.0 / (length * lax.axis_size("zero")) ** 0.5
    ctx = lax.axis_index("ctx")
    xi, yi, zi, ci = lax.axis_index("zero"), ctx // 8, (ctx // 2) % 4, ctx % 2
    idx = jnp.stack([xi, yi, zi, ci]).astype(jnp.int32)
    rows_y = [[ctx_index(y, z, c) for z in range(NZ) for c in range(NC)] for y in range(NY)]

    x1, x3 = ctx_hop(x, dz=1), ctx_hop(x, dz=-1)
    at = (2 * zi + ci) * HD
    own_w = jnp.concatenate(
        [lax.dynamic_slice(w_qkv, (0, i * heads * HD + at), (512, HD)) for i in range(3)], axis=1
    )
    (bundle,) = call(
        pack, [shape((8, 2, HD, HD), BF)], [after(idx, own_w), grad_out[0], saved[0, 0]]
    )
    gs = lax.all_to_all(bundle, "ctx", 0, 0, axis_index_groups=rows_y)
    w2, w1, w3 = (x_hop(own_w, s) for s in (2, 1, -1))
    x2a, x2b = ctx_hop(x1[:64], dz=1), ctx_hop(x3[64:], dz=-1)
    (own_w,) = call(relay, [shape((2048, 384), BF)], [idx, own_w, w1, w3, w2], flops=1 << 33, limit=6)
    first = [x, x1, x3]
    first += [ctx_hop(p, dc=1) for p in first]
    (xa,) = call(stack, [shape((768, 2048), BF)], [idx, *first], flops=1 << 33, limit=10)
    last = [x2a, x2b]
    last += [ctx_hop(after(p, gs), dc=1) for p in last]

    big = 2 * 1024 * 2048 * 384
    qkv, r, total, xb = call(
        project,
        [
            shape((1024, 384), BF),
            shape((8, HD, HD), F32),
            shape((HD, HD), BF),
            shape((256, 2048), BF),
        ],
        [idx, xa, *last, own_w, gs],
        flops=big,
    )
    totals = [ctx_hop(total, dy=s) for s in (1, 2, 3)]
    dq, dk0, dv0, xt = call(
        lambda *refs: within(alpha, beta, *refs),
        [shape((1024, HD), BF), shape((1024, HD), F32), shape((1024, HD), F32), shape((2048, 1024), BF)],
        [idx, xa, xb, gs, qkv],
        flops=big // 4,
    )
    dqkv, keep, send = call(
        lambda *refs: finish(beta, *refs),
        [shape((1024, 384), BF), shape((NZ, TOK, 384), BF), shape((NZ, TOK, 384), BF)],
        [idx, qkv, dq, dk0, dv0, r, *totals],
        flops=big // 16,
    )
    got = ctx_hop(send, dc=1)
    other_w = ctx_hop(after(own_w, send), dc=1)
    parts = call(
        weights,
        [shape((4, 8, 16, 384), BF)] * 4,
        [idx, xt, dqkv],
        [pltpu.VMEM((NY, 8, NX, 16, 384), BF)],
        flops=big,
    )
    gx, up, down, far_up, far_down = call(
        back,
        [shape((TOK, 2048), F32)] + [shape((TOK, 2048), BF)] * 2 + [shape((64, 2048), BF)] * 2,
        [idx, keep, got, own_w, other_w],
        [pltpu.VMEM((NZ, TOK, 2048), F32)],
        flops=big,
        deps=(parts[0],),
    )
    parts = [parts[0]] + [plane_hop(parts[s], s, 0) for s in (1, 2, 3)]
    far_up, far_down = ctx_hop(far_up, dz=1), ctx_hop(far_down, dz=-1)
    parts = call(turn, [shape((8, 16, 384), BF)] * 4, [idx, *parts], deps=(gx,), limit=4)
    up, down = call(
        merge, [shape((TOK, 2048), BF)] * 2, [idx, up, down, far_up, far_down], flops=1 << 33, deps=(parts[0],), limit=6
    )
    parts = [parts[0]] + [plane_hop(parts[s], s, 1) for s in (1, 2, 3)]
    up, down = ctx_hop(up, dz=1), ctx_hop(down, dz=-1)
    owned = sum(p.astype(F32) for p in parts)
    owned = lax.all_to_all(owned, "ctx", 0, 0, axis_index_groups=rows_y)
    (grad_w,) = call(
        lambda *refs: collect(scale, *refs),
        [shape((16, 3 * heads * HD), F32)],
        [idx, owned],
        flops=1 << 31,
        limit=4,
    )
    grad_x = (gx + up.astype(F32) + down.astype(F32)).astype(BF)
    return (grad_x[None], grad_w)


def solution(mesh):
    in_specs = (
        P("zero", "ctx", None),
        P("zero", "ctx", None),
        P("zero", "ctx", None, None, None),
        P("zero", None),
    )
    out_specs = (P("zero", "ctx", None), P(("ctx", "zero"), None))
    return jax.shard_map(body, mesh=mesh, in_specs=in_specs, out_specs=out_specs, check_vma=False)
```

```python
import jax
import jax.numpy as jnp
from jax import lax
from jax.experimental import pallas as pl
from jax.experimental.pallas import tpu as pltpu
from jax.sharding import PartitionSpec as P

NY, NZ, NC, NX = 4, 4, 2, 4
TOK, HD = 128, 128
BF, F32 = jnp.bfloat16, jnp.float32


def ctx_index(y, z, c):
    return (y * NZ + z) * NC + c


def ctx_hop(block, dy=0, dz=0, dc=0):
    route = [
        (ctx_index(y, z, c), ctx_index((y + dy) % NY, (z + dz) % NZ, (c + dc) % NC))
        for y in range(NY)
        for z in range(NZ)
        for c in range(NC)
    ]
    return lax.ppermute(block, "ctx", route)


def x_hop(block, dx):
    return lax.ppermute(block, "zero", [(i, (i + dx) % NX) for i in range(NX)])


def plane_hop(block, step, stage):
    route = []
    for y in range(NY):
        for z in range(NZ):
            for c in range(NC):
                for x in range(NX):
                    dx, dy = (step, 0) if c == stage else (0, step)
                    to = ctx_index((y + dy) % NY, z, c) * NX + (x + dx) % NX
                    route.append((ctx_index(y, z, c) * NX + x, to))
    return lax.ppermute(block, ("ctx", "zero"), route)


def dot(a, b):
    return lax.dot_general(a, b, (((1,), (0,)), ((), ())), preferred_element_type=F32)


def dot_nt(a, b):
    return lax.dot_general(a, b, (((1,), (1,)), ((), ())), preferred_element_type=F32)


def dot_tn(a, b):
    return lax.dot_general(a, b, (((0,), (0,)), ((), ())), preferred_element_type=F32)


def call(kernel, outs, ins, scratch=(), flops=0, limit=16, deps=(), free=()):
    count = len(ins)

    def run(*refs):
        kernel(*refs[:count], *refs[count + len(deps) :])

    moved = sum(a.size * a.dtype.itemsize for a in list(ins) + list(outs))
    vmem = pl.BlockSpec(memory_space=pltpu.VMEM)
    return pl.pallas_call(
        run,
        out_shape=list(outs),
        in_specs=[pl.BlockSpec(memory_space=pltpu.SMEM)]
        + [pl.BlockSpec(memory_space=pl.ANY) if i in free else vmem for i in range(1, count)]
        + [pl.BlockSpec(memory_space=pl.ANY)] * len(deps),
        out_specs=[vmem] * len(outs),
        scratch_shapes=list(scratch),
        compiler_params=pltpu.CompilerParams(vmem_limit_bytes=limit << 20),
        cost_estimate=pl.CostEstimate(flops=flops, bytes_accessed=moved, transcendentals=0),
    )(*ins, *deps)


def shape(dims, dtype):
    return jax.ShapeDtypeStruct(dims, dtype)


def after(value, deps):
    return lax.optimization_barrier((value, deps))[0]


def columns(place, step, start=0, size=512):
    block = lax.rem(place + NX - step, NX)
    return pl.ds(pl.multiple_of(block * 512 + start, 256), size)


NEAR = (0, 1, 3)


def block_at(idx, place):
    slot = NEAR[place % 3] if place < 6 else 2
    mate = place in (3, 4, 5, 7)
    core = 1 - idx[3] if mate else idx[3]
    return lax.rem(idx[2] + NZ - slot, NZ) * 2 + core


def rows_of(idx, z, mate):
    slot = lax.rem(idx[2] + NZ - z, NZ)
    near = jnp.where(slot == 3, 2, slot) + 3 * mate
    return pl.ds(pl.multiple_of(jnp.where(slot == 2, 6 + mate, near) * TOK, TOK), TOK)


def pack(idx, cot, state, out):
    for h in range(8):
        out[h, 0] = cot[:, h * HD : (h + 1) * HD]
        out[h, 1] = state[h].astype(BF)


def relay(idx, w0, w1, w3, w2, wkeep):
    for part, step in ((w0, 0), (w1, 1), (w3, 3), (w2, 2)):
        wkeep[columns(idx[0], step, 0, 512), :] = part[...]


def stack(idx, *refs):
    parts, xa = refs[:6], refs[6]
    for i, part in enumerate(parts):
        xa[i * TOK : (i + 1) * TOK, :] = part[...]


def project(idx, xa, x2a, x2b, m2a, m2b, wkeep, gs, qkv, r, total, xb):
    for i, part in enumerate((x2a, x2b, m2a, m2b)):
        xb[i * 64 : (i + 1) * 64, :] = part[...]
    whole = jnp.zeros((HD, HD), F32)
    for m in range(4):
        rows = slice(m * 256, (m + 1) * 256)
        tokens = xa[rows, :] if m < 3 else xb[...]
        rounded = dot(tokens, wkeep[...]).astype(BF)
        qkv[rows, :] = rounded
        for i in range(2):
            block = block_at(idx, 2 * m + i)
            piece = dot_tn(rounded[i * TOK : (i + 1) * TOK, :HD], gs[block, 0])
            r[block] = piece
            whole += piece
    total[...] = whole.astype(BF)


def within(alpha, beta, idx, xa, xb, gs, qkv, dq, dk0, dv0, xt):
    rowi = lax.broadcasted_iota(jnp.int32, (TOK, TOK), 0)
    coli = lax.broadcasted_iota(jnp.int32, (TOK, TOK), 1)
    mask = rowi >= coli
    for place in range(8):
        rows = slice(place * TOK, (place + 1) * TOK)
        q, k, v = (qkv[rows, i * HD : (i + 1) * HD] for i in range(3))
        block = block_at(idx, place)
        g, state = gs[block, 0], gs[block, 1]
        p1 = jnp.where(mask, dot_nt(g, v), 0.0).astype(BF)
        p2 = jnp.where(mask, dot_nt(q, k), 0.0).astype(BF)
        dq[rows, :] = (alpha * dot_nt(g, state) + beta * dot(p1, k)).astype(BF)
        dk0[rows, :] = dot_tn(p1, q)
        dv0[rows, :] = dot_tn(p2, g)
        xt[:, rows] = xa[rows, :].T if place < 6 else xb[place * TOK - 768 : place * TOK - 640, :].T


def finish(beta, idx, qkv, dq, dk0, dv0, r, t1, t2, t3, dqkv, keep, send):
    yi, ci = idx[1], idx[3]
    acc = jnp.zeros((HD, HD), F32)
    for step, total in enumerate((t1, t2, t3)):
        use = jnp.where(yi < step + 1, 1.0, 0.0).astype(F32)
        acc += use * total[...].astype(F32)
    for b in range(7, -1, -1):
        rows = rows_of(idx, b // 2, jnp.where(ci == b % 2, 0, 1))
        k, v = qkv[rows, HD : 2 * HD], qkv[rows, 2 * HD :]
        later = acc.astype(BF)
        dqkv[rows, :HD] = dq[rows, :]
        dqkv[rows, HD : 2 * HD] = (beta * (dk0[rows, :] + dot_nt(v, later))).astype(BF)
        dqkv[rows, 2 * HD :] = (beta * (dv0[rows, :] + dot(k, later))).astype(BF)
        acc += r[b]
    for z in range(NZ):
        keep[z] = dqkv[rows_of(idx, z, 0), :]
        send[z] = dqkv[rows_of(idx, z, 1), :]


def weights(idx, xt, dqkv, *refs):
    outs, buf = refs[:4], refs[4]
    xi, yi, ci = idx[0], idx[1], idx[3]
    for m in range(4):
        rows = slice(m * 512, (m + 1) * 512)
        tile = dot(xt[rows, :], dqkv[...]).astype(BF)
        buf[m] = tile.reshape(8, NX, 16, 384)
    for s in range(4):
        for j in range(4):
            y = jnp.where(ci == 0, j, lax.rem(yi + s, NY))
            x = jnp.where(ci == 0, lax.rem(xi + s, NX), j)
            for g in range(8):
                outs[s][j, g] = buf[y, g, x]


def turn(idx, *refs):
    parts, outs = refs[:4], refs[4:]
    place = jnp.where(idx[3] == 0, idx[1], idx[0])
    for s in range(4):
        j = lax.rem(place + s, 4)
        for g in range(8):
            outs[s][g] = sum(p[j, g].astype(F32) for p in parts).astype(BF)


def far_back(idx, keep, got, own, other, far_up, far_down):
    far = lax.rem(idx[2] + 2, NZ)
    for n in range(4):
        cols = slice(n * 512, (n + 1) * 512)
        part = (dot_nt(keep[far], own[cols, :]) + dot_nt(got[far], other[cols, :])).astype(BF)
        far_up[:, cols] = part[:64, :]
        far_down[:, cols] = part[64:, :]


def near_back(idx, keep, got, own, other, mine_gx, up, down, mine, theirs):
    for i, step in enumerate((0, 1, 3)):
        z = lax.rem(idx[2] + step, NZ)
        rows = slice(i * TOK, (i + 1) * TOK)
        mine[rows, :] = keep[z]
        theirs[rows, :] = got[z]
    for n in range(4):
        cols = slice(n * 512, (n + 1) * 512)
        part = dot_nt(mine[...], own[cols, :]) + dot_nt(theirs[...], other[cols, :])
        mine_gx[:, cols] = part[:TOK, :]
        up[:, cols] = part[TOK : 2 * TOK, :].astype(BF)
        down[:, cols] = part[2 * TOK :, :].astype(BF)


def merge(idx, up, down, from_low, from_high, new_up, new_down):
    new_up[:64, :] = (up[:64, :].astype(F32) + from_low[...].astype(F32)).astype(BF)
    new_up[64:, :] = up[64:, :]
    new_down[:64, :] = down[:64, :]
    new_down[64:, :] = (down[64:, :].astype(F32) + from_high[...].astype(F32)).astype(BF)


def collect(scale, idx, parts, out):
    for head in range(8):
        for i in range(3):
            at = i * 1024 + head * HD
            out[:, at : at + HD] = parts[head, :, i * HD : (i + 1) * HD].astype(F32) * scale


def body(inputs, grad_out, saved, w_qkv):
    x = inputs[0]
    heads, head_size = saved.shape[2], saved.shape[3]
    length = x.shape[0] * lax.axis_size("ctx")
    alpha = 1.0 / head_size**0.5
    beta = 1.0 / (head_size * length) ** 0.5
    scale = 1.0 / (length * lax.axis_size("zero")) ** 0.5
    ctx = lax.axis_index("ctx")
    xi, yi, zi, ci = lax.axis_index("zero"), ctx // 8, (ctx // 2) % 4, ctx % 2
    idx = jnp.stack([xi, yi, zi, ci]).astype(jnp.int32)
    rows_y = [[ctx_index(y, z, c) for z in range(NZ) for c in range(NC)] for y in range(NY)]

    x1, x3 = ctx_hop(x, dz=1), ctx_hop(x, dz=-1)
    at = (2 * zi + ci) * HD
    own_w = jnp.concatenate(
        [lax.dynamic_slice(w_qkv, (0, i * heads * HD + at), (512, HD)) for i in range(3)], axis=1
    )
    (bundle,) = call(
        pack, [shape((8, 2, HD, HD), BF)], [after(idx, own_w), grad_out[0], saved[0, 0]]
    )
    gs = lax.all_to_all(bundle, "ctx", 0, 0, axis_index_groups=rows_y)
    w2, w1, w3 = (x_hop(own_w, s) for s in (2, 1, -1))
    x2a, x2b = ctx_hop(x1[:64], dz=1), ctx_hop(x3[64:], dz=-1)
    (own_w,) = call(relay, [shape((2048, 384), BF)], [idx, own_w, w1, w3, w2], flops=1 << 33, limit=6)
    first = [x, x1, x3]
    first += [ctx_hop(p, dc=1) for p in first]
    (xa,) = call(stack, [shape((768, 2048), BF)], [idx, *first], flops=1 << 33, limit=10)
    last = [x2a, x2b]
    last += [ctx_hop(after(p, gs), dc=1) for p in last]

    big = 2 * 1024 * 2048 * 384
    qkv, r, total, xb = call(
        project,
        [
            shape((1024, 384), BF),
            shape((8, HD, HD), F32),
            shape((HD, HD), BF),
            shape((256, 2048), BF),
        ],
        [idx, xa, *last, own_w, gs],
        flops=big,
    )
    totals = [ctx_hop(total, dy=s) for s in (1, 2, 3)]
    dq, dk0, dv0, xt = call(
        lambda *refs: within(alpha, beta, *refs),
        [shape((1024, HD), BF), shape((1024, HD), F32), shape((1024, HD), F32), shape((2048, 1024), BF)],
        [idx, xa, xb, gs, qkv],
        flops=big // 4,
    )
    dqkv, keep, send = call(
        lambda *refs: finish(beta, *refs),
        [shape((1024, 384), BF), shape((NZ, TOK, 384), BF), shape((NZ, TOK, 384), BF)],
        [idx, qkv, dq, dk0, dv0, r, *totals],
        flops=big // 16,
    )
    got = ctx_hop(send, dc=1)
    other_w = ctx_hop(after(own_w, send), dc=1)
    far_up, far_down = call(
        far_back,
        [shape((64, 2048), BF)] * 2,
        [idx, keep, got, own_w, other_w],
        flops=big // 4,
        limit=8,
    )
    parts = call(
        weights,
        [shape((4, 8, 16, 384), BF)] * 4,
        [idx, xt, dqkv],
        [pltpu.VMEM((NY, 8, NX, 16, 384), BF)],
        flops=big,
        deps=(far_up,),
    )
    gx, up, down = call(
        near_back,
        [shape((TOK, 2048), F32)] + [shape((TOK, 2048), BF)] * 2,
        [idx, keep, got, own_w, other_w],
        [pltpu.VMEM((384, 384), BF)] * 2,
        flops=big,
        deps=(parts[0],),
        limit=12,
    )
    parts = [parts[0]] + [plane_hop(parts[s], s, 0) for s in (1, 2, 3)]
    far_up, far_down = ctx_hop(far_up, dz=1), ctx_hop(far_down, dz=-1)
    parts = call(turn, [shape((8, 16, 384), BF)] * 4, [idx, *parts], deps=(gx,), limit=4)
    up, down = call(
        merge, [shape((TOK, 2048), BF)] * 2, [idx, up, down, far_up, far_down], flops=1 << 34, deps=(gx,), limit=6
    )
    parts = [parts[0]] + [plane_hop(parts[s], s, 1) for s in (1, 2, 3)]
    up, down = ctx_hop(up, dz=1), ctx_hop(down, dz=-1)
    owned = sum(p.astype(F32) for p in parts).astype(BF)
    owned = lax.all_to_all(owned, "ctx", 0, 0, axis_index_groups=rows_y)
    (grad_w,) = call(
        lambda *refs: collect(scale, *refs),
        [shape((16, 3 * heads * HD), F32)],
        [idx, owned],
        flops=0,
        limit=4,
    )
    grad_x = (gx + up.astype(F32) + down.astype(F32)).astype(BF)
    return (grad_x[None], grad_w)


def solution(mesh):
    in_specs = (
        P("zero", "ctx", None),
        P("zero", "ctx", None),
        P("zero", "ctx", None, None, None),
        P("zero", None),
    )
    out_specs = (P("zero", "ctx", None), P(("ctx", "zero"), None))
    return jax.shard_map(body, mesh=mesh, in_specs=in_specs, out_specs=out_specs, check_vma=False)
```

```python
import jax
import jax.numpy as jnp
from jax import lax
from jax.experimental import pallas as pl
from jax.experimental.pallas import tpu as pltpu
from jax.sharding import PartitionSpec as P

NY, NZ, NC, NX = 4, 4, 2, 4
TOK, HD = 128, 128
BF, F32 = jnp.bfloat16, jnp.float32


def ctx_index(y, z, c):
    return (y * NZ + z) * NC + c


def ctx_hop(block, dy=0, dz=0, dc=0):
    route = [
        (ctx_index(y, z, c), ctx_index((y + dy) % NY, (z + dz) % NZ, (c + dc) % NC))
        for y in range(NY)
        for z in range(NZ)
        for c in range(NC)
    ]
    return lax.ppermute(block, "ctx", route)


def x_hop(block, dx):
    return lax.ppermute(block, "zero", [(i, (i + dx) % NX) for i in range(NX)])


def plane_hop(block, step, stage):
    route = []
    for y in range(NY):
        for z in range(NZ):
            for c in range(NC):
                for x in range(NX):
                    dx, dy = (step, 0) if c == stage else (0, step)
                    to = ctx_index((y + dy) % NY, z, c) * NX + (x + dx) % NX
                    route.append((ctx_index(y, z, c) * NX + x, to))
    return lax.ppermute(block, ("ctx", "zero"), route)


def dot(a, b):
    return lax.dot_general(a, b, (((1,), (0,)), ((), ())), preferred_element_type=F32)


def dot_nt(a, b):
    return lax.dot_general(a, b, (((1,), (1,)), ((), ())), preferred_element_type=F32)


def dot_tn(a, b):
    return lax.dot_general(a, b, (((0,), (0,)), ((), ())), preferred_element_type=F32)


def call(kernel, outs, ins, scratch=(), flops=0, limit=16, deps=(), free=()):
    count = len(ins)

    def run(*refs):
        kernel(*refs[:count], *refs[count + len(deps) :])

    moved = sum(a.size * a.dtype.itemsize for a in list(ins) + list(outs))
    vmem = pl.BlockSpec(memory_space=pltpu.VMEM)
    return pl.pallas_call(
        run,
        out_shape=list(outs),
        in_specs=[pl.BlockSpec(memory_space=pltpu.SMEM)]
        + [pl.BlockSpec(memory_space=pl.ANY) if i in free else vmem for i in range(1, count)]
        + [pl.BlockSpec(memory_space=pl.ANY)] * len(deps),
        out_specs=[vmem] * len(outs),
        scratch_shapes=list(scratch),
        compiler_params=pltpu.CompilerParams(vmem_limit_bytes=limit << 20),
        cost_estimate=pl.CostEstimate(flops=flops, bytes_accessed=moved, transcendentals=0),
    )(*ins, *deps)


def shape(dims, dtype):
    return jax.ShapeDtypeStruct(dims, dtype)


def after(value, deps):
    return lax.optimization_barrier((value, deps))[0]


def columns(place, step, start=0, size=512):
    block = lax.rem(place + NX - step, NX)
    return pl.ds(pl.multiple_of(block * 512 + start, 256), size)


NEAR = (0, 1, 3)


def block_at(idx, place):
    slot = NEAR[place % 3] if place < 6 else 2
    mate = place in (3, 4, 5, 7)
    core = 1 - idx[3] if mate else idx[3]
    return lax.rem(idx[2] + NZ - slot, NZ) * 2 + core


def rows_of(idx, z, mate):
    slot = lax.rem(idx[2] + NZ - z, NZ)
    near = jnp.where(slot == 3, 2, slot) + 3 * mate
    return pl.ds(pl.multiple_of(jnp.where(slot == 2, 6 + mate, near) * TOK, TOK), TOK)


def pack(idx, cot, state, out):
    for h in range(8):
        out[h, 0] = cot[:, h * HD : (h + 1) * HD]
        out[h, 1] = state[h].astype(BF)


def relay(idx, w0, w1, w3, w2, wkeep):
    for part, step in ((w0, 0), (w1, 1), (w3, 3), (w2, 2)):
        wkeep[columns(idx[0], step, 0, 512), :] = part[...]


def stack(idx, *refs):
    parts, xa = refs[:6], refs[6]
    for i, part in enumerate(parts):
        xa[i * TOK : (i + 1) * TOK, :] = part[...]


def project(idx, xa, x2a, x2b, m2a, m2b, wkeep, gs, qkv, r, total, xb):
    for i, part in enumerate((x2a, x2b, m2a, m2b)):
        xb[i * 64 : (i + 1) * 64, :] = part[...]
    whole = jnp.zeros((HD, HD), F32)
    for m in range(4):
        rows = slice(m * 256, (m + 1) * 256)
        tokens = xa[rows, :] if m < 3 else xb[...]
        rounded = dot(tokens, wkeep[...]).astype(BF)
        qkv[rows, :] = rounded
        for i in range(2):
            block = block_at(idx, 2 * m + i)
            piece = dot_tn(rounded[i * TOK : (i + 1) * TOK, :HD], gs[block, 0])
            r[block] = piece
            whole += piece
    total[...] = whole.astype(BF)


def within(alpha, beta, idx, xa, xb, gs, qkv, dq, dk0, dv0, xt):
    rowi = lax.broadcasted_iota(jnp.int32, (TOK, TOK), 0)
    coli = lax.broadcasted_iota(jnp.int32, (TOK, TOK), 1)
    mask = rowi >= coli
    for place in range(8):
        rows = slice(place * TOK, (place + 1) * TOK)
        q, k, v = (qkv[rows, i * HD : (i + 1) * HD] for i in range(3))
        block = block_at(idx, place)
        g, state = gs[block, 0], gs[block, 1]
        p1 = jnp.where(mask, dot_nt(g, v), 0.0).astype(BF)
        p2 = jnp.where(mask, dot_nt(q, k), 0.0).astype(BF)
        dq[rows, :] = (alpha * dot_nt(g, state) + beta * dot(p1, k)).astype(BF)
        dk0[rows, :] = dot_tn(p1, q)
        dv0[rows, :] = dot_tn(p2, g)
        xt[:, rows] = xa[rows, :].T if place < 6 else xb[place * TOK - 768 : place * TOK - 640, :].T


def finish(beta, idx, qkv, dq, dk0, dv0, r, t1, t2, t3, dqkv, keep, send):
    yi, ci = idx[1], idx[3]
    acc = jnp.zeros((HD, HD), F32)
    for step, total in enumerate((t1, t2, t3)):
        use = jnp.where(yi < step + 1, 1.0, 0.0).astype(F32)
        acc += use * total[...].astype(F32)
    for b in range(7, -1, -1):
        rows = rows_of(idx, b // 2, jnp.where(ci == b % 2, 0, 1))
        k, v = qkv[rows, HD : 2 * HD], qkv[rows, 2 * HD :]
        later = acc.astype(BF)
        dqkv[rows, :HD] = dq[rows, :]
        dqkv[rows, HD : 2 * HD] = (beta * (dk0[rows, :] + dot_nt(v, later))).astype(BF)
        dqkv[rows, 2 * HD :] = (beta * (dv0[rows, :] + dot(k, later))).astype(BF)
        acc += r[b]
    for z in range(NZ):
        keep[z] = dqkv[rows_of(idx, z, 0), :]
        send[z] = dqkv[rows_of(idx, z, 1), :]


def weights(idx, xt, dqkv, *refs):
    outs, buf = refs[:4], refs[4]
    xi, yi, ci = idx[0], idx[1], idx[3]
    for m in range(4):
        rows = slice(m * 512, (m + 1) * 512)
        tile = dot(xt[rows, :], dqkv[...]).astype(BF)
        buf[m] = tile.reshape(8, NX, 16, 384)
    for s in range(4):
        for j in range(4):
            y = jnp.where(ci == 0, j, lax.rem(yi + s, NY))
            x = jnp.where(ci == 0, lax.rem(xi + s, NX), j)
            for g in range(8):
                outs[s][j, g] = buf[y, g, x]


def turn(idx, *refs):
    parts, outs = refs[:4], refs[4:]
    place = jnp.where(idx[3] == 0, idx[1], idx[0])
    for s in range(4):
        j = lax.rem(place + s, 4)
        for g in range(8):
            outs[s][g] = sum(p[j, g].astype(F32) for p in parts).astype(BF)


def far_back(idx, keep, got, own, other, far_up, far_down):
    far = lax.rem(idx[2] + 2, NZ)
    for n in range(4):
        cols = slice(n * 512, (n + 1) * 512)
        part = (dot_nt(keep[far], own[cols, :]) + dot_nt(got[far], other[cols, :])).astype(BF)
        far_up[:, cols] = part[:64, :]
        far_down[:, cols] = part[64:, :]


def near_back(idx, keep, got, own, other, mine_gx, up, down, mine, theirs):
    for i, step in enumerate((0, 1, 3)):
        z = lax.rem(idx[2] + step, NZ)
        rows = slice(i * TOK, (i + 1) * TOK)
        mine[rows, :] = keep[z]
        theirs[rows, :] = got[z]
    for n in range(4):
        cols = slice(n * 512, (n + 1) * 512)
        part = dot_nt(mine[...], own[cols, :]) + dot_nt(theirs[...], other[cols, :])
        mine_gx[:, cols] = part[:TOK, :]
        up[:, cols] = part[TOK : 2 * TOK, :].astype(BF)
        down[:, cols] = part[2 * TOK :, :].astype(BF)


def merge(idx, up, down, from_low, from_high, new_up, new_down):
    new_up[:64, :] = (up[:64, :].astype(F32) + from_low[...].astype(F32)).astype(BF)
    new_up[64:, :] = up[64:, :]
    new_down[:64, :] = down[:64, :]
    new_down[64:, :] = (down[64:, :].astype(F32) + from_high[...].astype(F32)).astype(BF)


def close(scale, idx, parts, mine, up, down, grad_w, grad_x):
    for head in range(8):
        for i in range(3):
            at = i * 1024 + head * HD
            grad_w[:, at : at + HD] = parts[head, :, i * HD : (i + 1) * HD].astype(F32) * scale
    grad_x[...] = (mine[...] + up[...].astype(F32) + down[...].astype(F32)).astype(BF)


def body(inputs, grad_out, saved, w_qkv):
    x = inputs[0]
    heads, head_size = saved.shape[2], saved.shape[3]
    length = x.shape[0] * lax.axis_size("ctx")
    alpha = 1.0 / head_size**0.5
    beta = 1.0 / (head_size * length) ** 0.5
    scale = 1.0 / (length * lax.axis_size("zero")) ** 0.5
    ctx = lax.axis_index("ctx")
    xi, yi, zi, ci = lax.axis_index("zero"), ctx // 8, (ctx // 2) % 4, ctx % 2
    idx = jnp.stack([xi, yi, zi, ci]).astype(jnp.int32)
    rows_y = [[ctx_index(y, z, c) for z in range(NZ) for c in range(NC)] for y in range(NY)]

    x1, x3 = ctx_hop(x, dz=1), ctx_hop(x, dz=-1)
    at = (2 * zi + ci) * HD
    own_w = jnp.concatenate(
        [lax.dynamic_slice(w_qkv, (0, i * heads * HD + at), (512, HD)) for i in range(3)], axis=1
    )
    (bundle,) = call(
        pack, [shape((8, 2, HD, HD), BF)], [after(idx, own_w), grad_out[0], saved[0, 0]]
    )
    gs = lax.all_to_all(bundle, "ctx", 0, 0, axis_index_groups=rows_y)
    w2, w1, w3 = (x_hop(own_w, s) for s in (2, 1, -1))
    x2a, x2b = ctx_hop(x1[:64], dz=1), ctx_hop(x3[64:], dz=-1)
    (own_w,) = call(relay, [shape((2048, 384), BF)], [idx, own_w, w1, w3, w2], flops=1 << 33, limit=6)
    first = [x, x1, x3]
    first += [ctx_hop(p, dc=1) for p in first]
    (xa,) = call(stack, [shape((768, 2048), BF)], [idx, *first], flops=1 << 33, limit=10)
    last = [x2a, x2b]
    last += [ctx_hop(after(p, gs), dc=1) for p in last]

    big = 2 * 1024 * 2048 * 384
    qkv, r, total, xb = call(
        project,
        [
            shape((1024, 384), BF),
            shape((8, HD, HD), F32),
            shape((HD, HD), BF),
            shape((256, 2048), BF),
        ],
        [idx, xa, *last, own_w, gs],
        flops=big,
    )
    totals = [ctx_hop(total, dy=s) for s in (1, 2, 3)]
    dq, dk0, dv0, xt = call(
        lambda *refs: within(alpha, beta, *refs),
        [shape((1024, HD), BF), shape((1024, HD), F32), shape((1024, HD), F32), shape((2048, 1024), BF)],
        [idx, xa, xb, gs, qkv],
        flops=big // 4,
    )
    dqkv, keep, send = call(
        lambda *refs: finish(beta, *refs),
        [shape((1024, 384), BF), shape((NZ, TOK, 384), BF), shape((NZ, TOK, 384), BF)],
        [idx, qkv, dq, dk0, dv0, r, *totals],
        flops=big // 16,
    )
    got = ctx_hop(send, dc=1)
    other_w = ctx_hop(after(own_w, send), dc=1)
    parts = call(
        weights,
        [shape((4, 8, 16, 384), BF)] * 4,
        [idx, xt, dqkv],
        [pltpu.VMEM((NY, 8, NX, 16, 384), BF)],
        flops=big,
    )
    far_up, far_down = call(
        far_back,
        [shape((64, 2048), BF)] * 2,
        [idx, keep, got, own_w, other_w],
        flops=big // 4,
        deps=(parts[0],),
        limit=8,
    )
    gx, up, down = call(
        near_back,
        [shape((TOK, 2048), F32)] + [shape((TOK, 2048), BF)] * 2,
        [idx, keep, got, own_w, other_w],
        [pltpu.VMEM((384, 384), BF)] * 2,
        flops=big,
        deps=(far_up,),
        limit=12,
    )
    parts = [parts[0]] + [plane_hop(parts[s], s, 0) for s in (1, 2, 3)]
    far_up, far_down = ctx_hop(far_up, dz=1), ctx_hop(far_down, dz=-1)
    parts = call(turn, [shape((8, 16, 384), BF)] * 4, [idx, *parts], deps=(gx,), limit=4)
    up, down = call(
        merge, [shape((TOK, 2048), BF)] * 2, [idx, up, down, far_up, far_down], flops=1 << 34, deps=(parts[0],), limit=6
    )
    parts = [parts[0]] + [plane_hop(parts[s], s, 1) for s in (1, 2, 3)]
    up, down = ctx_hop(up, dz=1), ctx_hop(down, dz=-1)
    owned = sum(p.astype(F32) for p in parts).astype(BF)
    owned = lax.all_to_all(owned, "ctx", 0, 0, axis_index_groups=rows_y)
    grad_w, grad_x = call(
        lambda *refs: close(scale, *refs),
        [shape((16, 3 * heads * HD), F32), shape((TOK, 2048), BF)],
        [idx, owned, gx, up, down],
        flops=0,
        limit=8,
    )
    return (grad_x[None], grad_w)


def solution(mesh):
    in_specs = (
        P("zero", "ctx", None),
        P("zero", "ctx", None),
        P("zero", "ctx", None, None, None),
        P("zero", None),
    )
    out_specs = (P("zero", "ctx", None), P(("ctx", "zero"), None))
    return jax.shard_map(body, mesh=mesh, in_specs=in_specs, out_specs=out_specs, check_vma=False)
```

```python
import jax
import jax.numpy as jnp
from jax import lax
from jax.experimental import pallas as pl
from jax.experimental.pallas import tpu as pltpu
from jax.sharding import PartitionSpec as P

NY, NZ, NC, NX = 4, 4, 2, 4
TOK, HD = 128, 128
BF, F32 = jnp.bfloat16, jnp.float32


def ctx_index(y, z, c):
    return (y * NZ + z) * NC + c


def ctx_hop(block, dy=0, dz=0, dc=0):
    route = [
        (ctx_index(y, z, c), ctx_index((y + dy) % NY, (z + dz) % NZ, (c + dc) % NC))
        for y in range(NY)
        for z in range(NZ)
        for c in range(NC)
    ]
    return lax.ppermute(block, "ctx", route)


def x_hop(block, dx):
    return lax.ppermute(block, "zero", [(i, (i + dx) % NX) for i in range(NX)])


def plane_hop(block, step, stage):
    route = []
    for y in range(NY):
        for z in range(NZ):
            for c in range(NC):
                for x in range(NX):
                    dx, dy = (step, 0) if c == stage else (0, step)
                    to = ctx_index((y + dy) % NY, z, c) * NX + (x + dx) % NX
                    route.append((ctx_index(y, z, c) * NX + x, to))
    return lax.ppermute(block, ("ctx", "zero"), route)


def dot(a, b):
    return lax.dot_general(a, b, (((1,), (0,)), ((), ())), preferred_element_type=F32)


def dot_nt(a, b):
    return lax.dot_general(a, b, (((1,), (1,)), ((), ())), preferred_element_type=F32)


def dot_tn(a, b):
    return lax.dot_general(a, b, (((0,), (0,)), ((), ())), preferred_element_type=F32)


def call(kernel, outs, ins, scratch=(), flops=0, limit=16, deps=(), free=()):
    count = len(ins)

    def run(*refs):
        kernel(*refs[:count], *refs[count + len(deps) :])

    moved = sum(a.size * a.dtype.itemsize for a in list(ins) + list(outs))
    vmem = pl.BlockSpec(memory_space=pltpu.VMEM)
    return pl.pallas_call(
        run,
        out_shape=list(outs),
        in_specs=[pl.BlockSpec(memory_space=pltpu.SMEM)]
        + [pl.BlockSpec(memory_space=pl.ANY) if i in free else vmem for i in range(1, count)]
        + [pl.BlockSpec(memory_space=pl.ANY)] * len(deps),
        out_specs=[vmem] * len(outs),
        scratch_shapes=list(scratch),
        compiler_params=pltpu.CompilerParams(vmem_limit_bytes=limit << 20),
        cost_estimate=pl.CostEstimate(flops=flops, bytes_accessed=moved, transcendentals=0),
    )(*ins, *deps)


def shape(dims, dtype):
    return jax.ShapeDtypeStruct(dims, dtype)


def after(value, deps):
    return lax.optimization_barrier((value, deps))[0]


def columns(place, step, start=0, size=512):
    block = lax.rem(place + NX - step, NX)
    return pl.ds(pl.multiple_of(block * 512 + start, 256), size)


NEAR = (0, 1, 3)


def block_at(idx, place):
    slot = NEAR[place % 3] if place < 6 else 2
    mate = place in (3, 4, 5, 7)
    core = 1 - idx[3] if mate else idx[3]
    return lax.rem(idx[2] + NZ - slot, NZ) * 2 + core


def rows_of(idx, z, mate):
    slot = lax.rem(idx[2] + NZ - z, NZ)
    near = jnp.where(slot == 3, 2, slot) + 3 * mate
    return pl.ds(pl.multiple_of(jnp.where(slot == 2, 6 + mate, near) * TOK, TOK), TOK)


def pack(idx, cot, state, out):
    for h in range(8):
        out[h, 0] = cot[:, h * HD : (h + 1) * HD]
        out[h, 1] = state[h].astype(BF)


def relay(idx, w0, w1, w3, w2, wkeep):
    for part, step in ((w0, 0), (w1, 1), (w3, 3), (w2, 2)):
        wkeep[columns(idx[0], step, 0, 512), :] = part[...]


def stack(idx, *refs):
    parts, xa = refs[:6], refs[6]
    for i, part in enumerate(parts):
        xa[i * TOK : (i + 1) * TOK, :] = part[...]


def halve(idx, x1, x3, low, high):
    low[...] = x1[:64, :]
    high[...] = x3[64:, :]


def project(idx, xa, x2a, x2b, m2a, m2b, wkeep, gs, qkv, r, total, xb):
    for i, part in enumerate((x2a, x2b, m2a, m2b)):
        xb[i * 64 : (i + 1) * 64, :] = part[...]
    whole = jnp.zeros((HD, HD), F32)
    for m in range(4):
        rows = slice(m * 256, (m + 1) * 256)
        tokens = xa[rows, :] if m < 3 else xb[...]
        rounded = dot(tokens, wkeep[...]).astype(BF)
        qkv[rows, :] = rounded
        for i in range(2):
            block = block_at(idx, 2 * m + i)
            piece = dot_tn(rounded[i * TOK : (i + 1) * TOK, :HD], gs[block, 0])
            r[block] = piece
            whole += piece
    total[...] = whole.astype(BF)


def within(alpha, beta, idx, xa, xb, gs, qkv, dq, dk0, dv0, xt):
    rowi = lax.broadcasted_iota(jnp.int32, (TOK, TOK), 0)
    coli = lax.broadcasted_iota(jnp.int32, (TOK, TOK), 1)
    mask = rowi >= coli
    for place in range(8):
        rows = slice(place * TOK, (place + 1) * TOK)
        q, k, v = (qkv[rows, i * HD : (i + 1) * HD] for i in range(3))
        block = block_at(idx, place)
        g, state = gs[block, 0], gs[block, 1]
        p1 = jnp.where(mask, dot_nt(g, v), 0.0).astype(BF)
        p2 = jnp.where(mask, dot_nt(q, k), 0.0).astype(BF)
        dq[rows, :] = (alpha * dot_nt(g, state) + beta * dot(p1, k)).astype(BF)
        dk0[rows, :] = dot_tn(p1, q)
        dv0[rows, :] = dot_tn(p2, g)
        xt[:, rows] = xa[rows, :].T if place < 6 else xb[place * TOK - 768 : place * TOK - 640, :].T


def finish(beta, idx, qkv, dq, dk0, dv0, r, t1, t2, t3, dqkv, keep, send):
    yi, ci = idx[1], idx[3]
    acc = jnp.zeros((HD, HD), F32)
    for step, total in enumerate((t1, t2, t3)):
        use = jnp.where(yi < step + 1, 1.0, 0.0).astype(F32)
        acc += use * total[...].astype(F32)
    for b in range(7, -1, -1):
        rows = rows_of(idx, b // 2, jnp.where(ci == b % 2, 0, 1))
        k, v = qkv[rows, HD : 2 * HD], qkv[rows, 2 * HD :]
        later = acc.astype(BF)
        dqkv[rows, :HD] = dq[rows, :]
        dqkv[rows, HD : 2 * HD] = (beta * (dk0[rows, :] + dot_nt(v, later))).astype(BF)
        dqkv[rows, 2 * HD :] = (beta * (dv0[rows, :] + dot(k, later))).astype(BF)
        acc += r[b]
    for z in range(NZ):
        keep[z] = dqkv[rows_of(idx, z, 0), :]
        send[z] = dqkv[rows_of(idx, z, 1), :]


def weights(idx, xt, dqkv, *refs):
    outs, buf = refs[:4], refs[4]
    xi, yi, ci = idx[0], idx[1], idx[3]
    for m in range(4):
        rows = slice(m * 512, (m + 1) * 512)
        tile = dot(xt[rows, :], dqkv[...]).astype(BF)
        buf[m] = tile.reshape(8, NX, 16, 384)
    for s in range(4):
        for j in range(4):
            y = jnp.where(ci == 0, j, lax.rem(yi + s, NY))
            x = jnp.where(ci == 0, lax.rem(xi + s, NX), j)
            for g in range(8):
                outs[s][j, g] = buf[y, g, x]


def turn(idx, *refs):
    parts, outs = refs[:4], refs[4:]
    place = jnp.where(idx[3] == 0, idx[1], idx[0])
    for s in range(4):
        j = lax.rem(place + s, 4)
        for g in range(8):
            outs[s][g] = sum(p[j, g].astype(F32) for p in parts).astype(BF)


def far_back(idx, keep, got, own, other, far_up, far_down):
    far = lax.rem(idx[2] + 2, NZ)
    for n in range(4):
        cols = slice(n * 512, (n + 1) * 512)
        part = (dot_nt(keep[far], own[cols, :]) + dot_nt(got[far], other[cols, :])).astype(BF)
        far_up[:, cols] = part[:64, :]
        far_down[:, cols] = part[64:, :]


def near_back(idx, keep, got, own, other, mine_gx, up, down, mine, theirs):
    for i, step in enumerate((0, 1, 3)):
        z = lax.rem(idx[2] + step, NZ)
        rows = slice(i * TOK, (i + 1) * TOK)
        mine[rows, :] = keep[z]
        theirs[rows, :] = got[z]
    for n in range(4):
        cols = slice(n * 512, (n + 1) * 512)
        part = dot_nt(mine[...], own[cols, :]) + dot_nt(theirs[...], other[cols, :])
        mine_gx[:, cols] = part[:TOK, :]
        up[:, cols] = part[TOK : 2 * TOK, :].astype(BF)
        down[:, cols] = part[2 * TOK :, :].astype(BF)


def merge(idx, up, down, from_low, from_high, new_up, new_down):
    new_up[:64, :] = (up[:64, :].astype(F32) + from_low[...].astype(F32)).astype(BF)
    new_up[64:, :] = up[64:, :]
    new_down[:64, :] = down[:64, :]
    new_down[64:, :] = (down[64:, :].astype(F32) + from_high[...].astype(F32)).astype(BF)


def close(scale, idx, parts, mine, up, down, grad_w, grad_x):
    for head in range(8):
        for i in range(3):
            at = i * 1024 + head * HD
            grad_w[:, at : at + HD] = parts[head, :, i * HD : (i + 1) * HD].astype(F32) * scale
    grad_x[...] = (mine[...] + up[...].astype(F32) + down[...].astype(F32)).astype(BF)


def body(inputs, grad_out, saved, w_qkv):
    x = inputs[0]
    heads, head_size = saved.shape[2], saved.shape[3]
    length = x.shape[0] * lax.axis_size("ctx")
    alpha = 1.0 / head_size**0.5
    beta = 1.0 / (head_size * length) ** 0.5
    scale = 1.0 / (length * lax.axis_size("zero")) ** 0.5
    ctx = lax.axis_index("ctx")
    xi, yi, zi, ci = lax.axis_index("zero"), ctx // 8, (ctx // 2) % 4, ctx % 2
    idx = jnp.stack([xi, yi, zi, ci]).astype(jnp.int32)
    rows_y = [[ctx_index(y, z, c) for z in range(NZ) for c in range(NC)] for y in range(NY)]

    x1, x3 = ctx_hop(x, dz=1), ctx_hop(x, dz=-1)
    at = (2 * zi + ci) * HD
    own_w = jnp.concatenate(
        [lax.dynamic_slice(w_qkv, (0, i * heads * HD + at), (512, HD)) for i in range(3)], axis=1
    )
    (bundle,) = call(
        pack, [shape((8, 2, HD, HD), BF)], [after(idx, own_w), grad_out[0], saved[0, 0]]
    )
    gs = lax.all_to_all(bundle, "ctx", 0, 0, axis_index_groups=rows_y)
    w2, w1, w3 = (x_hop(own_w, s) for s in (2, 1, -1))
    low, high = call(halve, [shape((64, 2048), BF)] * 2, [idx, x1, x3], limit=6, deps=())
    x2a, x2b = ctx_hop(low, dz=1), ctx_hop(high, dz=-1)
    (own_w,) = call(relay, [shape((2048, 384), BF)], [idx, own_w, w1, w3, w2], flops=1 << 33, limit=6)
    first = [x, x1, x3]
    first += [ctx_hop(p, dc=1) for p in first]
    (xa,) = call(stack, [shape((768, 2048), BF)], [idx, *first], flops=1 << 33, limit=10)
    last = [x2a, x2b]
    last += [ctx_hop(after(p, gs), dc=1) for p in last]

    big = 2 * 1024 * 2048 * 384
    qkv, r, total, xb = call(
        project,
        [
            shape((1024, 384), BF),
            shape((8, HD, HD), F32),
            shape((HD, HD), BF),
            shape((256, 2048), BF),
        ],
        [idx, xa, *last, own_w, gs],
        flops=big,
    )
    totals = [ctx_hop(total, dy=s) for s in (1, 2, 3)]
    dq, dk0, dv0, xt = call(
        lambda *refs: within(alpha, beta, *refs),
        [shape((1024, HD), BF), shape((1024, HD), F32), shape((1024, HD), F32), shape((2048, 1024), BF)],
        [idx, xa, xb, gs, qkv],
        flops=big // 4,
    )
    dqkv, keep, send = call(
        lambda *refs: finish(beta, *refs),
        [shape((1024, 384), BF), shape((NZ, TOK, 384), BF), shape((NZ, TOK, 384), BF)],
        [idx, qkv, dq, dk0, dv0, r, *totals],
        flops=big // 16,
    )
    got = ctx_hop(send, dc=1)
    other_w = ctx_hop(after(own_w, send), dc=1)
    parts = call(
        weights,
        [shape((4, 8, 16, 384), BF)] * 4,
        [idx, xt, dqkv],
        [pltpu.VMEM((NY, 8, NX, 16, 384), BF)],
        flops=big,
    )
    far_up, far_down = call(
        far_back,
        [shape((64, 2048), BF)] * 2,
        [idx, keep, got, own_w, other_w],
        flops=big // 4,
        deps=(parts[0],),
        limit=8,
    )
    gx, up, down = call(
        near_back,
        [shape((TOK, 2048), F32)] + [shape((TOK, 2048), BF)] * 2,
        [idx, keep, got, own_w, other_w],
        [pltpu.VMEM((384, 384), BF)] * 2,
        flops=big,
        deps=(far_up,),
        limit=12,
    )
    parts = [parts[0]] + [plane_hop(parts[s], s, 0) for s in (1, 2, 3)]
    far_up, far_down = ctx_hop(far_up, dz=1), ctx_hop(far_down, dz=-1)
    parts = call(turn, [shape((8, 16, 384), BF)] * 4, [idx, *parts], deps=(gx,), limit=4)
    up, down = call(
        merge, [shape((TOK, 2048), BF)] * 2, [idx, up, down, far_up, far_down], flops=1 << 34, deps=(parts[0],), limit=6
    )
    parts = [parts[0]] + [plane_hop(parts[s], s, 1) for s in (1, 2, 3)]
    up, down = ctx_hop(up, dz=1), ctx_hop(down, dz=-1)
    owned = sum(p.astype(F32) for p in parts).astype(BF)
    owned = lax.all_to_all(owned, "ctx", 0, 0, axis_index_groups=rows_y)
    grad_w, grad_x = call(
        lambda *refs: close(scale, *refs),
        [shape((16, 3 * heads * HD), F32), shape((TOK, 2048), BF)],
        [idx, owned, gx, up, down],
        flops=0,
        limit=8,
    )
    return (grad_x[None], grad_w)


def solution(mesh):
    in_specs = (
        P("zero", "ctx", None),
        P("zero", "ctx", None),
        P("zero", "ctx", None, None, None),
        P("zero", None),
    )
    out_specs = (P("zero", "ctx", None), P(("ctx", "zero"), None))
    return jax.shard_map(body, mesh=mesh, in_specs=in_specs, out_specs=out_specs, check_vma=False)
```

```python
import jax
import jax.numpy as jnp
from jax import lax
from jax.experimental import pallas as pl
from jax.experimental.pallas import tpu as pltpu
from jax.sharding import PartitionSpec as P

NY, NZ, NC, NX = 4, 4, 2, 4
TOK, HD = 128, 128
BF, F32 = jnp.bfloat16, jnp.float32


def ctx_index(y, z, c):
    return (y * NZ + z) * NC + c


def ctx_hop(block, dy=0, dz=0, dc=0):
    route = [
        (ctx_index(y, z, c), ctx_index((y + dy) % NY, (z + dz) % NZ, (c + dc) % NC))
        for y in range(NY)
        for z in range(NZ)
        for c in range(NC)
    ]
    return lax.ppermute(block, "ctx", route)


def x_hop(block, dx):
    return lax.ppermute(block, "zero", [(i, (i + dx) % NX) for i in range(NX)])


def plane_hop(block, step, stage):
    route = []
    for y in range(NY):
        for z in range(NZ):
            for c in range(NC):
                for x in range(NX):
                    dx, dy = (step, 0) if c == stage else (0, step)
                    to = ctx_index((y + dy) % NY, z, c) * NX + (x + dx) % NX
                    route.append((ctx_index(y, z, c) * NX + x, to))
    return lax.ppermute(block, ("ctx", "zero"), route)


def dot(a, b):
    return lax.dot_general(a, b, (((1,), (0,)), ((), ())), preferred_element_type=F32)


def dot_nt(a, b):
    return lax.dot_general(a, b, (((1,), (1,)), ((), ())), preferred_element_type=F32)


def dot_tn(a, b):
    return lax.dot_general(a, b, (((0,), (0,)), ((), ())), preferred_element_type=F32)


def call(kernel, outs, ins, scratch=(), flops=0, limit=16, deps=(), free=()):
    count = len(ins)

    def run(*refs):
        kernel(*refs[:count], *refs[count + len(deps) :])

    moved = sum(a.size * a.dtype.itemsize for a in list(ins) + list(outs))
    vmem = pl.BlockSpec(memory_space=pltpu.VMEM)
    return pl.pallas_call(
        run,
        out_shape=list(outs),
        in_specs=[pl.BlockSpec(memory_space=pltpu.SMEM)]
        + [pl.BlockSpec(memory_space=pl.ANY) if i in free else vmem for i in range(1, count)]
        + [pl.BlockSpec(memory_space=pl.ANY)] * len(deps),
        out_specs=[vmem] * len(outs),
        scratch_shapes=list(scratch),
        compiler_params=pltpu.CompilerParams(vmem_limit_bytes=limit << 20),
        cost_estimate=pl.CostEstimate(flops=flops, bytes_accessed=moved, transcendentals=0),
    )(*ins, *deps)


def shape(dims, dtype):
    return jax.ShapeDtypeStruct(dims, dtype)


def after(value, deps):
    return lax.optimization_barrier((value, deps))[0]


def columns(place, step, start=0, size=512):
    block = lax.rem(place + NX - step, NX)
    return pl.ds(pl.multiple_of(block * 512 + start, 256), size)


NEAR = (0, 1, 3)


def block_at(idx, place):
    slot = NEAR[place % 3] if place < 6 else 2
    mate = place in (3, 4, 5, 7)
    core = 1 - idx[3] if mate else idx[3]
    return lax.rem(idx[2] + NZ - slot, NZ) * 2 + core


def rows_of(idx, z, mate):
    slot = lax.rem(idx[2] + NZ - z, NZ)
    near = jnp.where(slot == 3, 2, slot) + 3 * mate
    return pl.ds(pl.multiple_of(jnp.where(slot == 2, 6 + mate, near) * TOK, TOK), TOK)


def pack(idx, cot, state, out):
    for h in range(8):
        out[h, 0] = cot[:, h * HD : (h + 1) * HD]
        out[h, 1] = state[h].astype(BF)


def gate(idx, w1, w3, w2, out):
    out[...] = w1[:16, :HD] + w3[:16, :HD] + w2[:16, :HD]


def stack(idx, *refs):
    parts, xa = refs[:6], refs[6]
    for i, part in enumerate(parts):
        xa[i * TOK : (i + 1) * TOK, :] = part[...]


def project(idx, xa, x2a, x2b, m2a, m2b, w0, w1, w3, w2, gs, qkv, r, total, xb, wkeep):
    for i, part in enumerate((x2a, x2b, m2a, m2b)):
        xb[i * 64 : (i + 1) * 64, :] = part[...]
    for part, step in ((w0, 0), (w1, 1), (w3, 3), (w2, 2)):
        wkeep[columns(idx[0], step, 0, 512), :] = part[...]
    whole = jnp.zeros((HD, HD), F32)
    for m in range(4):
        rows = slice(m * 256, (m + 1) * 256)
        tokens = xa[rows, :] if m < 3 else xb[...]
        rounded = dot(tokens, wkeep[...]).astype(BF)
        qkv[rows, :] = rounded
        for i in range(2):
            block = block_at(idx, 2 * m + i)
            piece = dot_tn(rounded[i * TOK : (i + 1) * TOK, :HD], gs[block, 0])
            r[block] = piece
            whole += piece
    total[...] = whole.astype(BF)


def within(alpha, beta, idx, xa, xb, gs, qkv, dq, dk0, dv0, xt):
    rowi = lax.broadcasted_iota(jnp.int32, (TOK, TOK), 0)
    coli = lax.broadcasted_iota(jnp.int32, (TOK, TOK), 1)
    mask = rowi >= coli
    for place in range(8):
        rows = slice(place * TOK, (place + 1) * TOK)
        q, k, v = (qkv[rows, i * HD : (i + 1) * HD] for i in range(3))
        block = block_at(idx, place)
        g, state = gs[block, 0], gs[block, 1]
        p1 = jnp.where(mask, dot_nt(g, v), 0.0).astype(BF)
        p2 = jnp.where(mask, dot_nt(q, k), 0.0).astype(BF)
        dq[rows, :] = (alpha * dot_nt(g, state) + beta * dot(p1, k)).astype(BF)
        dk0[rows, :] = dot_tn(p1, q)
        dv0[rows, :] = dot_tn(p2, g)
        xt[:, rows] = xa[rows, :].T if place < 6 else xb[place * TOK - 768 : place * TOK - 640, :].T


def finish(beta, idx, qkv, dq, dk0, dv0, r, t1, t2, t3, dqkv, keep, send):
    yi, ci = idx[1], idx[3]
    acc = jnp.zeros((HD, HD), F32)
    for step, total in enumerate((t1, t2, t3)):
        use = jnp.where(yi < step + 1, 1.0, 0.0).astype(F32)
        acc += use * total[...].astype(F32)
    for b in range(7, -1, -1):
        rows = rows_of(idx, b // 2, jnp.where(ci == b % 2, 0, 1))
        k, v = qkv[rows, HD : 2 * HD], qkv[rows, 2 * HD :]
        later = acc.astype(BF)
        dqkv[rows, :HD] = dq[rows, :]
        dqkv[rows, HD : 2 * HD] = (beta * (dk0[rows, :] + dot_nt(v, later))).astype(BF)
        dqkv[rows, 2 * HD :] = (beta * (dv0[rows, :] + dot(k, later))).astype(BF)
        acc += r[b]
    for z in range(NZ):
        keep[z] = dqkv[rows_of(idx, z, 0), :]
        send[z] = dqkv[rows_of(idx, z, 1), :]


def weights(idx, xt, dqkv, *refs):
    outs, buf = refs[:4], refs[4]
    xi, yi, ci = idx[0], idx[1], idx[3]
    for m in range(4):
        rows = slice(m * 512, (m + 1) * 512)
        tile = dot(xt[rows, :], dqkv[...]).astype(BF)
        buf[m] = tile.reshape(8, NX, 16, 384)
    for s in range(4):
        for j in range(4):
            y = jnp.where(ci == 0, j, lax.rem(yi + s, NY))
            x = jnp.where(ci == 0, lax.rem(xi + s, NX), j)
            for g in range(8):
                outs[s][j, g] = buf[y, g, x]


def turn(idx, *refs):
    parts, outs = refs[:4], refs[4:]
    place = jnp.where(idx[3] == 0, idx[1], idx[0])
    for s in range(4):
        j = lax.rem(place + s, 4)
        for g in range(8):
            outs[s][g] = sum(p[j, g].astype(F32) for p in parts).astype(BF)


def far_back(idx, keep, got, own, other, far_up, far_down):
    far = lax.rem(idx[2] + 2, NZ)
    for n in range(4):
        cols = slice(n * 512, (n + 1) * 512)
        part = (dot_nt(keep[far], own[cols, :]) + dot_nt(got[far], other[cols, :])).astype(BF)
        far_up[:, cols] = part[:64, :]
        far_down[:, cols] = part[64:, :]


def near_back(idx, keep, got, own, other, mine_gx, up, down, mine, theirs):
    for i, step in enumerate((0, 1, 3)):
        z = lax.rem(idx[2] + step, NZ)
        rows = slice(i * TOK, (i + 1) * TOK)
        mine[rows, :] = keep[z]
        theirs[rows, :] = got[z]
    for n in range(4):
        cols = slice(n * 512, (n + 1) * 512)
        part = dot_nt(mine[...], own[cols, :]) + dot_nt(theirs[...], other[cols, :])
        mine_gx[:, cols] = part[:TOK, :]
        up[:, cols] = part[TOK : 2 * TOK, :].astype(BF)
        down[:, cols] = part[2 * TOK :, :].astype(BF)


def merge(idx, up, down, from_low, from_high, new_up, new_down):
    new_up[:64, :] = (up[:64, :].astype(F32) + from_low[...].astype(F32)).astype(BF)
    new_up[64:, :] = up[64:, :]
    new_down[:64, :] = down[:64, :]
    new_down[64:, :] = (down[64:, :].astype(F32) + from_high[...].astype(F32)).astype(BF)


def close(scale, idx, parts, mine, up, down, grad_w, grad_x):
    for head in range(8):
        for i in range(3):
            at = i * 1024 + head * HD
            grad_w[:, at : at + HD] = parts[head, :, i * HD : (i + 1) * HD].astype(F32) * scale
    grad_x[...] = (mine[...] + up[...].astype(F32) + down[...].astype(F32)).astype(BF)


def body(inputs, grad_out, saved, w_qkv):
    x = inputs[0]
    heads, head_size = saved.shape[2], saved.shape[3]
    length = x.shape[0] * lax.axis_size("ctx")
    alpha = 1.0 / head_size**0.5
    beta = 1.0 / (head_size * length) ** 0.5
    scale = 1.0 / (length * lax.axis_size("zero")) ** 0.5
    ctx = lax.axis_index("ctx")
    xi, yi, zi, ci = lax.axis_index("zero"), ctx // 8, (ctx // 2) % 4, ctx % 2
    idx = jnp.stack([xi, yi, zi, ci]).astype(jnp.int32)
    rows_y = [[ctx_index(y, z, c) for z in range(NZ) for c in range(NC)] for y in range(NY)]

    x1, x3 = ctx_hop(x, dz=1), ctx_hop(x, dz=-1)
    at = (2 * zi + ci) * HD
    own_w = jnp.concatenate(
        [lax.dynamic_slice(w_qkv, (0, i * heads * HD + at), (512, HD)) for i in range(3)], axis=1
    )
    (bundle,) = call(
        pack, [shape((8, 2, HD, HD), BF)], [after(idx, own_w), grad_out[0], saved[0, 0]]
    )
    gs = lax.all_to_all(bundle, "ctx", 0, 0, axis_index_groups=rows_y)
    w2, w1, w3 = (x_hop(own_w, s) for s in (2, 1, -1))
    x2a, x2b = ctx_hop(x1[:64], dz=1), ctx_hop(x3[64:], dz=-1)
    first = [x, x1, x3]
    first += [ctx_hop(p, dc=1) for p in first]
    (token,) = call(gate, [shape((16, HD), BF)], [idx, w1, w3, w2], flops=1 << 33, limit=4)
    (xa,) = call(stack, [shape((768, 2048), BF)], [idx, *first], flops=1 << 33, limit=10, deps=(token,))
    last = [x2a, x2b]
    last += [ctx_hop(after(p, gs), dc=1) for p in last]

    big = 2 * 1024 * 2048 * 384
    qkv, r, total, xb, whole_w = call(
        project,
        [
            shape((1024, 384), BF),
            shape((8, HD, HD), F32),
            shape((HD, HD), BF),
            shape((256, 2048), BF),
            shape((2048, 384), BF),
        ],
        [idx, xa, *last, own_w, w1, w3, w2, gs],
        flops=big,
    )
    own_w = whole_w
    totals = [ctx_hop(total, dy=s) for s in (1, 2, 3)]
    dq, dk0, dv0, xt = call(
        lambda *refs: within(alpha, beta, *refs),
        [shape((1024, HD), BF), shape((1024, HD), F32), shape((1024, HD), F32), shape((2048, 1024), BF)],
        [idx, xa, xb, gs, qkv],
        flops=big // 4,
    )
    dqkv, keep, send = call(
        lambda *refs: finish(beta, *refs),
        [shape((1024, 384), BF), shape((NZ, TOK, 384), BF), shape((NZ, TOK, 384), BF)],
        [idx, qkv, dq, dk0, dv0, r, *totals],
        flops=big // 16,
    )
    got = ctx_hop(send, dc=1)
    other_w = ctx_hop(after(own_w, send), dc=1)
    parts = call(
        weights,
        [shape((4, 8, 16, 384), BF)] * 4,
        [idx, xt, dqkv],
        [pltpu.VMEM((NY, 8, NX, 16, 384), BF)],
        flops=big,
    )
    far_up, far_down = call(
        far_back,
        [shape((64, 2048), BF)] * 2,
        [idx, keep, got, own_w, other_w],
        flops=big // 4,
        deps=(parts[0],),
        limit=8,
    )
    gx, up, down = call(
        near_back,
        [shape((TOK, 2048), F32)] + [shape((TOK, 2048), BF)] * 2,
        [idx, keep, got, own_w, other_w],
        [pltpu.VMEM((384, 384), BF)] * 2,
        flops=big,
        deps=(far_up,),
        limit=12,
    )
    parts = [parts[0]] + [plane_hop(parts[s], s, 0) for s in (1, 2, 3)]
    far_up, far_down = ctx_hop(far_up, dz=1), ctx_hop(far_down, dz=-1)
    parts = call(turn, [shape((8, 16, 384), BF)] * 4, [idx, *parts], deps=(gx,), limit=4)
    up, down = call(
        merge, [shape((TOK, 2048), BF)] * 2, [idx, up, down, far_up, far_down], flops=1 << 34, deps=(parts[0],), limit=6
    )
    parts = [parts[0]] + [plane_hop(parts[s], s, 1) for s in (1, 2, 3)]
    up, down = ctx_hop(up, dz=1), ctx_hop(down, dz=-1)
    owned = sum(p.astype(F32) for p in parts).astype(BF)
    owned = lax.all_to_all(owned, "ctx", 0, 0, axis_index_groups=rows_y)
    grad_w, grad_x = call(
        lambda *refs: close(scale, *refs),
        [shape((16, 3 * heads * HD), F32), shape((TOK, 2048), BF)],
        [idx, owned, gx, up, down],
        flops=0,
        limit=8,
    )
    return (grad_x[None], grad_w)


def solution(mesh):
    in_specs = (
        P("zero", "ctx", None),
        P("zero", "ctx", None),
        P("zero", "ctx", None, None, None),
        P("zero", None),
    )
    out_specs = (P("zero", "ctx", None), P(("ctx", "zero"), None))
    return jax.shard_map(body, mesh=mesh, in_specs=in_specs, out_specs=out_specs, check_vma=False)
```

```python
import jax
import jax.numpy as jnp
from jax import lax
from jax.experimental import pallas as pl
from jax.experimental.pallas import tpu as pltpu
from jax.sharding import PartitionSpec as P

NY, NZ, NC, NX = 4, 4, 2, 4
TOK, HD = 128, 128
BF, F32 = jnp.bfloat16, jnp.float32


def ctx_index(y, z, c):
    return (y * NZ + z) * NC + c


def ctx_hop(block, dy=0, dz=0, dc=0):
    route = [
        (ctx_index(y, z, c), ctx_index((y + dy) % NY, (z + dz) % NZ, (c + dc) % NC))
        for y in range(NY)
        for z in range(NZ)
        for c in range(NC)
    ]
    return lax.ppermute(block, "ctx", route)


def x_hop(block, dx):
    return lax.ppermute(block, "zero", [(i, (i + dx) % NX) for i in range(NX)])


def plane_hop(block, step, stage):
    route = []
    for y in range(NY):
        for z in range(NZ):
            for c in range(NC):
                for x in range(NX):
                    dx, dy = (step, 0) if c == stage else (0, step)
                    to = ctx_index((y + dy) % NY, z, c) * NX + (x + dx) % NX
                    route.append((ctx_index(y, z, c) * NX + x, to))
    return lax.ppermute(block, ("ctx", "zero"), route)


def dot(a, b):
    return lax.dot_general(a, b, (((1,), (0,)), ((), ())), preferred_element_type=F32)


def dot_nt(a, b):
    return lax.dot_general(a, b, (((1,), (1,)), ((), ())), preferred_element_type=F32)


def dot_tn(a, b):
    return lax.dot_general(a, b, (((0,), (0,)), ((), ())), preferred_element_type=F32)


def call(kernel, outs, ins, scratch=(), flops=0, limit=16, deps=(), free=()):
    count = len(ins)

    def run(*refs):
        kernel(*refs[:count], *refs[count + len(deps) :])

    moved = sum(a.size * a.dtype.itemsize for a in list(ins) + list(outs))
    vmem = pl.BlockSpec(memory_space=pltpu.VMEM)
    return pl.pallas_call(
        run,
        out_shape=list(outs),
        in_specs=[pl.BlockSpec(memory_space=pltpu.SMEM)]
        + [pl.BlockSpec(memory_space=pl.ANY) if i in free else vmem for i in range(1, count)]
        + [pl.BlockSpec(memory_space=pl.ANY)] * len(deps),
        out_specs=[vmem] * len(outs),
        scratch_shapes=list(scratch),
        compiler_params=pltpu.CompilerParams(vmem_limit_bytes=limit << 20),
        cost_estimate=pl.CostEstimate(flops=flops, bytes_accessed=moved, transcendentals=0),
    )(*ins, *deps)


def shape(dims, dtype):
    return jax.ShapeDtypeStruct(dims, dtype)


def after(value, deps):
    return lax.optimization_barrier((value, deps))[0]


def columns(place, step, start=0, size=512):
    block = lax.rem(place + NX - step, NX)
    return pl.ds(pl.multiple_of(block * 512 + start, 256), size)


NEAR = (0, 1, 3)


def block_at(idx, place):
    slot = NEAR[place % 3] if place < 6 else 2
    mate = place in (3, 4, 5, 7)
    core = 1 - idx[3] if mate else idx[3]
    return lax.rem(idx[2] + NZ - slot, NZ) * 2 + core


def rows_of(idx, z, mate):
    slot = lax.rem(idx[2] + NZ - z, NZ)
    near = jnp.where(slot == 3, 2, slot) + 3 * mate
    return pl.ds(pl.multiple_of(jnp.where(slot == 2, 6 + mate, near) * TOK, TOK), TOK)


def pack(idx, cot, state, out):
    for h in range(8):
        out[h, 0] = cot[:, h * HD : (h + 1) * HD]
        out[h, 1] = state[h].astype(BF)


def gate(idx, w1, w3, w2, out):
    out[...] = w1[:16, :HD] + w3[:16, :HD] + w2[:16, :HD]


def stack(idx, *refs):
    parts, xa = refs[:6], refs[6]
    for i, part in enumerate(parts):
        xa[i * TOK : (i + 1) * TOK, :] = part[...]


def project(idx, xa, x2a, x2b, m2a, m2b, w0, w1, w3, w2, gs, qkv, r, total, xb, wkeep):
    for i, part in enumerate((x2a, x2b, m2a, m2b)):
        xb[i * 64 : (i + 1) * 64, :] = part[...]
    for part, step in ((w0, 0), (w1, 1), (w3, 3), (w2, 2)):
        wkeep[columns(idx[0], step, 0, 512), :] = part[...]
    whole = jnp.zeros((HD, HD), F32)
    for m in range(4):
        rows = slice(m * 256, (m + 1) * 256)
        tokens = xa[rows, :] if m < 3 else xb[...]
        rounded = dot(tokens, wkeep[...]).astype(BF)
        qkv[rows, :] = rounded
        for i in range(2):
            block = block_at(idx, 2 * m + i)
            piece = dot_tn(rounded[i * TOK : (i + 1) * TOK, :HD], gs[block, 0])
            r[block] = piece
            whole += piece
    total[...] = whole.astype(BF)


def within(alpha, beta, idx, xa, xb, gs, qkv, dq, dk0, dv0, xt):
    rowi = lax.broadcasted_iota(jnp.int32, (TOK, TOK), 0)
    coli = lax.broadcasted_iota(jnp.int32, (TOK, TOK), 1)
    mask = rowi >= coli
    for place in range(8):
        rows = slice(place * TOK, (place + 1) * TOK)
        q, k, v = (qkv[rows, i * HD : (i + 1) * HD] for i in range(3))
        block = block_at(idx, place)
        g, state = gs[block, 0], gs[block, 1]
        p1 = jnp.where(mask, dot_nt(g, v), 0.0).astype(BF)
        p2 = jnp.where(mask, dot_nt(q, k), 0.0).astype(BF)
        dq[rows, :] = (alpha * dot_nt(g, state) + beta * dot(p1, k)).astype(BF)
        dk0[rows, :] = dot_tn(p1, q)
        dv0[rows, :] = dot_tn(p2, g)
        xt[:, rows] = xa[rows, :].T if place < 6 else xb[place * TOK - 768 : place * TOK - 640, :].T


def finish(beta, idx, qkv, dq, dk0, dv0, r, t1, t2, t3, dqkv, keep, send):
    yi, ci = idx[1], idx[3]
    acc = jnp.zeros((HD, HD), F32)
    for step, total in enumerate((t1, t2, t3)):
        use = jnp.where(yi < step + 1, 1.0, 0.0).astype(F32)
        acc += use * total[...].astype(F32)
    for b in range(7, -1, -1):
        rows = rows_of(idx, b // 2, jnp.where(ci == b % 2, 0, 1))
        k, v = qkv[rows, HD : 2 * HD], qkv[rows, 2 * HD :]
        later = acc.astype(BF)
        dqkv[rows, :HD] = dq[rows, :]
        dqkv[rows, HD : 2 * HD] = (beta * (dk0[rows, :] + dot_nt(v, later))).astype(BF)
        dqkv[rows, 2 * HD :] = (beta * (dv0[rows, :] + dot(k, later))).astype(BF)
        acc += r[b]
    for z in range(NZ):
        keep[z] = dqkv[rows_of(idx, z, 0), :]
        send[z] = dqkv[rows_of(idx, z, 1), :]


def weights(idx, xt, dqkv, *refs):
    outs, buf = refs[:4], refs[4]
    xi, yi, ci = idx[0], idx[1], idx[3]
    for m in range(4):
        rows = slice(m * 512, (m + 1) * 512)
        tile = dot(xt[rows, :], dqkv[...]).astype(BF)
        buf[m] = tile.reshape(8, NX, 16, 384)
    for s in range(4):
        for j in range(4):
            y = jnp.where(ci == 0, j, lax.rem(yi + s, NY))
            x = jnp.where(ci == 0, lax.rem(xi + s, NX), j)
            for g in range(8):
                outs[s][j, g] = buf[y, g, x]


def turn(idx, *refs):
    parts, outs = refs[:4], refs[4:]
    place = jnp.where(idx[3] == 0, idx[1], idx[0])
    for s in range(4):
        j = lax.rem(place + s, 4)
        for g in range(8):
            outs[s][g] = sum(p[j, g].astype(F32) for p in parts).astype(BF)


def far_back(idx, keep, got, own, other, far_up, far_down):
    far = lax.rem(idx[2] + 2, NZ)
    for n in range(4):
        cols = slice(n * 512, (n + 1) * 512)
        part = (dot_nt(keep[far], own[cols, :]) + dot_nt(got[far], other[cols, :])).astype(BF)
        far_up[:, cols] = part[:64, :]
        far_down[:, cols] = part[64:, :]


def near_back(idx, keep, got, own, other, mine_gx, up, down, mine, theirs):
    for i, step in enumerate((0, 1, 3)):
        z = lax.rem(idx[2] + step, NZ)
        rows = slice(i * TOK, (i + 1) * TOK)
        mine[rows, :] = keep[z]
        theirs[rows, :] = got[z]
    for n in range(4):
        cols = slice(n * 512, (n + 1) * 512)
        part = dot_nt(mine[...], own[cols, :]) + dot_nt(theirs[...], other[cols, :])
        mine_gx[:, cols] = part[:TOK, :]
        up[:, cols] = part[TOK : 2 * TOK, :].astype(BF)
        down[:, cols] = part[2 * TOK :, :].astype(BF)


def merge(idx, up, down, from_low, from_high, new_up, new_down):
    new_up[:64, :] = (up[:64, :].astype(F32) + from_low[...].astype(F32)).astype(BF)
    new_up[64:, :] = up[64:, :]
    new_down[:64, :] = down[:64, :]
    new_down[64:, :] = (down[64:, :].astype(F32) + from_high[...].astype(F32)).astype(BF)


def close(scale, idx, parts, mine, up, down, grad_w, grad_x):
    for head in range(8):
        for i in range(3):
            at = i * 1024 + head * HD
            grad_w[:, at : at + HD] = parts[head, :, i * HD : (i + 1) * HD].astype(F32) * scale
    grad_x[...] = (mine[...] + up[...].astype(F32) + down[...].astype(F32)).astype(BF)


def body(inputs, grad_out, saved, w_qkv):
    x = inputs[0]
    heads, head_size = saved.shape[2], saved.shape[3]
    length = x.shape[0] * lax.axis_size("ctx")
    alpha = 1.0 / head_size**0.5
    beta = 1.0 / (head_size * length) ** 0.5
    scale = 1.0 / (length * lax.axis_size("zero")) ** 0.5
    ctx = lax.axis_index("ctx")
    xi, yi, zi, ci = lax.axis_index("zero"), ctx // 8, (ctx // 2) % 4, ctx % 2
    idx = jnp.stack([xi, yi, zi, ci]).astype(jnp.int32)
    rows_y = [[ctx_index(y, z, c) for z in range(NZ) for c in range(NC)] for y in range(NY)]

    x1, x3 = ctx_hop(x, dz=1), ctx_hop(x, dz=-1)
    at = (2 * zi + ci) * HD
    own_w = jnp.concatenate(
        [lax.dynamic_slice(w_qkv, (0, i * heads * HD + at), (512, HD)) for i in range(3)], axis=1
    )
    (bundle,) = call(
        pack, [shape((8, 2, HD, HD), BF)], [after(idx, own_w), grad_out[0], saved[0, 0]]
    )
    gs = lax.all_to_all(bundle, "ctx", 0, 0, axis_index_groups=rows_y)
    w2, w1, w3 = (x_hop(own_w, s) for s in (2, 1, -1))
    x2a, x2b = ctx_hop(x1[:64], dz=1), ctx_hop(x3[64:], dz=-1)
    first = [x, x1, x3]
    first += [ctx_hop(p, dc=1) for p in first]
    (token,) = call(gate, [shape((16, HD), BF)], [idx, w1, w3, w2], flops=1 << 33, limit=4)
    (xa,) = call(stack, [shape((768, 2048), BF)], [idx, *first], flops=1 << 33, limit=10, deps=(token,))
    last = [x2a, x2b]
    last += [ctx_hop(after(p, gs), dc=1) for p in last]

    big = 2 * 1024 * 2048 * 384
    qkv, r, total, xb, whole_w = call(
        project,
        [
            shape((1024, 384), BF),
            shape((8, HD, HD), F32),
            shape((HD, HD), BF),
            shape((256, 2048), BF),
            shape((2048, 384), BF),
        ],
        [idx, xa, *last, own_w, w1, w3, w2, gs],
        flops=big,
    )
    own_w = whole_w
    far, near, last_one = (ctx_hop(total, dy=s) for s in (2, 1, 3))
    totals = [near, far, last_one]
    dq, dk0, dv0, xt = call(
        lambda *refs: within(alpha, beta, *refs),
        [shape((1024, HD), BF), shape((1024, HD), F32), shape((1024, HD), F32), shape((2048, 1024), BF)],
        [idx, xa, xb, gs, qkv],
        flops=big // 4,
    )
    dqkv, keep, send = call(
        lambda *refs: finish(beta, *refs),
        [shape((1024, 384), BF), shape((NZ, TOK, 384), BF), shape((NZ, TOK, 384), BF)],
        [idx, qkv, dq, dk0, dv0, r, *totals],
        flops=big // 16,
    )
    got = ctx_hop(send, dc=1)
    other_w = ctx_hop(after(own_w, send), dc=1)
    parts = call(
        weights,
        [shape((4, 8, 16, 384), BF)] * 4,
        [idx, xt, dqkv],
        [pltpu.VMEM((NY, 8, NX, 16, 384), BF)],
        flops=big,
    )
    far_up, far_down = call(
        far_back,
        [shape((64, 2048), BF)] * 2,
        [idx, keep, got, own_w, other_w],
        flops=big // 4,
        deps=(parts[0],),
        limit=8,
    )
    gx, up, down = call(
        near_back,
        [shape((TOK, 2048), F32)] + [shape((TOK, 2048), BF)] * 2,
        [idx, keep, got, own_w, other_w],
        [pltpu.VMEM((384, 384), BF)] * 2,
        flops=big,
        deps=(far_up,),
        limit=12,
    )
    parts = [parts[0]] + [plane_hop(parts[s], s, 0) for s in (2, 1, 3)]
    far_up, far_down = ctx_hop(far_up, dz=1), ctx_hop(far_down, dz=-1)
    parts = call(turn, [shape((8, 16, 384), BF)] * 4, [idx, *parts], deps=(gx,), limit=4)
    up, down = call(
        merge, [shape((TOK, 2048), BF)] * 2, [idx, up, down, far_up, far_down], flops=1 << 34, deps=(parts[0],), limit=6
    )
    parts = [parts[0]] + [plane_hop(parts[s], s, 1) for s in (2, 1, 3)]
    up, down = ctx_hop(up, dz=1), ctx_hop(down, dz=-1)
    owned = sum(p.astype(F32) for p in parts).astype(BF)
    owned = lax.all_to_all(owned, "ctx", 0, 0, axis_index_groups=rows_y)
    grad_w, grad_x = call(
        lambda *refs: close(scale, *refs),
        [shape((16, 3 * heads * HD), F32), shape((TOK, 2048), BF)],
        [idx, owned, gx, up, down],
        flops=0,
        limit=8,
    )
    return (grad_x[None], grad_w)


def solution(mesh):
    in_specs = (
        P("zero", "ctx", None),
        P("zero", "ctx", None),
        P("zero", "ctx", None, None, None),
        P("zero", None),
    )
    out_specs = (P("zero", "ctx", None), P(("ctx", "zero"), None))
    return jax.shard_map(body, mesh=mesh, in_specs=in_specs, out_specs=out_specs, check_vma=False)
```

```python
import jax
import jax.numpy as jnp
from jax import lax
from jax.experimental import pallas as pl
from jax.experimental.pallas import tpu as pltpu
from jax.sharding import PartitionSpec as P

NY, NZ, NC, NX = 4, 4, 2, 4
TOK, HD = 128, 128
BF, F32 = jnp.bfloat16, jnp.float32


def ctx_index(y, z, c):
    return (y * NZ + z) * NC + c


def ctx_hop(block, dy=0, dz=0, dc=0):
    route = [
        (ctx_index(y, z, c), ctx_index((y + dy) % NY, (z + dz) % NZ, (c + dc) % NC))
        for y in range(NY)
        for z in range(NZ)
        for c in range(NC)
    ]
    return lax.ppermute(block, "ctx", route)


def x_hop(block, dx):
    return lax.ppermute(block, "zero", [(i, (i + dx) % NX) for i in range(NX)])


def plane_hop(block, step, stage):
    route = []
    for y in range(NY):
        for z in range(NZ):
            for c in range(NC):
                for x in range(NX):
                    dx, dy = (step, 0) if c == stage else (0, step)
                    to = ctx_index((y + dy) % NY, z, c) * NX + (x + dx) % NX
                    route.append((ctx_index(y, z, c) * NX + x, to))
    return lax.ppermute(block, ("ctx", "zero"), route)


def dot(a, b):
    return lax.dot_general(a, b, (((1,), (0,)), ((), ())), preferred_element_type=F32)


def dot_nt(a, b):
    return lax.dot_general(a, b, (((1,), (1,)), ((), ())), preferred_element_type=F32)


def dot_tn(a, b):
    return lax.dot_general(a, b, (((0,), (0,)), ((), ())), preferred_element_type=F32)


def call(kernel, outs, ins, scratch=(), flops=0, limit=16, deps=(), free=()):
    count = len(ins)

    def run(*refs):
        kernel(*refs[:count], *refs[count + len(deps) :])

    moved = sum(a.size * a.dtype.itemsize for a in list(ins) + list(outs))
    vmem = pl.BlockSpec(memory_space=pltpu.VMEM)
    return pl.pallas_call(
        run,
        out_shape=list(outs),
        in_specs=[pl.BlockSpec(memory_space=pltpu.SMEM)]
        + [pl.BlockSpec(memory_space=pl.ANY) if i in free else vmem for i in range(1, count)]
        + [pl.BlockSpec(memory_space=pl.ANY)] * len(deps),
        out_specs=[vmem] * len(outs),
        scratch_shapes=list(scratch),
        compiler_params=pltpu.CompilerParams(vmem_limit_bytes=limit << 20),
        cost_estimate=pl.CostEstimate(flops=flops, bytes_accessed=moved, transcendentals=0),
    )(*ins, *deps)


def shape(dims, dtype):
    return jax.ShapeDtypeStruct(dims, dtype)


def after(value, deps):
    return lax.optimization_barrier((value, deps))[0]


def columns(place, step, start=0, size=512):
    block = lax.rem(place + NX - step, NX)
    return pl.ds(pl.multiple_of(block * 512 + start, 256), size)


NEAR = (0, 1, 3)


def block_at(idx, place):
    slot = NEAR[place % 3] if place < 6 else 2
    mate = place in (3, 4, 5, 7)
    core = 1 - idx[3] if mate else idx[3]
    return lax.rem(idx[2] + NZ - slot, NZ) * 2 + core


def rows_of(idx, z, mate):
    slot = lax.rem(idx[2] + NZ - z, NZ)
    near = jnp.where(slot == 3, 2, slot) + 3 * mate
    return pl.ds(pl.multiple_of(jnp.where(slot == 2, 6 + mate, near) * TOK, TOK), TOK)


def gate(idx, w1, w3, w2, out):
    out[...] = w1[:16, :HD] + w3[:16, :HD] + w2[:16, :HD]


def stack(idx, *refs):
    parts, xa = refs[:6], refs[6]
    for i, part in enumerate(parts):
        xa[i * TOK : (i + 1) * TOK, :] = part[...]


def project(idx, xa, x2a, x2b, m2a, m2b, w0, w1, w3, w2, gs, qkv, r, total, xb, wkeep):
    for i, part in enumerate((x2a, x2b, m2a, m2b)):
        xb[i * 64 : (i + 1) * 64, :] = part[...]
    for part, step in ((w0, 0), (w1, 1), (w3, 3), (w2, 2)):
        wkeep[columns(idx[0], step, 0, 512), :] = part[...]
    whole = jnp.zeros((HD, HD), F32)
    for m in range(4):
        rows = slice(m * 256, (m + 1) * 256)
        tokens = xa[rows, :] if m < 3 else xb[...]
        rounded = dot(tokens, wkeep[...]).astype(BF)
        qkv[rows, :] = rounded
        for i in range(2):
            block = block_at(idx, 2 * m + i)
            piece = dot_tn(rounded[i * TOK : (i + 1) * TOK, :HD], gs[block, 0])
            r[block] = piece
            whole += piece
    total[...] = whole.astype(BF)


def within(alpha, beta, idx, xa, xb, gs, qkv, dq, dk0, dv0, xt):
    rowi = lax.broadcasted_iota(jnp.int32, (TOK, TOK), 0)
    coli = lax.broadcasted_iota(jnp.int32, (TOK, TOK), 1)
    mask = rowi >= coli
    for place in range(8):
        rows = slice(place * TOK, (place + 1) * TOK)
        q, k, v = (qkv[rows, i * HD : (i + 1) * HD] for i in range(3))
        block = block_at(idx, place)
        g, state = gs[block, 0], gs[block, 1]
        p1 = jnp.where(mask, dot_nt(g, v), 0.0).astype(BF)
        p2 = jnp.where(mask, dot_nt(q, k), 0.0).astype(BF)
        dq[rows, :] = (alpha * dot_nt(g, state) + beta * dot(p1, k)).astype(BF)
        dk0[rows, :] = dot_tn(p1, q)
        dv0[rows, :] = dot_tn(p2, g)
        xt[:, rows] = xa[rows, :].T if place < 6 else xb[place * TOK - 768 : place * TOK - 640, :].T


def finish(beta, idx, qkv, dq, dk0, dv0, r, t1, t2, t3, dqkv, keep, send):
    yi, ci = idx[1], idx[3]
    acc = jnp.zeros((HD, HD), F32)
    for step, total in enumerate((t1, t2, t3)):
        use = jnp.where(yi < step + 1, 1.0, 0.0).astype(F32)
        acc += use * total[...].astype(F32)
    for b in range(7, -1, -1):
        rows = rows_of(idx, b // 2, jnp.where(ci == b % 2, 0, 1))
        k, v = qkv[rows, HD : 2 * HD], qkv[rows, 2 * HD :]
        later = acc.astype(BF)
        dqkv[rows, :HD] = dq[rows, :]
        dqkv[rows, HD : 2 * HD] = (beta * (dk0[rows, :] + dot_nt(v, later))).astype(BF)
        dqkv[rows, 2 * HD :] = (beta * (dv0[rows, :] + dot(k, later))).astype(BF)
        acc += r[b]
    for z in range(NZ):
        keep[z] = dqkv[rows_of(idx, z, 0), :]
        send[z] = dqkv[rows_of(idx, z, 1), :]


def weights(idx, xt, dqkv, *refs):
    outs, buf = refs[:4], refs[4]
    xi, yi, ci = idx[0], idx[1], idx[3]
    for m in range(4):
        rows = slice(m * 512, (m + 1) * 512)
        tile = dot(xt[rows, :], dqkv[...]).astype(BF)
        buf[m] = tile.reshape(8, NX, 16, 384)
    for s in range(4):
        for j in range(4):
            y = jnp.where(ci == 0, j, lax.rem(yi + s, NY))
            x = jnp.where(ci == 0, lax.rem(xi + s, NX), j)
            for g in range(8):
                outs[s][j, g] = buf[y, g, x]


def turn(idx, *refs):
    parts, outs = refs[:4], refs[4:]
    place = jnp.where(idx[3] == 0, idx[1], idx[0])
    for s in range(4):
        j = lax.rem(place + s, 4)
        for g in range(8):
            outs[s][g] = sum(p[j, g].astype(F32) for p in parts).astype(BF)


def far_back(idx, keep, got, own, other, far_up, far_down):
    far = lax.rem(idx[2] + 2, NZ)
    for n in range(4):
        cols = slice(n * 512, (n + 1) * 512)
        part = (dot_nt(keep[far], own[cols, :]) + dot_nt(got[far], other[cols, :])).astype(BF)
        far_up[:, cols] = part[:64, :]
        far_down[:, cols] = part[64:, :]


def near_back(idx, keep, got, own, other, mine_gx, up, down, mine, theirs):
    for i, step in enumerate((0, 1, 3)):
        z = lax.rem(idx[2] + step, NZ)
        rows = slice(i * TOK, (i + 1) * TOK)
        mine[rows, :] = keep[z]
        theirs[rows, :] = got[z]
    for n in range(4):
        cols = slice(n * 512, (n + 1) * 512)
        part = dot_nt(mine[...], own[cols, :]) + dot_nt(theirs[...], other[cols, :])
        mine_gx[:, cols] = part[:TOK, :]
        up[:, cols] = part[TOK : 2 * TOK, :].astype(BF)
        down[:, cols] = part[2 * TOK :, :].astype(BF)


def merge(idx, up, down, from_low, from_high, new_up, new_down):
    new_up[:64, :] = (up[:64, :].astype(F32) + from_low[...].astype(F32)).astype(BF)
    new_up[64:, :] = up[64:, :]
    new_down[:64, :] = down[:64, :]
    new_down[64:, :] = (down[64:, :].astype(F32) + from_high[...].astype(F32)).astype(BF)


def close(scale, idx, parts, mine, up, down, grad_w, grad_x):
    for head in range(8):
        for i in range(3):
            at = i * 1024 + head * HD
            grad_w[:, at : at + HD] = parts[head, :, i * HD : (i + 1) * HD].astype(F32) * scale
    grad_x[...] = (mine[...] + up[...].astype(F32) + down[...].astype(F32)).astype(BF)


def body(inputs, grad_out, saved, w_qkv):
    x = inputs[0]
    heads, head_size = saved.shape[2], saved.shape[3]
    length = x.shape[0] * lax.axis_size("ctx")
    alpha = 1.0 / head_size**0.5
    beta = 1.0 / (head_size * length) ** 0.5
    scale = 1.0 / (length * lax.axis_size("zero")) ** 0.5
    ctx = lax.axis_index("ctx")
    xi, yi, zi, ci = lax.axis_index("zero"), ctx // 8, (ctx // 2) % 4, ctx % 2
    idx = jnp.stack([xi, yi, zi, ci]).astype(jnp.int32)
    rows_y = [[ctx_index(y, z, c) for z in range(NZ) for c in range(NC)] for y in range(NY)]

    x1, x3 = ctx_hop(x, dz=1), ctx_hop(x, dz=-1)
    at = (2 * zi + ci) * HD
    own_w = jnp.concatenate(
        [lax.dynamic_slice(w_qkv, (0, i * heads * HD + at), (512, HD)) for i in range(3)], axis=1
    )
    cot = grad_out[0].reshape(TOK, heads, HD).transpose(1, 0, 2)
    bundle = jnp.stack([cot, saved[0, 0].astype(BF)], axis=1)
    gs = lax.all_to_all(bundle, "ctx", 0, 0, axis_index_groups=rows_y)
    w2, w1, w3 = (x_hop(own_w, s) for s in (2, 1, -1))
    x2a, x2b = ctx_hop(x1[:64], dz=1), ctx_hop(x3[64:], dz=-1)
    first = [x, x1, x3]
    first += [ctx_hop(p, dc=1) for p in first]
    (token,) = call(gate, [shape((16, HD), BF)], [idx, w1, w3, w2], flops=1 << 33, limit=4)
    (xa,) = call(stack, [shape((768, 2048), BF)], [idx, *first], flops=1 << 33, limit=10, deps=(token,))
    last = [x2a, x2b]
    last += [ctx_hop(after(p, gs), dc=1) for p in last]

    big = 2 * 1024 * 2048 * 384
    qkv, r, total, xb, whole_w = call(
        project,
        [
            shape((1024, 384), BF),
            shape((8, HD, HD), F32),
            shape((HD, HD), BF),
            shape((256, 2048), BF),
            shape((2048, 384), BF),
        ],
        [idx, xa, *last, own_w, w1, w3, w2, gs],
        flops=big,
    )
    own_w = whole_w
    far, near, last_one = (ctx_hop(total, dy=s) for s in (2, 1, 3))
    totals = [near, far, last_one]
    dq, dk0, dv0, xt = call(
        lambda *refs: within(alpha, beta, *refs),
        [shape((1024, HD), BF), shape((1024, HD), F32), shape((1024, HD), F32), shape((2048, 1024), BF)],
        [idx, xa, xb, gs, qkv],
        flops=big // 4,
    )
    dqkv, keep, send = call(
        lambda *refs: finish(beta, *refs),
        [shape((1024, 384), BF), shape((NZ, TOK, 384), BF), shape((NZ, TOK, 384), BF)],
        [idx, qkv, dq, dk0, dv0, r, *totals],
        flops=big // 16,
    )
    got = ctx_hop(send, dc=1)
    other_w = ctx_hop(after(own_w, send), dc=1)
    parts = call(
        weights,
        [shape((4, 8, 16, 384), BF)] * 4,
        [idx, xt, dqkv],
        [pltpu.VMEM((NY, 8, NX, 16, 384), BF)],
        flops=big,
    )
    far_up, far_down = call(
        far_back,
        [shape((64, 2048), BF)] * 2,
        [idx, keep, got, own_w, other_w],
        flops=big // 4,
        deps=(parts[0],),
        limit=8,
    )
    gx, up, down = call(
        near_back,
        [shape((TOK, 2048), F32)] + [shape((TOK, 2048), BF)] * 2,
        [idx, keep, got, own_w, other_w],
        [pltpu.VMEM((384, 384), BF)] * 2,
        flops=big,
        deps=(far_up,),
        limit=12,
    )
    parts = [parts[0]] + [plane_hop(parts[s], s, 0) for s in (2, 1, 3)]
    far_up, far_down = ctx_hop(far_up, dz=1), ctx_hop(far_down, dz=-1)
    parts = call(turn, [shape((8, 16, 384), BF)] * 4, [idx, *parts], deps=(gx,), limit=4)
    up, down = call(
        merge, [shape((TOK, 2048), BF)] * 2, [idx, up, down, far_up, far_down], flops=1 << 34, deps=(parts[0],), limit=6
    )
    parts = [parts[0]] + [plane_hop(parts[s], s, 1) for s in (2, 1, 3)]
    up, down = ctx_hop(up, dz=1), ctx_hop(down, dz=-1)
    owned = sum(p.astype(F32) for p in parts).astype(BF)
    owned = lax.all_to_all(owned, "ctx", 0, 0, axis_index_groups=rows_y)
    grad_w, grad_x = call(
        lambda *refs: close(scale, *refs),
        [shape((16, 3 * heads * HD), F32), shape((TOK, 2048), BF)],
        [idx, owned, gx, up, down],
        flops=0,
        limit=8,
    )
    return (grad_x[None], grad_w)


def solution(mesh):
    in_specs = (
        P("zero", "ctx", None),
        P("zero", "ctx", None),
        P("zero", "ctx", None, None, None),
        P("zero", None),
    )
    out_specs = (P("zero", "ctx", None), P(("ctx", "zero"), None))
    return jax.shard_map(body, mesh=mesh, in_specs=in_specs, out_specs=out_specs, check_vma=False)
```
